32 devices in a mesh: leaf: 16 (over z, x, core), head: 2 (over y).
Axes of the slice: x: 2, y: 2, z: 4, core: 2. Of those that a mesh axis runs over, the one named last changes fastest.
Arguments:
- queries: bfloat16 [3072, 73728], P('leaf', 'head'), may hold values from -80 to 80
- d_out: bfloat16 [3072, 65536], P('leaf', 'head'), may hold values from -24 to 24
- branch_latent: bfloat16 [3072, 576], P('leaf'), may hold values from -6 to 6
- trunk_latent: bfloat16 [256, 8, 576], P('leaf'), may hold values from -6 to 6
- ancestors: int32 [16, 32], replicated, may hold values from 0 to 255, as said below
- anc_count: int32 [16], replicated, may hold values from 24 to 32, as said below
Outputs:
- d_queries: bfloat16 [3072, 73728], P('leaf', 'head')
- d_branch: float32 [3072, 576], P(('leaf', 'head'))
- d_trunk: float32 [256, 8, 576], P('leaf', 'head')
The draws below stay inside these ranges and needn't reach their ends.
Inputs may be any that keep to these rules, and one draw needn't show every extreme that they name: `ancestors`: each row lists 32 different trunk blocks; the owner of a block is its number // 16; a row lists 2 blocks of each owner that it names, never more. `anc_count`: some branch has all 32 slots live.
All inputs are finite; a program needn't handle non-finite values.
Results may differ from the reference program's by a relative error of at most 0.014.
Values may be sent and summed in bfloat16 or wider, within the bound.
No kernel may reach another device: no remote copies, remote signals or barrier semaphores. Data moves between devices by JAX's collectives and lax.ppermute only.
A program may use at most 192 MiB of HBM per device.

```python
import jax
import jax.numpy as jnp
from jax import lax

HEADS = 128
RANK = 512
QK_HEAD = 192
LATENT = 576
BR_DEV = 192
BLK = 8
CAP = 2
ANC = 32
TRK_BLK = 16
TOKENS = 3072
TRUNK_BLOCKS = 256
N_LEAF = 16


def latent_field(key):
    base = jax.random.fold_in(key, 11)
    field = jax.random.normal(base, (TOKENS, LATENT), jnp.float32)
    return jnp.clip(field, -6.0, 6.0)


def draw_branch_latent(key, part):
    return latent_field(key).astype(jnp.bfloat16)


def draw_queries(key, part):
    sub = jax.random.fold_in(key, 23)
    base = jax.random.normal(sub, (TOKENS, HEADS, LATENT), jnp.float32)
    return jnp.clip(base, -80.0, 80.0).reshape(TOKENS, HEADS * LATENT).astype(jnp.bfloat16)


def draw_ancestors(key, part):
    row_keys = jax.random.split(jax.random.fold_in(key, 31), N_LEAF)

    def one_row(row_key):
        owner_key, block_key = jax.random.split(row_key)
        chosen = jax.random.permutation(owner_key, N_LEAF)[:ANC // CAP]
        group_keys = jax.random.split(block_key, ANC // CAP)
        local_picks = jax.vmap(lambda gk: jax.random.permutation(gk, TRK_BLK)[:CAP])(group_keys)
        return (chosen[:, None] * TRK_BLK + local_picks).reshape(ANC)
    return jax.vmap(one_row)(row_keys).astype(jnp.int32)


def draw_anc_count(key, part):
    dropped = jax.random.randint(jax.random.fold_in(key, 37), (N_LEAF,), 0, ANC // 4 + 1)
    full_at = jax.random.randint(jax.random.fold_in(key, 41), (), 0, N_LEAF)
    dropped = jnp.where(jnp.arange(N_LEAF, dtype=jnp.int32) == full_at, 0, dropped)
    return (ANC - dropped).astype(jnp.int32)


def block_levels(own_key, extent, shards, least, largest):
    def one(axis_at, shards_of):
        heights = jax.random.uniform(jax.random.fold_in(jax.random.fold_in(own_key, 6), axis_at), (shards_of,), jnp.float32, least / len(shards), largest / len(shards))
        return jnp.repeat(jnp.exp(heights), extent[axis_at] // shards_of).reshape((-1,) + (1,) * (len(extent) - axis_at - 1))

    loudness = one(*shards[0])
    for cut in shards[1:]:
        loudness = loudness * one(*cut)
    return loudness


def normal_values(rng, dims, spread, bound, pieces=(), kind=jnp.bfloat16):
    entries = spread * jax.random.normal(rng, dims, jnp.float32)
    if pieces:
        entries = entries * block_levels(rng, dims, pieces, -0.22, 0.18)
    return jnp.clip(entries, -bound, bound).astype(kind)


def setup_inputs(seed: int = 0) -> dict:
    splits = jax.random.split(jax.random.key(seed), 7)
    return {
        "queries": draw_queries(jax.random.fold_in(splits[6], 71), 0),
        "d_out": normal_values(splits[1], (TOKENS, HEADS * RANK), 4.0, 24.0, ((0, 16), (1, 2))),
        "branch_latent": draw_branch_latent(jax.random.fold_in(splits[6], 71), 0),
        "trunk_latent": normal_values(splits[3], (TRUNK_BLOCKS, BLK, LATENT), 1.0, 6.0, ((0, 16),)),
        "ancestors": draw_ancestors(jax.random.fold_in(splits[6], 71), 0),
        "anc_count": draw_anc_count(jax.random.fold_in(splits[6], 71), 0),
    }


def reference(queries, d_out, branch_latent, trunk_latent, ancestors, anc_count):
    score_scale = float(QK_HEAD) ** -0.5
    far_rows = ANC * BLK

    def one_branch(branch):
        start = branch * BR_DEV
        query_heads = lax.dynamic_slice_in_dim(queries, start, BR_DEV, 0).reshape(BR_DEV, HEADS, LATENT).astype(jnp.float32)
        grad_heads = lax.dynamic_slice_in_dim(d_out, start, BR_DEV, 0).reshape(BR_DEV, HEADS, RANK).astype(jnp.float32)
        own_rows = lax.dynamic_slice_in_dim(branch_latent, start, BR_DEV, 0)
        listed = ancestors[branch]
        own_count = anc_count[branch]
        far_data = jnp.take(trunk_latent, listed, axis=0).reshape(far_rows, LATENT)
        key_rows = jnp.concatenate([far_data, own_rows], axis=0).astype(jnp.float32)
        far_ok = (jnp.arange(far_rows, dtype=jnp.int32) // BLK) < own_count
        causal = jnp.arange(BR_DEV, dtype=jnp.int32)[None, :] <= jnp.arange(BR_DEV, dtype=jnp.int32)[:, None]
        allowed = jnp.concatenate([jnp.broadcast_to(far_ok[None, :], (BR_DEV, far_rows)), causal], axis=1)
        scores = jnp.einsum("thc,kc->htk", query_heads, key_rows) * score_scale
        scores = jnp.where(allowed[None], scores, -1e30)
        row_max = jnp.max(scores, axis=2, keepdims=True)
        expo = jnp.exp(scores - row_max)
        attn = expo / jnp.sum(expo, axis=2, keepdims=True)
        attn_low = lax.optimization_barrier(attn.astype(jnp.bfloat16)).astype(jnp.float32)
        d_prob = jnp.einsum("thr,kr->htk", grad_heads, key_rows[:, :RANK])
        row_delta = jnp.sum(attn * d_prob, axis=2, keepdims=True)
        d_score = lax.optimization_barrier((attn * (d_prob - row_delta)).astype(jnp.bfloat16)).astype(jnp.float32)
        d_query = (jnp.einsum("htk,kc->thc", d_score, key_rows) * score_scale).astype(jnp.bfloat16)
        d_key = jnp.einsum("htk,thc->kc", d_score, query_heads) * score_scale
        d_value = jnp.einsum("htk,thr->kr", attn_low, grad_heads)
        d_key = d_key + jnp.pad(d_value, ((0, 0), (0, LATENT - RANK)))
        return d_query.reshape(BR_DEV, HEADS * LATENT), d_key

    branches = jnp.arange(N_LEAF, dtype=jnp.int32)
    d_query_all, d_key_all = lax.map(one_branch, branches)
    d_queries = d_query_all.reshape(TOKENS, HEADS * LATENT)
    d_branch = d_key_all[:, far_rows:].reshape(TOKENS, LATENT)
    far_grad = d_key_all[:, :far_rows].reshape(N_LEAF * ANC, BLK, LATENT)
    d_trunk = jnp.zeros((TRUNK_BLOCKS, BLK, LATENT), jnp.float32).at[ancestors.reshape(-1)].add(far_grad)
    return d_queries, d_branch, d_trunk
```

```python
import functools
import math

import jax
import jax.numpy as jnp
from jax import lax
from jax.experimental import pallas as pl
from jax.experimental.pallas import tpu as pltpu
from jax.sharding import PartitionSpec as P

RANK = 512
QK_HEAD = 192
LATENT = 576
BLK = 8
CAP = 2
ANC = 32
LANES = 128
PAIRS = 4
MASKED = -1e30
NT = (((1,), (1,)), ((), ()))
NN = (((1,), (0,)), ((), ()))
TN = (((0,), (0,)), ((), ()))


def mm(a, b, dims):
    return lax.dot_general(a, b, dims, preferred_element_type=jnp.float32)


def pieces(total, size):
    return [(at, min(size, total - at)) for at in range(0, total, size)]


def attn_kernel(
    far_bias, far, own, q, do, dq, dk,
    keys_e, keys_o, bias, q_e, q_o, do_e, do_o, s_e, s_o, dp_e, dp_o, p_e, p_o, ds_e, ds_o,
    acc_e, acc_o, acc_v, mid,
):
    far_rows, own_rows = far.shape[0], own.shape[0]
    rows = far_rows + own_rows
    tok = q.shape[0]
    stack = PAIRS * tok
    width = keys_e.shape[1]
    half = width - LATENT
    scale = float(QK_HEAD) ** -0.5
    exp_scale = scale * math.log2(math.e)
    step = pl.program_id(0)

    @pl.when(step == 0)
    def _():
        joined = jnp.concatenate([far[...], own[...]], axis=0).astype(jnp.float32)
        padded = jnp.concatenate([joined, jnp.zeros((rows, half), jnp.float32)], axis=1)
        keys_e[...] = padded.astype(jnp.bfloat16)
        keys_o[...] = pltpu.roll(padded, half, axis=1).astype(jnp.bfloat16)
        bias[:far_rows] = jnp.broadcast_to(far_bias[...], (far_rows, stack))
        key_at = lax.broadcasted_iota(jnp.int32, (own_rows, tok), 0)
        tok_at = lax.broadcasted_iota(jnp.int32, (own_rows, tok), 1)
        causal = jnp.where(key_at <= tok_at, 0.0, MASKED).astype(jnp.float32)
        bias[far_rows:] = jnp.concatenate([causal] * PAIRS, axis=1)
        acc_e[...] = jnp.zeros_like(acc_e)
        acc_o[...] = jnp.zeros_like(acc_o)
        acc_v[...] = jnp.zeros_like(acc_v)

    keys = (keys_e, keys_o)
    q_st, do_st = (q_e, q_o), (do_e, do_o)
    s_st, dp_st, p_st, ds_st = (s_e, s_o), (dp_e, dp_o), (p_e, p_o), (ds_e, ds_o)
    accs = (acc_e, acc_o)

    for pair in range(PAIRS):
        at = pair * 2 * LATENT
        block = pl.ds(pair * tok, tok)
        q_e[block, :] = q[:, at:at + width]
        q_o[block, :] = q[:, at + LATENT - half:at + 2 * LATENT]
        do_e[block, :] = do[:, pair * 2 * RANK:pair * 2 * RANK + RANK]
        do_o[block, :] = do[:, pair * 2 * RANK + RANK:(pair + 1) * 2 * RANK]

    def score(par, at, size):
        toks = pl.ds(at, size)
        s_st[par][:, toks] = mm(keys[par][...], q_st[par][toks, :], NT) + bias[:, toks]
        dp_st[par][:, toks] = mm(keys_e[:, :RANK], do_st[par][toks, :], NT)

    chunk = 64

    def soft(par, at):
        lane = pl.ds(at, LANES)
        s, dp, p_out, ds_out = s_st[par], dp_st[par], p_st[par], ds_st[par]
        chunks = pieces(rows, chunk)

        def fold(x):
            return x.reshape(-1, 8, LANES)

        top = None
        for r, n in chunks:
            part = jnp.max(fold(s[pl.ds(r, n), lane]), axis=0)
            top = part if top is None else jnp.maximum(top, part)
        top = jnp.max(top, axis=0, keepdims=True)
        total = jnp.zeros((8, LANES), jnp.float32)
        delta = jnp.zeros((8, LANES), jnp.float32)
        for r, n in chunks:
            e = jnp.exp2((s[pl.ds(r, n), lane] - top) * exp_scale)
            s[pl.ds(r, n), lane] = e
            total += jnp.sum(fold(e), axis=0)
            delta += jnp.sum(fold(e * dp[pl.ds(r, n), lane]), axis=0)
        inv = 1.0 / jnp.sum(total, axis=0, keepdims=True)
        delta = jnp.sum(delta, axis=0, keepdims=True) * inv
        for r, n in chunks:
            p = s[pl.ds(r, n), lane] * inv
            p_out[pl.ds(r, n), lane] = p.astype(jnp.bfloat16)
            ds_out[pl.ds(r, n), lane] = (p * (dp[pl.ds(r, n), lane] - delta)).astype(jnp.bfloat16)

    def grad_keys(par, at, size):
        cols = pl.ds(at, size)
        accs[par][:, cols] += mm(ds_st[par][...], q_st[par][:, cols], NN)

    def grad_values(par, at, size):
        cols = pl.ds(at, size)
        acc_v[:, cols] += mm(p_st[par][...], do_st[par][:, cols], NN)

    def grad_queries(par, pair):
        toks = pl.ds(pair * tok, tok)
        out = mm(ds_st[par][:, toks], keys[par][...], TN)
        at = pair * 2 * LATENT
        low = LATENT - half
        if par == 0:
            dq[:, at:at + low] = (out[:, :low] * scale).astype(dq.dtype)
            mid[toks, :] = out[:, low:]
        else:
            joint = out[:, :2 * half] + mid[toks, :]
            dq[:, at + low:at + low + 2 * half] = (joint * scale).astype(dq.dtype)
            dq[:, at + low + 2 * half:at + 2 * LATENT] = (out[:, 2 * half:] * scale).astype(dq.dtype)

    def outs(par):
        jobs = [functools.partial(grad_values, par, *piece) for piece in pieces(RANK, 256)]
        jobs += [functools.partial(grad_keys, par, *piece) for piece in pieces(width, 256)]
        jobs += [functools.partial(grad_queries, par, pair) for pair in range(PAIRS)]
        return jobs

    def softs(par):
        return [functools.partial(soft, par, at) for at in range(0, stack, LANES)]

    def scores(par):
        return [functools.partial(score, par, *piece) for piece in pieces(stack, 256)]

    def together(first, second):
        most = max(len(first), len(second))
        done_a = done_b = 0
        for i in range(1, most + 1):
            while done_a * most < i * len(first):
                first[done_a]()
                done_a += 1
            while done_b * most < i * len(second):
                second[done_b]()
                done_b += 1

    together(scores(0), [])
    together(scores(1), softs(0))
    together(outs(0), softs(1))
    together(outs(1), [])

    @pl.when(step == pl.num_programs(0) - 1)
    def _():
        shifted = pltpu.roll(acc_o[...], width - half, axis=1)
        both = (acc_e[...] + shifted) * scale
        dk[:, :RANK] = both[:, :RANK] + acc_v[...]
        dk[:, RANK:] = both[:, RANK:LATENT]


def attention(far_bias, far, own, queries, d_out):
    tok = queries.shape[0]
    heads = queries.shape[1] // LATENT
    steps = heads // (2 * PAIRS)
    far_rows, own_rows = far.shape[0], own.shape[0]
    rows = far_rows + own_rows
    stack = PAIRS * tok
    width = LATENT + 64
    bf16, f32 = jnp.bfloat16, jnp.float32

    def whole(i):
        return (0, 0)

    def along(i):
        return (0, i)

    scratch = [
        pltpu.VMEM((rows, width), bf16), pltpu.VMEM((rows, width), bf16),
        pltpu.VMEM((rows, stack), f32),
        pltpu.VMEM((stack, width), bf16), pltpu.VMEM((stack, width), bf16),
        pltpu.VMEM((stack, RANK), bf16), pltpu.VMEM((stack, RANK), bf16),
        pltpu.VMEM((rows, stack), f32), pltpu.VMEM((rows, stack), f32),
        pltpu.VMEM((rows, stack), f32), pltpu.VMEM((rows, stack), f32),
        pltpu.VMEM((rows, stack), bf16), pltpu.VMEM((rows, stack), bf16),
        pltpu.VMEM((rows, stack), bf16), pltpu.VMEM((rows, stack), bf16),
        pltpu.VMEM((rows, width), f32), pltpu.VMEM((rows, width), f32),
        pltpu.VMEM((rows, RANK), f32),
        pltpu.VMEM((stack, 128), f32),
    ]
    return pl.pallas_call(
        attn_kernel,
        grid=(steps,),
        in_specs=[
            pl.BlockSpec((far_rows, 1), whole),
            pl.BlockSpec((far_rows, LATENT), whole),
            pl.BlockSpec((own_rows, LATENT), whole),
            pl.BlockSpec((tok, 2 * PAIRS * LATENT), along),
            pl.BlockSpec((tok, 2 * PAIRS * RANK), along),
        ],
        out_specs=[
            pl.BlockSpec((tok, 2 * PAIRS * LATENT), along),
            pl.BlockSpec((rows, LATENT), whole),
        ],
        out_shape=[
            jax.ShapeDtypeStruct(queries.shape, queries.dtype),
            jax.ShapeDtypeStruct((rows, LATENT), f32),
        ],
        scratch_shapes=scratch,
        compiler_params=pltpu.CompilerParams(vmem_limit_bytes=56 * 1024 * 1024),
        cost_estimate=pl.CostEstimate(
            flops=2 * tok * heads * rows * (3 * LATENT + 2 * RANK),
            bytes_accessed=tok * heads * (4 * LATENT + 2 * RANK),
            transcendentals=tok * heads * rows,
        ),
    )(far_bias, far, own, queries, d_out)


def local(queries, d_out, branch_latent, trunk_latent, ancestors, anc_count):
    tok_rows = queries.shape[0]
    leafs = lax.axis_size("leaf")
    head_parts = lax.axis_size("head")
    me = lax.axis_index("leaf")
    my_part = lax.axis_index("head")
    trunk_count = trunk_latent.shape[0]
    far_rows = ANC * BLK

    owner_of = ancestors // trunk_count
    code = (ancestors % trunk_count) * ANC + jnp.arange(ANC, dtype=jnp.int32)[None, :]
    named = owner_of[:, None, :] == jnp.arange(leafs, dtype=jnp.int32)[None, :, None]
    none = trunk_count * ANC
    low = jnp.min(jnp.where(named, code[:, None, :], none), axis=2)
    high = jnp.max(jnp.where(named, code[:, None, :], -1), axis=2)
    codes = jnp.stack([low, high], axis=2)
    live = codes[:, :, 1:] >= 0
    asked = lax.dynamic_index_in_dim(codes, me, 1, keepdims=False)
    asked_live = lax.dynamic_index_in_dim(live, me, 1, keepdims=False)
    asked_block = jnp.where(asked_live, asked // ANC, -1).reshape(leafs * CAP)
    pick = asked_block[:, None] == jnp.arange(trunk_count, dtype=jnp.int32)[None, :]
    outgoing = mm(
        pick.astype(jnp.bfloat16), trunk_latent.reshape(trunk_count, BLK * LATENT), NN
    ).astype(jnp.bfloat16)
    incoming = lax.all_to_all(
        outgoing.reshape(leafs, CAP, BLK, LATENT), "leaf", split_axis=0, concat_axis=0, tiled=True
    ).reshape(leafs * CAP, BLK, LATENT)

    my_codes = lax.dynamic_index_in_dim(codes, me, 0, keepdims=False).reshape(leafs * CAP)
    my_live = jnp.repeat(lax.dynamic_index_in_dim(live, me, 0, keepdims=False).reshape(leafs), CAP)
    slot_of = my_codes % ANC
    own_count = lax.dynamic_index_in_dim(anc_count, me, 0, keepdims=False)
    packed = leafs * CAP == ANC
    if packed:
        far_slots = slot_of
        far = incoming
    else:
        hit = (slot_of[None, :] == jnp.arange(ANC, dtype=jnp.int32)[:, None]) & my_live[None, :]
        place = jnp.argmax(hit, axis=1)
        far_slots = jnp.arange(ANC, dtype=jnp.int32)
        far = jnp.take(incoming, place, axis=0)
    far_bias = jnp.where(far_slots < own_count, 0.0, MASKED).astype(jnp.float32)
    far_bias = jnp.repeat(far_bias, BLK)[:, None]

    d_queries, d_key = attention(
        far_bias, far.reshape(far_rows, LATENT), branch_latent, queries, d_out
    )

    far_grad = d_key[:far_rows].reshape(ANC, BLK, LATENT)
    if not packed:
        back = jnp.take(far_grad, jnp.where(my_live, slot_of, 0), axis=0)
        far_grad = jnp.where(my_live[:, None, None], back, 0.0)
    part_rows = BLK // head_parts
    sent = far_grad.reshape(leafs, CAP, head_parts, part_rows, LATENT).transpose(0, 2, 1, 3, 4)
    sent = sent.astype(jnp.bfloat16).reshape(leafs * head_parts, CAP, part_rows, LATENT)
    got = lax.all_to_all(sent, ("leaf", "head"), split_axis=0, concat_axis=0, tiled=True)
    sources = jnp.broadcast_to(asked_block.reshape(leafs, 1, CAP), (leafs, head_parts, CAP)).reshape(-1)
    place = jnp.arange(trunk_count, dtype=jnp.int32)[:, None] == sources[None, :]
    d_trunk = mm(
        place.astype(jnp.bfloat16), got.reshape(leafs * head_parts * CAP, part_rows * LATENT), NN
    ).reshape(trunk_count, part_rows, LATENT)

    own_grad = d_key[far_rows:].reshape(head_parts, tok_rows // head_parts, LATENT)
    d_branch = lax.dynamic_index_in_dim(own_grad, my_part, 0, keepdims=False)
    for hop in range(1, head_parts):
        theirs = lax.dynamic_index_in_dim(own_grad, (my_part + hop) % head_parts, 0, keepdims=False)
        route = [(i, (i + hop) % head_parts) for i in range(head_parts)]
        d_branch = d_branch + lax.ppermute(theirs, "head", route)
    return d_queries, d_branch, d_trunk


def solution(mesh):
    return jax.shard_map(
        local,
        mesh=mesh,
        in_specs=(
            P("leaf", "head"),
            P("leaf", "head"),
            P("leaf", None),
            P("leaf", None, None),
            P(),
            P(),
        ),
        out_specs=(P("leaf", "head"), P(("leaf", "head"), None), P("leaf", "head", None)),
        check_vma=False,
    )
```

```python
import functools
import math

import jax
import jax.numpy as jnp
from jax import lax
from jax.experimental import pallas as pl
from jax.experimental.pallas import tpu as pltpu
from jax.sharding import PartitionSpec as P

RANK = 512
QK_HEAD = 192
LATENT = 576
BLK = 8
CAP = 2
ANC = 32
LEAST_LIVE = 24
LANES = 128
WIDTH = 640
HALF = WIDTH - LATENT
PAIRS = 4
MASKED = -1e30
FAR_OFF = 1 << 20
SCALE = float(QK_HEAD) ** -0.5
EXP_SCALE = SCALE * math.log2(math.e)
MIB = 1024 * 1024
NT = (((1,), (1,)), ((), ()))
NN = (((1,), (0,)), ((), ()))
TN = (((0,), (0,)), ((), ()))


def mm(a, b, dims):
    return lax.dot_general(a, b, dims, preferred_element_type=jnp.float32)


def pieces(total, size):
    return [(at, min(size, total - at)) for at in range(0, total, size)]


def div(x, n):
    return x >> (n.bit_length() - 1) if n & (n - 1) == 0 else lax.div(x, jnp.full_like(x, n))


def mod(x, n):
    return x - div(x, n) * n


def column(rows):
    return lax.broadcasted_iota(jnp.int32, (rows, 1), 0)


def one_hot(place, size):
    lane = lax.broadcasted_iota(jnp.int32, (place.shape[0], size), 1)
    return jnp.where(lane == place, 1.0, 0.0).astype(jnp.bfloat16)


def token_part(tok):
    return 64 if tok % 64 == 0 else tok


def listed_blocks(ancestors, owned, second):
    leafs = ancestors.shape[0]
    rows = leafs * CAP * BLK
    named = ancestors[...].astype(jnp.float32)
    named = jnp.broadcast_to(named[:, None, :], (leafs, CAP * BLK, ANC)).reshape(rows, ANC)
    first = lax.axis_index("leaf") * owned
    low_end = first.astype(jnp.float32)
    mine = (named >= low_end) & (named < low_end + owned)
    low = jnp.min(jnp.where(mine, named, float(FAR_OFF)), axis=1, keepdims=True)
    high = jnp.max(jnp.where(mine, named, -1.0), axis=1, keepdims=True)
    return jnp.where(second, high, low).astype(jnp.int32) - first


def pick_kernel(ancestors, trunk, out):
    owned = trunk.shape[0] // BLK
    row = column(out.shape[0])
    block = listed_blocks(ancestors, owned, mod(div(row, BLK), CAP) == 1)
    sel = one_hot(block * BLK + mod(row, BLK), trunk.shape[0])
    out[...] = mm(sel, trunk[...], NN).astype(out.dtype)


def pick(ancestors, trunk):
    rows = ancestors.shape[0] * CAP * BLK
    return pl.pallas_call(
        pick_kernel,
        out_shape=jax.ShapeDtypeStruct((rows, LATENT), trunk.dtype),
        name="pick_blocks",
    )(ancestors, trunk)


def finish_kernel(ancestors, got, mine, *rest):
    theirs, (d_branch, d_trunk) = rest[:-2], rest[-2:]
    owned, part_rows = d_trunk.shape[0], d_trunk.shape[1]
    row = column(got.shape[0])
    block = listed_blocks(ancestors, owned, mod(div(row, part_rows), CAP) == 1)
    sel = one_hot(block * part_rows + mod(row, part_rows), owned * part_rows)
    total = mm(sel, got[...], TN)
    for b in range(owned):
        d_trunk[b] = total[b * part_rows:(b + 1) * part_rows]
    own = mine[...]
    for other in theirs:
        own = own + other[...]
    d_branch[...] = own


def finish(ancestors, got, mine, theirs, owned, part_rows):
    return pl.pallas_call(
        finish_kernel,
        out_shape=[
            jax.ShapeDtypeStruct(mine.shape, jnp.float32),
            jax.ShapeDtypeStruct((owned, part_rows, LATENT), jnp.float32),
        ],
        name="sum_gradients",
    )(ancestors, got, mine, *theirs)


def slot_places(ancestors, owned):
    row = column(ANC * BLK)
    mine = ancestors[pl.ds(lax.axis_index("leaf"), 1), :].astype(jnp.float32)
    mine = jnp.broadcast_to(mine, (ANC * BLK, ANC))
    lane = lax.broadcasted_iota(jnp.int32, (ANC * BLK, ANC), 1)
    block = jnp.max(jnp.where(lane == div(row, BLK), mine, -1.0), axis=1, keepdims=True)
    owner = div(block.astype(jnp.int32), owned)
    low_end = (owner * owned).astype(jnp.float32)
    below = (mine >= low_end) & (mine < block)
    second = jnp.max(jnp.where(below, 1.0, 0.0), axis=1, keepdims=True).astype(jnp.int32)
    return row, owner, second


def attn_kernel(
    owned, head_parts, anc_count, ancestors, incoming, own, q, do, ds, keys_e, keys_o, sent, *rest
):
    own_parts = rest[:head_parts]
    far_bias, causal, s_e, s_o, dp_e, dp_o, p_e, p_o, acc_e, acc_o, acc_v = rest[head_parts:]
    tok = q.shape[0]
    far_rows, rows = ANC * BLK, ANC * BLK + tok
    sub = token_part(tok)
    parts = tok // sub
    stack = PAIRS * sub
    least = LEAST_LIVE * BLK
    step = pl.program_id(0)

    @pl.when(step == 0)
    def _():
        row, owner, second = slot_places(ancestors, owned)
        sel = one_hot((owner * CAP + second) * BLK + mod(row, BLK), incoming.shape[0])
        far = mm(sel, incoming[...], NN)
        joined = jnp.concatenate([far, own[...].astype(jnp.float32)], axis=0)
        padded = jnp.concatenate([joined, jnp.zeros((rows, HALF), jnp.float32)], axis=1)
        keys_e[...] = padded.astype(jnp.bfloat16)
        keys_o[...] = pltpu.roll(padded, HALF, axis=1).astype(jnp.bfloat16)
        live = anc_count[lax.axis_index("leaf")]
        slot = div(lax.broadcasted_iota(jnp.int32, far_bias.shape, 0) + least, BLK)
        far_bias[...] = jnp.where(slot < live, 0.0, MASKED)
        key_at = lax.broadcasted_iota(jnp.int32, (sub, stack), 0)
        tok_at = mod(lax.broadcasted_iota(jnp.int32, (sub, stack), 1), sub)
        causal[...] = jnp.where(key_at <= tok_at, 0.0, MASKED)
        acc_e[...] = jnp.zeros_like(acc_e)
        acc_o[...] = jnp.zeros_like(acc_o)
        acc_v[...] = jnp.zeros_like(acc_v)

    keys = (keys_e, keys_o)
    s_st, dp_st, p_st, accs = (s_e, s_o), (dp_e, dp_o), (p_e, p_o), (acc_e, acc_o)

    def stacked(ref, j, first, pitch, at, size):
        toks = pl.ds(j * sub, sub)
        return jnp.concatenate(
            [ref[toks, pl.ds(first + i * pitch + at, size)] for i in range(PAIRS)], axis=0
        )

    def queries(par, j, at=0, size=WIDTH):
        return stacked(q, j, par * (LATENT - HALF), 2 * LATENT, at, size)

    def grads(par, j, at=0, size=RANK):
        return stacked(do, j, par * RANK, 2 * RANK, at, size)

    def seen(j):
        return far_rows + (j + 1) * sub

    def score(par, j):
        n, cols = seen(j), pl.ds(j * stack, stack)
        out = mm(keys[par][:n, :], queries(par, j), NT)
        s = s_st[par]
        s[:least, cols] = out[:least]
        s[least:far_rows, cols] = out[least:far_rows] + far_bias[...]
        if j > 0:
            s[far_rows:n - sub, cols] = out[far_rows:n - sub]
        s[n - sub:n, cols] = out[n - sub:] + causal[...]

    def prob(par, j):
        n, cols = seen(j), pl.ds(j * stack, stack)
        dp_st[par][:n, cols] = mm(keys_e[:n, :RANK], grads(par, j), NT)

    def soft(par, j, at):
        lane = pl.ds(j * stack + at, LANES)
        out_lane = pl.ds((par * parts + j) * stack + at, LANES)
        s, dp, p_out = s_st[par], dp_st[par], p_st[par]
        chunks = pieces(seen(j), 64)

        def fold(x):
            return x.reshape(-1, 8, LANES)

        top = None
        for r, n in chunks:
            part = jnp.max(fold(s[pl.ds(r, n), lane]), axis=0)
            top = part if top is None else jnp.maximum(top, part)
        top = jnp.max(top, axis=0, keepdims=True)
        total = jnp.zeros((8, LANES), jnp.float32)
        delta = jnp.zeros((8, LANES), jnp.float32)
        for r, n in chunks:
            e = jnp.exp2((s[pl.ds(r, n), lane] - top) * EXP_SCALE)
            s[pl.ds(r, n), lane] = e
            total += jnp.sum(fold(e), axis=0)
            delta += jnp.sum(fold(e * dp[pl.ds(r, n), lane]), axis=0)
        inv = 1.0 / jnp.sum(total, axis=0, keepdims=True)
        delta = jnp.sum(delta, axis=0, keepdims=True) * inv
        for r, n in chunks:
            p = s[pl.ds(r, n), lane] * inv
            p_out[pl.ds(r, n), lane] = p.astype(jnp.bfloat16)
            ds[0, pl.ds(r, n), out_lane] = (p * (dp[pl.ds(r, n), lane] - delta)).astype(ds.dtype)

    def grad_keys(par, j, at, size):
        n = seen(j)
        cols = pl.ds(at, size)
        d = ds[0, :n, pl.ds((par * parts + j) * stack, stack)]
        accs[par][:n, cols] += mm(d, queries(par, j, at, size), NN)

    def grad_values(par, j, at, size):
        n = seen(j)
        p = p_st[par][:n, pl.ds(j * stack, stack)]
        acc_v[:n, pl.ds(at, size)] += mm(p, grads(par, j, at, size), NN)

    units = [(par, j) for par in range(2) for j in range(parts)]

    def jobs_of(i):
        first, second, third = [], [], []
        if i < len(units):
            first = [functools.partial(score, *units[i]), functools.partial(prob, *units[i])]
        if 0 <= i - 1 < len(units):
            second = [functools.partial(soft, *units[i - 1], at) for at in range(0, stack, LANES)]
        if 0 <= i - 2 < len(units):
            unit = units[i - 2]
            third = [functools.partial(grad_values, *unit, *c) for c in pieces(RANK, 256)]
            third += [functools.partial(grad_keys, *unit, *c) for c in pieces(WIDTH, 256)]
        jobs = [first, second, third]
        order = [(k / len(group), g, job) for g, group in enumerate(jobs) for k, job in enumerate(group)]
        return [job for _, _, job in sorted(order, key=lambda item: item[:2])]

    for i in range(len(units) + 2):
        for job in jobs_of(i):
            job()

    @pl.when(step == pl.num_programs(0) - 1)
    def _():
        shifted = pltpu.roll(acc_o[...], WIDTH - HALF, axis=1)
        acc_e[...] = (acc_e[...] + shifted) * SCALE
        acc_e[:, :RANK] += acc_v[...]
        part_rows = BLK // head_parts
        row, owner, second = slot_places(ancestors, owned)
        inner = mod(row, BLK)
        place = (owner * head_parts + div(inner, part_rows)) * CAP + second
        place = place * part_rows + mod(inner, part_rows)
        sel = one_hot(place, sent.shape[0])
        far = acc_e[:far_rows, :LATENT].astype(jnp.bfloat16)
        sent[...] = mm(sel, far, TN).astype(sent.dtype)
        own_rows = tok // head_parts
        for hop, out in enumerate(own_parts):
            part = lax.rem(lax.axis_index("head") + hop, head_parts)
            at = pl.multiple_of(far_rows + part * own_rows, 8)
            out[...] = acc_e[pl.ds(at, own_rows), :LATENT]


def attention(owned, head_parts, anc_count, ancestors, incoming, own, queries, d_out):
    tok = queries.shape[0]
    heads = queries.shape[1] // LATENT
    steps = heads // (2 * PAIRS)
    far_rows, rows = ANC * BLK, ANC * BLK + tok
    toks = PAIRS * tok
    stack = PAIRS * token_part(tok)
    bf16, f32 = jnp.bfloat16, jnp.float32

    def whole(i):
        return (0, 0)

    def along(i):
        return (0, i)

    own_part = (tok // head_parts, LATENT)
    return pl.pallas_call(
        functools.partial(attn_kernel, owned, head_parts),
        grid=(steps,),
        in_specs=[
            pl.BlockSpec(memory_space=pltpu.SMEM),
            pl.BlockSpec(ancestors.shape, whole),
            pl.BlockSpec(incoming.shape, whole),
            pl.BlockSpec(own.shape, whole),
            pl.BlockSpec((tok, 2 * PAIRS * LATENT), along),
            pl.BlockSpec((tok, 2 * PAIRS * RANK), along),
        ],
        out_specs=[
            pl.BlockSpec((1, rows, 2 * toks), lambda i: (i, 0, 0)),
            pl.BlockSpec((rows, WIDTH), whole),
            pl.BlockSpec((rows, WIDTH), whole),
            pl.BlockSpec(incoming.shape, whole),
        ] + [pl.BlockSpec(own_part, whole)] * head_parts,
        out_shape=[
            jax.ShapeDtypeStruct((steps, rows, 2 * toks), bf16),
            jax.ShapeDtypeStruct((rows, WIDTH), bf16),
            jax.ShapeDtypeStruct((rows, WIDTH), bf16),
            jax.ShapeDtypeStruct(incoming.shape, bf16),
        ] + [jax.ShapeDtypeStruct(own_part, f32)] * head_parts,
        scratch_shapes=[
            pltpu.VMEM((far_rows - LEAST_LIVE * BLK, stack), f32),
            pltpu.VMEM((token_part(tok), stack), f32),
            pltpu.VMEM((rows, toks), f32), pltpu.VMEM((rows, toks), f32),
            pltpu.VMEM((rows, toks), f32), pltpu.VMEM((rows, toks), f32),
            pltpu.VMEM((rows, toks), bf16), pltpu.VMEM((rows, toks), bf16),
            pltpu.VMEM((rows, WIDTH), f32), pltpu.VMEM((rows, WIDTH), f32),
            pltpu.VMEM((rows, RANK), f32),
        ],
        compiler_params=pltpu.CompilerParams(vmem_limit_bytes=48 * MIB),
        cost_estimate=pl.CostEstimate(
            flops=2 * tok * heads * rows * (2 * LATENT + 2 * RANK),
            bytes_accessed=2 * tok * heads * (LATENT + RANK + rows),
            transcendentals=tok * heads * rows,
        ),
        name="score_gradients",
    )(anc_count, ancestors, incoming, own, queries, d_out)


def query_kernel(keys_e, keys_o, ds, dq):
    tok = dq.shape[0]
    rows = ds.shape[1]
    sub = token_part(tok)
    parts = tok // sub
    stack = PAIRS * sub
    low = LATENT - HALF
    for j in range(parts):
        n = rows - tok + (j + 1) * sub
        even = mm(ds[0, :n, pl.ds(j * stack, stack)], keys_e[:n, :], TN) * SCALE
        odd = mm(ds[0, :n, pl.ds((parts + j) * stack, stack)], keys_o[:n, :], TN) * SCALE
        for i in range(PAIRS):
            at = i * 2 * LATENT
            part = slice(i * sub, (i + 1) * sub)
            toks = pl.ds(j * sub, sub)
            dq[toks, at:at + low] = even[part, :low].astype(dq.dtype)
            joint = even[part, low:] + odd[part, :2 * HALF]
            dq[toks, at + low:at + low + 2 * HALF] = joint.astype(dq.dtype)
            dq[toks, at + low + 2 * HALF:at + 2 * LATENT] = odd[part, 2 * HALF:].astype(dq.dtype)


def query_gradients(keys_e, keys_o, ds, queries):
    tok = queries.shape[0]
    heads = queries.shape[1] // LATENT
    steps, rows = ds.shape[0], ds.shape[1]
    return pl.pallas_call(
        query_kernel,
        grid=(steps,),
        in_specs=[
            pl.BlockSpec(keys_e.shape, lambda i: (0, 0)),
            pl.BlockSpec(keys_o.shape, lambda i: (0, 0)),
            pl.BlockSpec((1,) + ds.shape[1:], lambda i: (i, 0, 0)),
        ],
        out_specs=pl.BlockSpec((tok, 2 * PAIRS * LATENT), lambda i: (0, i)),
        out_shape=jax.ShapeDtypeStruct(queries.shape, queries.dtype),
        compiler_params=pltpu.CompilerParams(vmem_limit_bytes=32 * MIB),
        cost_estimate=pl.CostEstimate(
            flops=2 * tok * heads * rows * LATENT,
            bytes_accessed=2 * tok * heads * (LATENT + rows),
            transcendentals=0,
        ),
        name="query_gradients",
    )(keys_e, keys_o, ds)


def local(queries, d_out, branch_latent, trunk_latent, ancestors, anc_count):
    leafs = lax.axis_size("leaf")
    head_parts = lax.axis_size("head")
    owned = trunk_latent.shape[0]
    part_rows = BLK // head_parts

    outgoing = pick(ancestors, trunk_latent.reshape(owned * BLK, LATENT))
    incoming = lax.all_to_all(
        outgoing.reshape(leafs, CAP * BLK, LATENT), "leaf", split_axis=0, concat_axis=0, tiled=True
    ).reshape(leafs * CAP * BLK, LATENT)

    ds, keys_e, keys_o, sent, mine, *others = attention(
        owned, head_parts, anc_count, ancestors, incoming, branch_latent, queries, d_out
    )

    got = lax.all_to_all(
        sent.reshape(leafs * head_parts, CAP * part_rows, LATENT),
        ("leaf", "head"), split_axis=0, concat_axis=0, tiled=True,
    ).reshape(leafs * CAP * BLK, LATENT)
    theirs = []
    for hop, part in enumerate(others, 1):
        route = [(i, (i + hop) % head_parts) for i in range(head_parts)]
        theirs.append(lax.ppermute(part, "head", route))

    d_queries = query_gradients(keys_e, keys_o, ds, queries)
    d_branch, d_trunk = finish(ancestors, got, mine, theirs, owned, part_rows)
    return d_queries, d_branch, d_trunk


def solution(mesh):
    return jax.shard_map(
        local,
        mesh=mesh,
        in_specs=(
            P("leaf", "head"),
            P("leaf", "head"),
            P("leaf", None),
            P("leaf", None, None),
            P(),
            P(),
        ),
        out_specs=(P("leaf", "head"), P(("leaf", "head"), None), P("leaf", "head", None)),
        check_vma=False,
    )
```

```python
import functools
import math

import jax
import jax.numpy as jnp
from jax import lax
from jax.experimental import pallas as pl
from jax.experimental.pallas import tpu as pltpu
from jax.sharding import PartitionSpec as P

RANK = 512
QK_HEAD = 192
LATENT = 576
BLK = 8
CAP = 2
ANC = 32
LEAST_LIVE = 24
LANES = 128
WIDTH = 640
HALF = WIDTH - LATENT
PAIRS = 4
MASKED = -1e30
FAR_OFF = 1 << 20
SCALE = float(QK_HEAD) ** -0.5
EXP_SCALE = SCALE * math.log2(math.e)
MIB = 1024 * 1024
NT = (((1,), (1,)), ((), ()))
NN = (((1,), (0,)), ((), ()))
TN = (((0,), (0,)), ((), ()))


def mm(a, b, dims):
    return lax.dot_general(a, b, dims, preferred_element_type=jnp.float32)


def pieces(total, size):
    return [(at, min(size, total - at)) for at in range(0, total, size)]


def div(x, n):
    return x >> (n.bit_length() - 1) if n & (n - 1) == 0 else lax.div(x, jnp.full_like(x, n))


def mod(x, n):
    return x - div(x, n) * n


def column(rows):
    return lax.broadcasted_iota(jnp.int32, (rows, 1), 0)


def one_hot(place, size):
    lane = lax.broadcasted_iota(jnp.int32, (place.shape[0], size), 1)
    return jnp.where(lane == place, 1.0, 0.0).astype(jnp.bfloat16)


def token_part(tok):
    return 64 if tok % 64 == 0 else tok


def listed_blocks(ancestors, owned, second):
    leafs = ancestors.shape[0]
    rows = leafs * CAP * BLK
    named = ancestors[...].astype(jnp.float32)
    named = jnp.broadcast_to(named[:, None, :], (leafs, CAP * BLK, ANC)).reshape(rows, ANC)
    first = lax.axis_index("leaf") * owned
    low_end = first.astype(jnp.float32)
    mine = (named >= low_end) & (named < low_end + owned)
    low = jnp.min(jnp.where(mine, named, float(FAR_OFF)), axis=1, keepdims=True)
    high = jnp.max(jnp.where(mine, named, -1.0), axis=1, keepdims=True)
    return jnp.where(second, high, low).astype(jnp.int32) - first


def pick_kernel(ancestors, trunk, out):
    owned = trunk.shape[0] // BLK
    row = column(out.shape[0])
    block = listed_blocks(ancestors, owned, mod(div(row, BLK), CAP) == 1)
    sel = one_hot(block * BLK + mod(row, BLK), trunk.shape[0])
    out[...] = mm(sel, trunk[...], NN).astype(out.dtype)


def pick(ancestors, trunk):
    rows = ancestors.shape[0] * CAP * BLK
    return pl.pallas_call(
        pick_kernel,
        out_shape=jax.ShapeDtypeStruct((rows, LATENT), trunk.dtype),
        name="pick_blocks",
    )(ancestors, trunk)


def finish_kernel(ancestors, got, mine, *rest):
    theirs, (d_branch, d_trunk) = rest[:-2], rest[-2:]
    owned, part_rows = d_trunk.shape[0], d_trunk.shape[1]
    row = column(got.shape[0])
    block = listed_blocks(ancestors, owned, mod(div(row, part_rows), CAP) == 1)
    sel = one_hot(block * part_rows + mod(row, part_rows), owned * part_rows)
    total = mm(sel, got[...], TN)
    for b in range(owned):
        d_trunk[b] = total[b * part_rows:(b + 1) * part_rows]
    own = mine[...]
    for other in theirs:
        own = own + other[...]
    d_branch[...] = own


def finish(ancestors, got, mine, theirs, owned, part_rows):
    return pl.pallas_call(
        finish_kernel,
        out_shape=[
            jax.ShapeDtypeStruct(mine.shape, jnp.float32),
            jax.ShapeDtypeStruct((owned, part_rows, LATENT), jnp.float32),
        ],
        compiler_params=pltpu.CompilerParams(vmem_limit_bytes=8 * MIB),
        name="sum_gradients",
    )(ancestors, got, mine, *theirs)


def slot_places(ancestors, owned):
    row = column(ANC * BLK)
    mine = ancestors[pl.ds(lax.axis_index("leaf"), 1), :].astype(jnp.float32)
    mine = jnp.broadcast_to(mine, (ANC * BLK, ANC))
    lane = lax.broadcasted_iota(jnp.int32, (ANC * BLK, ANC), 1)
    block = jnp.max(jnp.where(lane == div(row, BLK), mine, -1.0), axis=1, keepdims=True)
    owner = div(block.astype(jnp.int32), owned)
    low_end = (owner * owned).astype(jnp.float32)
    below = (mine >= low_end) & (mine < block)
    second = jnp.max(jnp.where(below, 1.0, 0.0), axis=1, keepdims=True).astype(jnp.int32)
    return row, owner, second


def attn_kernel(
    owned, head_parts, anc_count, ancestors, incoming, own, q, do, ds, keys_e, keys_o, sent, *rest
):
    own_parts = rest[:head_parts]
    far_bias, causal, q_st, s, dp, p_low, acc_k, acc_v = rest[head_parts:]
    tok = q.shape[0]
    far_rows, rows = ANC * BLK, ANC * BLK + tok
    sub = token_part(tok)
    parts = tok // sub
    stack = 2 * PAIRS * sub
    least = LEAST_LIVE * BLK
    step = pl.program_id(0)

    @pl.when(step == 0)
    def _():
        row, owner, second = slot_places(ancestors, owned)
        sel = one_hot((owner * CAP + second) * BLK + mod(row, BLK), incoming.shape[0])
        far = mm(sel, incoming[...], NN)
        joined = jnp.concatenate([far, own[...].astype(jnp.float32)], axis=0)
        padded = jnp.concatenate([joined, jnp.zeros((rows, HALF), jnp.float32)], axis=1)
        keys_e[...] = padded.astype(jnp.bfloat16)
        keys_o[...] = pltpu.roll(padded, HALF, axis=1).astype(jnp.bfloat16)
        live = anc_count[lax.axis_index("leaf")]
        slot = div(lax.broadcasted_iota(jnp.int32, far_bias.shape, 0) + least, BLK)
        far_bias[...] = jnp.where(slot < live, 0.0, MASKED)
        key_at = lax.broadcasted_iota(jnp.int32, (sub, stack), 0)
        tok_at = mod(lax.broadcasted_iota(jnp.int32, (sub, stack), 1), sub)
        causal[...] = jnp.where(key_at <= tok_at, 0.0, MASKED)
        acc_k[...] = jnp.zeros_like(acc_k)
        acc_v[...] = jnp.zeros_like(acc_v)

    def seen(j):
        return far_rows + (j + 1) * sub

    def lanes(j):
        return pl.ds(j * stack, stack)

    def fill(j):
        toks = pl.ds(j * sub, sub)
        for i in range(PAIRS):
            at = i * 2 * LATENT
            q_st[pl.ds(j * stack + i * sub, sub), :] = q[toks, at:at + WIDTH]
            odd = q[toks, at + LATENT - HALF:at + 2 * LATENT]
            odd = pltpu.roll(odd, WIDTH - HALF, axis=1)
            q_st[pl.ds(j * stack + (PAIRS + i) * sub, sub), :] = odd

    def grads(j):
        toks = pl.ds(j * sub, sub)
        heads = list(range(0, 2 * PAIRS, 2)) + list(range(1, 2 * PAIRS, 2))
        return jnp.concatenate([do[toks, pl.ds(h * RANK, RANK)] for h in heads], axis=0)

    def score(j):
        n, cols = seen(j), lanes(j)
        out = mm(keys_e[:n, :], q_st[cols, :], NT)
        s[:least, cols] = out[:least]
        s[least:far_rows, cols] = out[least:far_rows] + far_bias[...]
        if j > 0:
            s[far_rows:n - sub, cols] = out[far_rows:n - sub]
        s[n - sub:n, cols] = out[n - sub:] + causal[...]

    def prob(j):
        n = seen(j)
        dp[:n, lanes(j)] = mm(keys_e[:n, :RANK], grads(j), NT)

    def soft(j, at):
        lane = pl.ds(j * stack + at, LANES)
        chunks = pieces(seen(j), 64)

        def fold(x):
            return x.reshape(-1, 8, LANES)

        top = None
        for r, n in chunks:
            part = jnp.max(fold(s[pl.ds(r, n), lane]), axis=0)
            top = part if top is None else jnp.maximum(top, part)
        top = jnp.max(top, axis=0, keepdims=True)
        total = jnp.zeros((8, LANES), jnp.float32)
        delta = jnp.zeros((8, LANES), jnp.float32)
        for r, n in chunks:
            e = jnp.exp2((s[pl.ds(r, n), lane] - top) * EXP_SCALE)
            s[pl.ds(r, n), lane] = e
            total += jnp.sum(fold(e), axis=0)
            delta += jnp.sum(fold(e * dp[pl.ds(r, n), lane]), axis=0)
        inv = 1.0 / jnp.sum(total, axis=0, keepdims=True)
        delta = jnp.sum(delta, axis=0, keepdims=True) * inv
        for r, n in chunks:
            p = s[pl.ds(r, n), lane] * inv
            p_low[pl.ds(r, n), lane] = p.astype(jnp.bfloat16)
            ds[0, pl.ds(r, n), lane] = (p * (dp[pl.ds(r, n), lane] - delta)).astype(ds.dtype)

    def grad_values(j):
        n = seen(j)
        acc_v[:n, :] += mm(p_low[:n, lanes(j)], grads(j), NN)

    def grad_keys(j):
        n = seen(j)
        acc_k[:n, :] += mm(ds[0, :n, lanes(j)], q_st[lanes(j), :], NN)

    def jobs_of(i):
        groups = []
        if i < parts:
            groups.append([functools.partial(job, i) for job in (fill, score, prob)])
        if 0 <= i - 1 < parts:
            groups.append([functools.partial(soft, i - 1, at) for at in range(0, stack, LANES)])
        if 0 <= i - 2 < parts:
            groups.append([functools.partial(job, i - 2) for job in (grad_values, grad_keys)])
        order = [
            (k / len(group), g, job) for g, group in enumerate(groups) for k, job in enumerate(group)
        ]
        return [job for _, _, job in sorted(order, key=lambda item: item[:2])]

    for i in range(parts + 2):
        for job in jobs_of(i):
            job()

    @pl.when(step == pl.num_programs(0) - 1)
    def _():
        acc_k[...] = acc_k[...] * SCALE
        acc_k[:, :RANK] += acc_v[...]
        part_rows = BLK // head_parts
        row, owner, second = slot_places(ancestors, owned)
        inner = mod(row, BLK)
        place = (owner * head_parts + div(inner, part_rows)) * CAP + second
        place = place * part_rows + mod(inner, part_rows)
        sel = one_hot(place, sent.shape[0])
        far = acc_k[:far_rows, :LATENT].astype(jnp.bfloat16)
        sent[...] = mm(sel, far, TN).astype(sent.dtype)
        own_rows = tok // head_parts
        for hop, out in enumerate(own_parts):
            part = lax.rem(lax.axis_index("head") + hop, head_parts)
            at = pl.multiple_of(far_rows + part * own_rows, 8)
            out[...] = acc_k[pl.ds(at, own_rows), :LATENT]


def attention(owned, head_parts, anc_count, ancestors, incoming, own, queries, d_out):
    tok = queries.shape[0]
    heads = queries.shape[1] // LATENT
    steps = heads // (2 * PAIRS)
    far_rows, rows = ANC * BLK, ANC * BLK + tok
    toks = 2 * PAIRS * tok
    stack = 2 * PAIRS * token_part(tok)
    bf16, f32 = jnp.bfloat16, jnp.float32

    def whole(i):
        return (0, 0)

    def along(i):
        return (0, i)

    own_part = (tok // head_parts, LATENT)
    return pl.pallas_call(
        functools.partial(attn_kernel, owned, head_parts),
        grid=(steps,),
        in_specs=[
            pl.BlockSpec(memory_space=pltpu.SMEM),
            pl.BlockSpec(ancestors.shape, whole),
            pl.BlockSpec(incoming.shape, whole),
            pl.BlockSpec(own.shape, whole),
            pl.BlockSpec((tok, 2 * PAIRS * LATENT), along),
            pl.BlockSpec((tok, 2 * PAIRS * RANK), along),
        ],
        out_specs=[
            pl.BlockSpec((1, rows, toks), lambda i: (i, 0, 0)),
            pl.BlockSpec((rows, WIDTH), whole),
            pl.BlockSpec((rows, WIDTH), whole),
            pl.BlockSpec(incoming.shape, whole),
        ] + [pl.BlockSpec(own_part, whole)] * head_parts,
        out_shape=[
            jax.ShapeDtypeStruct((steps, rows, toks), bf16),
            jax.ShapeDtypeStruct((rows, WIDTH), bf16),
            jax.ShapeDtypeStruct((rows, WIDTH), bf16),
            jax.ShapeDtypeStruct(incoming.shape, bf16),
        ] + [jax.ShapeDtypeStruct(own_part, f32)] * head_parts,
        scratch_shapes=[
            pltpu.VMEM((far_rows - LEAST_LIVE * BLK, stack), f32),
            pltpu.VMEM((token_part(tok), stack), f32),
            pltpu.VMEM((toks, WIDTH), bf16),
            pltpu.VMEM((rows, toks), f32),
            pltpu.VMEM((rows, toks), f32),
            pltpu.VMEM((rows, toks), bf16),
            pltpu.VMEM((rows, WIDTH), f32),
            pltpu.VMEM((rows, RANK), f32),
        ],
        compiler_params=pltpu.CompilerParams(vmem_limit_bytes=60 * MIB),
        cost_estimate=pl.CostEstimate(
            flops=2 * tok * heads * rows * (2 * LATENT + 2 * RANK),
            bytes_accessed=2 * tok * heads * (LATENT + RANK + rows),
            transcendentals=tok * heads * rows,
        ),
        name="score_gradients",
    )(anc_count, ancestors, incoming, own, queries, d_out)


def query_kernel(keys_e, keys_o, ds, dq):
    tok = dq.shape[0]
    rows = ds.shape[1]
    sub = token_part(tok)
    parts = tok // sub
    stack = PAIRS * sub
    low = LATENT - HALF
    for j in range(parts):
        n = rows - tok + (j + 1) * sub
        even = mm(ds[0, :n, pl.ds(2 * j * stack, stack)], keys_e[:n, :], TN) * SCALE
        odd = mm(ds[0, :n, pl.ds((2 * j + 1) * stack, stack)], keys_o[:n, :], TN) * SCALE
        for i in range(PAIRS):
            at = i * 2 * LATENT
            part = slice(i * sub, (i + 1) * sub)
            toks = pl.ds(j * sub, sub)
            dq[toks, at:at + low] = even[part, :low].astype(dq.dtype)
            joint = even[part, low:] + odd[part, :2 * HALF]
            dq[toks, at + low:at + low + 2 * HALF] = joint.astype(dq.dtype)
            dq[toks, at + low + 2 * HALF:at + 2 * LATENT] = odd[part, 2 * HALF:].astype(dq.dtype)


def query_gradients(keys_e, keys_o, ds, queries):
    tok = queries.shape[0]
    heads = queries.shape[1] // LATENT
    steps, rows = ds.shape[0], ds.shape[1]
    return pl.pallas_call(
        query_kernel,
        grid=(steps,),
        in_specs=[
            pl.BlockSpec(keys_e.shape, lambda i: (0, 0)),
            pl.BlockSpec(keys_o.shape, lambda i: (0, 0)),
            pl.BlockSpec((1,) + ds.shape[1:], lambda i: (i, 0, 0)),
        ],
        out_specs=pl.BlockSpec((tok, 2 * PAIRS * LATENT), lambda i: (0, i)),
        out_shape=jax.ShapeDtypeStruct(queries.shape, queries.dtype),
        compiler_params=pltpu.CompilerParams(vmem_limit_bytes=60 * MIB),
        cost_estimate=pl.CostEstimate(
            flops=2 * tok * heads * rows * LATENT,
            bytes_accessed=2 * tok * heads * (LATENT + rows),
            transcendentals=0,
        ),
        name="query_gradients",
    )(keys_e, keys_o, ds)


def local(queries, d_out, branch_latent, trunk_latent, ancestors, anc_count):
    leafs = lax.axis_size("leaf")
    head_parts = lax.axis_size("head")
    owned = trunk_latent.shape[0]
    part_rows = BLK // head_parts

    outgoing = pick(ancestors, trunk_latent.reshape(owned * BLK, LATENT))
    incoming = lax.all_to_all(
        outgoing.reshape(leafs, CAP * BLK, LATENT), "leaf", split_axis=0, concat_axis=0, tiled=True
    ).reshape(leafs * CAP * BLK, LATENT)

    ds, keys_e, keys_o, sent, mine, *others = attention(
        owned, head_parts, anc_count, ancestors, incoming, branch_latent, queries, d_out
    )

    got = lax.all_to_all(
        sent.reshape(leafs * head_parts, CAP * part_rows, LATENT),
        ("leaf", "head"), split_axis=0, concat_axis=0, tiled=True,
    ).reshape(leafs * CAP * BLK, LATENT)
    theirs = []
    for hop, part in enumerate(others, 1):
        route = [(i, (i + hop) % head_parts) for i in range(head_parts)]
        theirs.append(lax.ppermute(part, "head", route))

    d_queries = query_gradients(keys_e, keys_o, ds, queries)
    d_branch, d_trunk = finish(ancestors, got, mine, theirs, owned, part_rows)
    return d_queries, d_branch, d_trunk


def solution(mesh):
    return jax.shard_map(
        local,
        mesh=mesh,
        in_specs=(
            P("leaf", "head"),
            P("leaf", "head"),
            P("leaf", None),
            P("leaf", None, None),
            P(),
            P(),
        ),
        out_specs=(P("leaf", "head"), P(("leaf", "head"), None), P("leaf", "head", None)),
        check_vma=False,
    )
```

```python
import functools
import math

import jax
import jax.numpy as jnp
from jax import lax
from jax.experimental import pallas as pl
from jax.experimental.pallas import tpu as pltpu
from jax.sharding import PartitionSpec as P

RANK = 512
QK_HEAD = 192
LATENT = 576
BLK = 8
CAP = 2
ANC = 32
LEAST_LIVE = 24
LANES = 128
WIDTH = 640
HALF = WIDTH - LATENT
PAIRS = 4
MASKED = -1e30
FAR_OFF = 1 << 20
SCALE = float(QK_HEAD) ** -0.5
EXP_SCALE = SCALE * math.log2(math.e)
MIB = 1024 * 1024
NT = (((1,), (1,)), ((), ()))
NN = (((1,), (0,)), ((), ()))
TN = (((0,), (0,)), ((), ()))


def mm(a, b, dims):
    return lax.dot_general(a, b, dims, preferred_element_type=jnp.float32)


def pieces(total, size):
    return [(at, min(size, total - at)) for at in range(0, total, size)]


def div(x, n):
    return x >> (n.bit_length() - 1) if n & (n - 1) == 0 else lax.div(x, jnp.full_like(x, n))


def mod(x, n):
    return x - div(x, n) * n


def column(rows):
    return lax.broadcasted_iota(jnp.int32, (rows, 1), 0)


def one_hot(place, size):
    lane = lax.broadcasted_iota(jnp.int32, (place.shape[0], size), 1)
    return jnp.where(lane == place, 1.0, 0.0).astype(jnp.bfloat16)


def token_part(tok):
    return 64 if tok % 64 == 0 else tok


def listed_blocks(ancestors, owned, second):
    leafs = ancestors.shape[0]
    rows = leafs * CAP * BLK
    named = ancestors[...].astype(jnp.float32)
    named = jnp.broadcast_to(named[:, None, :], (leafs, CAP * BLK, ANC)).reshape(rows, ANC)
    first = lax.axis_index("leaf") * owned
    low_end = first.astype(jnp.float32)
    mine = (named >= low_end) & (named < low_end + owned)
    low = jnp.min(jnp.where(mine, named, float(FAR_OFF)), axis=1, keepdims=True)
    high = jnp.max(jnp.where(mine, named, -1.0), axis=1, keepdims=True)
    return jnp.where(second, high, low).astype(jnp.int32) - first


def pick_kernel(ancestors, trunk, out):
    owned = trunk.shape[0] // BLK
    row = column(out.shape[0])
    block = listed_blocks(ancestors, owned, mod(div(row, BLK), CAP) == 1)
    sel = one_hot(block * BLK + mod(row, BLK), trunk.shape[0])
    out[...] = mm(sel, trunk[...], NN).astype(out.dtype)


def pick(ancestors, trunk):
    rows = ancestors.shape[0] * CAP * BLK
    return pl.pallas_call(
        pick_kernel,
        out_shape=jax.ShapeDtypeStruct((rows, LATENT), trunk.dtype),
        name="pick_blocks",
    )(ancestors, trunk)


def finish_kernel(ancestors, got, mine, *rest):
    theirs, (d_branch, d_trunk) = rest[:-2], rest[-2:]
    owned, part_rows = d_trunk.shape[0], d_trunk.shape[1]
    row = column(got.shape[0])
    block = listed_blocks(ancestors, owned, mod(div(row, part_rows), CAP) == 1)
    sel = one_hot(block * part_rows + mod(row, part_rows), owned * part_rows)
    total = mm(sel, got[...], TN)
    for b in range(owned):
        d_trunk[b] = total[b * part_rows:(b + 1) * part_rows]
    own = mine[...]
    for other in theirs:
        own = own + other[...]
    d_branch[...] = own


def finish(ancestors, got, mine, theirs, owned, part_rows):
    return pl.pallas_call(
        finish_kernel,
        out_shape=[
            jax.ShapeDtypeStruct(mine.shape, jnp.float32),
            jax.ShapeDtypeStruct((owned, part_rows, LATENT), jnp.float32),
        ],
        compiler_params=pltpu.CompilerParams(vmem_limit_bytes=8 * MIB),
        name="sum_gradients",
    )(ancestors, got, mine, *theirs)


def slot_places(ancestors, owned):
    row = column(ANC * BLK)
    mine = ancestors[pl.ds(lax.axis_index("leaf"), 1), :].astype(jnp.float32)
    mine = jnp.broadcast_to(mine, (ANC * BLK, ANC))
    lane = lax.broadcasted_iota(jnp.int32, (ANC * BLK, ANC), 1)
    block = jnp.max(jnp.where(lane == div(row, BLK), mine, -1.0), axis=1, keepdims=True)
    owner = div(block.astype(jnp.int32), owned)
    low_end = (owner * owned).astype(jnp.float32)
    below = (mine >= low_end) & (mine < block)
    second = jnp.max(jnp.where(below, 1.0, 0.0), axis=1, keepdims=True).astype(jnp.int32)
    return row, owner, second


def attn_kernel(
    owned, head_parts, anc_count, ancestors, incoming, own, q, do, ds, keys_e, keys_o, sent, *rest
):
    own_parts = rest[:head_parts]
    far_bias, causal, q_st, s, dp, p_low, tops, acc_k, acc_v = rest[head_parts:]
    tok = q.shape[0]
    far_rows, rows = ANC * BLK, ANC * BLK + tok
    sub = token_part(tok)
    parts = tok // sub
    stack = 2 * PAIRS * sub
    least = LEAST_LIVE * BLK
    step = pl.program_id(0)

    @pl.when(step == 0)
    def _():
        row, owner, second = slot_places(ancestors, owned)
        sel = one_hot((owner * CAP + second) * BLK + mod(row, BLK), incoming.shape[0])
        far = mm(sel, incoming[...], NN)
        joined = jnp.concatenate([far, own[...].astype(jnp.float32)], axis=0)
        padded = jnp.concatenate([joined, jnp.zeros((rows, HALF), jnp.float32)], axis=1)
        keys_e[...] = padded.astype(jnp.bfloat16)
        keys_o[...] = pltpu.roll(padded, HALF, axis=1).astype(jnp.bfloat16)
        live = anc_count[lax.axis_index("leaf")]
        slot = div(lax.broadcasted_iota(jnp.int32, far_bias.shape, 0) + least, BLK)
        far_bias[...] = jnp.where(slot < live, 0.0, MASKED)
        key_at = lax.broadcasted_iota(jnp.int32, causal.shape, 0)
        tok_at = mod(lax.broadcasted_iota(jnp.int32, causal.shape, 1), sub)
        causal[...] = jnp.where(key_at <= tok_at, 0.0, MASKED)
        acc_k[...] = jnp.zeros_like(acc_k)
        acc_v[...] = jnp.zeros_like(acc_v)

    def seen(j):
        return far_rows + (j + 1) * sub

    def lanes(j):
        return pl.ds(j * stack, stack)

    def fill(j):
        toks = pl.ds(j * sub, sub)
        for i in range(PAIRS):
            at = i * 2 * LATENT
            q_st[pl.ds(j * stack + i * sub, sub), :] = q[toks, at:at + WIDTH]
            odd = q[toks, at + LATENT - HALF:at + 2 * LATENT]
            odd = pltpu.roll(odd, WIDTH - HALF, axis=1)
            q_st[pl.ds(j * stack + (PAIRS + i) * sub, sub), :] = odd

    heads = list(range(0, 2 * PAIRS, 2)) + list(range(1, 2 * PAIRS, 2))

    def grads(j, first, count, at=0, size=RANK):
        toks = pl.ds(j * sub, sub)
        cols = [pl.ds(h * RANK + at, size) for h in heads[first:first + count]]
        return jnp.concatenate([do[toks, c] for c in cols], axis=0)

    def fold(x):
        return x.reshape(-1, 8, x.shape[1])

    def score(j, at):
        n, cols = seen(j), pl.ds(j * stack + at, stack // 2)
        out = mm(keys_e[:n, :], q_st[cols, :], NT)
        near = [(0, out[:least]), (least, out[least:far_rows] + far_bias[...])]
        if j > 0:
            near.append((far_rows, out[far_rows:n - sub]))
        near.append((n - sub, out[n - sub:] + causal[...]))
        top = None
        for r, part in near:
            s[pl.ds(r, part.shape[0]), cols] = part
            part = jnp.max(fold(part), axis=0)
            top = part if top is None else jnp.maximum(top, part)
        tops[:, cols] = top

    def prob(j, at):
        n, cols = seen(j), pl.ds(j * stack + at, stack // 2)
        dp[:n, cols] = mm(keys_e[:n, :RANK], grads(j, at // sub, PAIRS), NT)

    state = {}

    def soft_sums(j, at):
        lane = pl.ds(j * stack + at, LANES)
        top = jnp.max(tops[:, lane], axis=0, keepdims=True)
        total = jnp.zeros((8, LANES), jnp.float32)
        delta = jnp.zeros((8, LANES), jnp.float32)
        for r, n in pieces(seen(j), 64):
            e = jnp.exp2((s[pl.ds(r, n), lane] - top) * EXP_SCALE)
            s[pl.ds(r, n), lane] = e
            total += jnp.sum(fold(e), axis=0)
            delta += jnp.sum(fold(e * dp[pl.ds(r, n), lane]), axis=0)
        inv = 1.0 / jnp.sum(total, axis=0, keepdims=True)
        state[j, at] = inv, jnp.sum(delta, axis=0, keepdims=True) * inv

    def soft_outs(j, at):
        lane = pl.ds(j * stack + at, LANES)
        inv, delta = state.pop((j, at))
        for r, n in pieces(seen(j), 64):
            p = s[pl.ds(r, n), lane] * inv
            p_low[pl.ds(r, n), lane] = p.astype(jnp.bfloat16)
            ds[0, pl.ds(r, n), lane] = (p * (dp[pl.ds(r, n), lane] - delta)).astype(ds.dtype)

    def grad_values(j, at, size):
        n, cols = seen(j), pl.ds(at, size)
        acc_v[:n, cols] += mm(p_low[:n, lanes(j)], grads(j, 0, 2 * PAIRS, at, size), NN)

    def grad_keys(j, at, size):
        n, cols = seen(j), pl.ds(at, size)
        acc_k[:n, cols] += mm(ds[0, :n, lanes(j)], q_st[lanes(j), cols], NN)

    def jobs_of(i):
        products, passes = [], []
        if i < parts:
            products += [functools.partial(fill, i)]
            for at in (0, stack // 2):
                products += [functools.partial(score, i, at), functools.partial(prob, i, at)]
        if 0 <= i - 2 < parts:
            products += [functools.partial(grad_values, i - 2, *c) for c in pieces(RANK, 256)]
            products += [functools.partial(grad_keys, i - 2, *c) for c in pieces(WIDTH, 256)]
        if 0 <= i - 1 < parts:
            for at in range(0, stack, LANES):
                passes += [functools.partial(job, i - 1, at) for job in (soft_sums, soft_outs)]
        order = [
            (k / len(group), g, job)
            for g, group in enumerate((products, passes)) for k, job in enumerate(group)
        ]
        return [job for _, _, job in sorted(order, key=lambda item: item[:2])]

    for i in range(parts + 2):
        for job in jobs_of(i):
            job()

    @pl.when(step == pl.num_programs(0) - 1)
    def _():
        acc_k[...] = acc_k[...] * SCALE
        acc_k[:, :RANK] += acc_v[...]
        part_rows = BLK // head_parts
        row, owner, second = slot_places(ancestors, owned)
        inner = mod(row, BLK)
        place = (owner * head_parts + div(inner, part_rows)) * CAP + second
        place = place * part_rows + mod(inner, part_rows)
        sel = one_hot(place, sent.shape[0])
        far = acc_k[:far_rows, :LATENT].astype(jnp.bfloat16)
        sent[...] = mm(sel, far, TN).astype(sent.dtype)
        own_rows = tok // head_parts
        for hop, out in enumerate(own_parts):
            part = lax.rem(lax.axis_index("head") + hop, head_parts)
            at = pl.multiple_of(far_rows + part * own_rows, 8)
            out[...] = acc_k[pl.ds(at, own_rows), :LATENT]


def attention(owned, head_parts, anc_count, ancestors, incoming, own, queries, d_out):
    tok = queries.shape[0]
    heads = queries.shape[1] // LATENT
    steps = heads // (2 * PAIRS)
    far_rows, rows = ANC * BLK, ANC * BLK + tok
    toks = 2 * PAIRS * tok
    stack = 2 * PAIRS * token_part(tok)
    bf16, f32 = jnp.bfloat16, jnp.float32

    def whole(i):
        return (0, 0)

    def along(i):
        return (0, i)

    own_part = (tok // head_parts, LATENT)
    return pl.pallas_call(
        functools.partial(attn_kernel, owned, head_parts),
        grid=(steps,),
        in_specs=[
            pl.BlockSpec(memory_space=pltpu.SMEM),
            pl.BlockSpec(ancestors.shape, whole),
            pl.BlockSpec(incoming.shape, whole),
            pl.BlockSpec(own.shape, whole),
            pl.BlockSpec((tok, 2 * PAIRS * LATENT), along),
            pl.BlockSpec((tok, 2 * PAIRS * RANK), along),
        ],
        out_specs=[
            pl.BlockSpec((1, rows, toks), lambda i: (i, 0, 0)),
            pl.BlockSpec((rows, WIDTH), whole),
            pl.BlockSpec((rows, WIDTH), whole),
            pl.BlockSpec(incoming.shape, whole),
        ] + [pl.BlockSpec(own_part, whole)] * head_parts,
        out_shape=[
            jax.ShapeDtypeStruct((steps, rows, toks), bf16),
            jax.ShapeDtypeStruct((rows, WIDTH), bf16),
            jax.ShapeDtypeStruct((rows, WIDTH), bf16),
            jax.ShapeDtypeStruct(incoming.shape, bf16),
        ] + [jax.ShapeDtypeStruct(own_part, f32)] * head_parts,
        scratch_shapes=[
            pltpu.VMEM((far_rows - LEAST_LIVE * BLK, stack // 2), f32),
            pltpu.VMEM((token_part(tok), stack // 2), f32),
            pltpu.VMEM((toks, WIDTH), bf16),
            pltpu.VMEM((rows, toks), f32),
            pltpu.VMEM((rows, toks), f32),
            pltpu.VMEM((rows, toks), bf16),
            pltpu.VMEM((8, toks), f32),
            pltpu.VMEM((rows, WIDTH), f32),
            pltpu.VMEM((rows, RANK), f32),
        ],
        compiler_params=pltpu.CompilerParams(vmem_limit_bytes=36 * MIB),
        cost_estimate=pl.CostEstimate(
            flops=2 * tok * heads * rows * (2 * LATENT + 2 * RANK),
            bytes_accessed=2 * tok * heads * (LATENT + RANK + rows),
            transcendentals=tok * heads * rows,
        ),
        name="score_gradients",
    )(anc_count, ancestors, incoming, own, queries, d_out)


def query_kernel(keys_e, keys_o, ds, dq):
    tok = dq.shape[0]
    rows = ds.shape[1]
    sub = token_part(tok)
    parts = tok // sub
    stack = PAIRS * sub
    low = LATENT - HALF
    for j in range(parts):
        n = rows - tok + (j + 1) * sub
        even = mm(ds[0, :n, pl.ds(2 * j * stack, stack)], keys_e[:n, :], TN) * SCALE
        odd = mm(ds[0, :n, pl.ds((2 * j + 1) * stack, stack)], keys_o[:n, :], TN) * SCALE
        for i in range(PAIRS):
            at = i * 2 * LATENT
            part = slice(i * sub, (i + 1) * sub)
            toks = pl.ds(j * sub, sub)
            dq[toks, at:at + low] = even[part, :low].astype(dq.dtype)
            joint = even[part, low:] + odd[part, :2 * HALF]
            dq[toks, at + low:at + low + 2 * HALF] = joint.astype(dq.dtype)
            dq[toks, at + low + 2 * HALF:at + 2 * LATENT] = odd[part, 2 * HALF:].astype(dq.dtype)


def query_gradients(keys_e, keys_o, ds, queries):
    tok = queries.shape[0]
    heads = queries.shape[1] // LATENT
    steps, rows = ds.shape[0], ds.shape[1]
    return pl.pallas_call(
        query_kernel,
        grid=(steps,),
        in_specs=[
            pl.BlockSpec(keys_e.shape, lambda i: (0, 0)),
            pl.BlockSpec(keys_o.shape, lambda i: (0, 0)),
            pl.BlockSpec((1,) + ds.shape[1:], lambda i: (i, 0, 0)),
        ],
        out_specs=pl.BlockSpec((tok, 2 * PAIRS * LATENT), lambda i: (0, i)),
        out_shape=jax.ShapeDtypeStruct(queries.shape, queries.dtype),
        compiler_params=pltpu.CompilerParams(vmem_limit_bytes=16 * MIB),
        cost_estimate=pl.CostEstimate(
            flops=2 * tok * heads * rows * LATENT,
            bytes_accessed=2 * tok * heads * (LATENT + rows),
            transcendentals=0,
        ),
        name="query_gradients",
    )(keys_e, keys_o, ds)


def local(queries, d_out, branch_latent, trunk_latent, ancestors, anc_count):
    leafs = lax.axis_size("leaf")
    head_parts = lax.axis_size("head")
    owned = trunk_latent.shape[0]
    part_rows = BLK // head_parts

    outgoing = pick(ancestors, trunk_latent.reshape(owned * BLK, LATENT))
    incoming = lax.all_to_all(
        outgoing.reshape(leafs, CAP * BLK, LATENT), "leaf", split_axis=0, concat_axis=0, tiled=True
    ).reshape(leafs * CAP * BLK, LATENT)

    ds, keys_e, keys_o, sent, mine, *others = attention(
        owned, head_parts, anc_count, ancestors, incoming, branch_latent, queries, d_out
    )

    got = lax.all_to_all(
        sent.reshape(leafs * head_parts, CAP * part_rows, LATENT),
        ("leaf", "head"), split_axis=0, concat_axis=0, tiled=True,
    ).reshape(leafs * CAP * BLK, LATENT)
    theirs = []
    for hop, part in enumerate(others, 1):
        route = [(i, (i + hop) % head_parts) for i in range(head_parts)]
        theirs.append(lax.ppermute(part, "head", route))

    d_queries = query_gradients(keys_e, keys_o, ds, queries)
    d_branch, d_trunk = finish(ancestors, got, mine, theirs, owned, part_rows)
    return d_queries, d_branch, d_trunk


def solution(mesh):
    return jax.shard_map(
        local,
        mesh=mesh,
        in_specs=(
            P("leaf", "head"),
            P("leaf", "head"),
            P("leaf", None),
            P("leaf", None, None),
            P(),
            P(),
        ),
        out_specs=(P("leaf", "head"), P(("leaf", "head"), None), P("leaf", "head", None)),
        check_vma=False,
    )
```

```python
import functools
import math

import jax
import jax.numpy as jnp
from jax import lax
from jax.experimental import pallas as pl
from jax.experimental.pallas import tpu as pltpu
from jax.sharding import PartitionSpec as P

RANK = 512
QK_HEAD = 192
LATENT = 576
BLK = 8
CAP = 2
ANC = 32
LANES = 128
WIDTH = 640
HALF = WIDTH - LATENT
PAIRS = 4
MASKED = -1e30
FAR_OFF = 1 << 20
SCALE = float(QK_HEAD) ** -0.5
EXP_SCALE = SCALE * math.log2(math.e)
MIB = 1024 * 1024
NT = (((1,), (1,)), ((), ()))
NN = (((1,), (0,)), ((), ()))
TN = (((0,), (0,)), ((), ()))


def mm(a, b, dims):
    return lax.dot_general(a, b, dims, preferred_element_type=jnp.float32)


def pieces(total, size):
    return [(at, min(size, total - at)) for at in range(0, total, size)]


def div(x, n):
    return x >> (n.bit_length() - 1) if n & (n - 1) == 0 else lax.div(x, jnp.full_like(x, n))


def mod(x, n):
    return x - div(x, n) * n


def column(rows):
    return lax.broadcasted_iota(jnp.int32, (rows, 1), 0)


def one_hot(place, size):
    lane = lax.broadcasted_iota(jnp.int32, (place.shape[0], size), 1)
    return jnp.where(lane == place, 1.0, 0.0).astype(jnp.bfloat16)


def token_part(tok):
    return 64 if tok % 64 == 0 else tok


def listed_blocks(ancestors, owned, second):
    leafs = ancestors.shape[0]
    rows = leafs * CAP * BLK
    named = ancestors[...].astype(jnp.float32)
    named = jnp.broadcast_to(named[:, None, :], (leafs, CAP * BLK, ANC)).reshape(rows, ANC)
    first = lax.axis_index("leaf") * owned
    low_end = first.astype(jnp.float32)
    mine = (named >= low_end) & (named < low_end + owned)
    low = jnp.min(jnp.where(mine, named, float(FAR_OFF)), axis=1, keepdims=True)
    high = jnp.max(jnp.where(mine, named, -1.0), axis=1, keepdims=True)
    return jnp.where(second, high, low).astype(jnp.int32) - first


def pick_kernel(ancestors, trunk, out):
    owned = trunk.shape[0] // BLK
    row = column(out.shape[0])
    block = listed_blocks(ancestors, owned, mod(div(row, BLK), CAP) == 1)
    sel = one_hot(block * BLK + mod(row, BLK), trunk.shape[0])
    out[...] = mm(sel, trunk[...], NN).astype(out.dtype)


def pick(ancestors, trunk):
    rows = ancestors.shape[0] * CAP * BLK
    return pl.pallas_call(
        pick_kernel,
        out_shape=jax.ShapeDtypeStruct((rows, LATENT), trunk.dtype),
        name="pick_blocks",
    )(ancestors, trunk)


def finish_kernel(ancestors, got, mine, *rest):
    theirs, (d_branch, d_trunk) = rest[:-2], rest[-2:]
    owned, part_rows = d_trunk.shape[0], d_trunk.shape[1]
    row = column(got.shape[0])
    block = listed_blocks(ancestors, owned, mod(div(row, part_rows), CAP) == 1)
    sel = one_hot(block * part_rows + mod(row, part_rows), owned * part_rows)
    total = mm(sel, got[...], TN)
    for b in range(owned):
        d_trunk[b] = total[b * part_rows:(b + 1) * part_rows]
    own = mine[...]
    for other in theirs:
        own = own + other[...]
    d_branch[...] = own


def finish(ancestors, got, mine, theirs, owned, part_rows):
    return pl.pallas_call(
        finish_kernel,
        out_shape=[
            jax.ShapeDtypeStruct(mine.shape, jnp.float32),
            jax.ShapeDtypeStruct((owned, part_rows, LATENT), jnp.float32),
        ],
        compiler_params=pltpu.CompilerParams(vmem_limit_bytes=8 * MIB),
        name="sum_gradients",
    )(ancestors, got, mine, *theirs)


def slot_places(ancestors, owned):
    row = column(ANC * BLK)
    mine = ancestors[pl.ds(lax.axis_index("leaf"), 1), :].astype(jnp.float32)
    mine = jnp.broadcast_to(mine, (ANC * BLK, ANC))
    lane = lax.broadcasted_iota(jnp.int32, (ANC * BLK, ANC), 1)
    block = jnp.max(jnp.where(lane == div(row, BLK), mine, -1.0), axis=1, keepdims=True)
    owner = div(block.astype(jnp.int32), owned)
    low_end = (owner * owned).astype(jnp.float32)
    below = (mine >= low_end) & (mine < block)
    second = jnp.max(jnp.where(below, 1.0, 0.0), axis=1, keepdims=True).astype(jnp.int32)
    return row, owner, second


def attn_kernel(
    owned, head_parts, ahead, anc_count, ancestors, incoming, own, q, do, dq, ds, keys_e, keys_o, sent,
    *rest
):
    own_parts = rest[:head_parts]
    scratch = rest[head_parts:]
    bias, cols_e, cols_o, s_e, s_o, dp_e, dp_o, p_e, p_o, d_e, d_o, acc_e, acc_o, acc_v = scratch
    tok = q.shape[0]
    far_rows, rows = ANC * BLK, ANC * BLK + tok
    lanes = keys_e.shape[0]
    sub = token_part(tok)
    parts = tok // sub
    step = pl.program_id(0)

    @pl.when(step == 0)
    def _():
        row, owner, second = slot_places(ancestors, owned)
        sel = one_hot((owner * CAP + second) * BLK + mod(row, BLK), incoming.shape[0])
        far = mm(sel, incoming[...], NN)
        joined = jnp.concatenate([far, own[...].astype(jnp.float32)], axis=0)
        padded = jnp.concatenate([joined, jnp.zeros((rows, HALF), jnp.float32)], axis=1)
        if lanes > rows:
            padded = jnp.concatenate([padded, jnp.zeros((lanes - rows, WIDTH), jnp.float32)], axis=0)
        keys_e[...] = padded.astype(jnp.bfloat16)
        cols_e[...] = padded.T.astype(jnp.bfloat16)
        moved = pltpu.roll(padded, HALF, axis=1)
        keys_o[...] = moved.astype(jnp.bfloat16)
        cols_o[...] = moved.T.astype(jnp.bfloat16)
        live = anc_count[lax.axis_index("leaf")]
        key_at = lax.broadcasted_iota(jnp.int32, bias.shape, 1)
        tok_at = lax.broadcasted_iota(jnp.int32, bias.shape, 0)
        far_ok = (key_at < far_rows) & (key_at < live * BLK)
        own_ok = (key_at >= far_rows) & (key_at - far_rows <= tok_at)
        bias[...] = jnp.where(far_ok | own_ok, 0.0, MASKED)
        acc_e[...] = jnp.zeros_like(acc_e)
        acc_o[...] = jnp.zeros_like(acc_o)
        acc_v[...] = jnp.zeros_like(acc_v)

    keys, cols = (keys_e, keys_o), (cols_e, cols_o)
    s_st, dp_st, p_st, d_st, accs = (s_e, s_o), (dp_e, dp_o), (p_e, p_o), (d_e, d_o), (acc_e, acc_o)

    def seen(j):
        return far_rows + (j + 1) * sub

    def seen_lanes(j):
        return -(-seen(j) // LANES) * LANES

    def head_queries(par, pair, toks):
        return q[toks, pl.ds(pair * 2 * LATENT + par * (LATENT - HALF), WIDTH)]

    def head_grads(par, pair, toks):
        return do[toks, pl.ds((2 * pair + par) * RANK, RANK)]

    def stacked(of, par, toks):
        return jnp.concatenate([of(par, pair, toks) for pair in range(PAIRS)], axis=0)

    every = slice(0, tok)

    def put(to, out, at, plus=None):
        size = out.shape[1]
        for pair in range(PAIRS):
            for j in range(parts):
                n = min(size, seen_lanes(j) - at)
                if n > 0:
                    r = pair * tok + j * sub
                    kept = out[r:r + sub, :n]
                    if plus is not None:
                        kept = kept + plus[j * sub:(j + 1) * sub, at:at + n]
                    to[r:r + sub, at:at + n] = kept

    def score(par, at, size):
        out = mm(stacked(head_queries, par, every), cols[par][:, at:at + size], NN)
        put(s_st[par], out, at, bias)

    def prob(par, at, size):
        out = mm(stacked(head_grads, par, every), cols_e[:RANK, at:at + size], NN)
        put(dp_st[par], out, at)

    def soft(par, pair, j, half):
        n, size = seen_lanes(j), sub // 2
        block = pl.ds(pair * tok + j * sub + half * size, size)
        s, dp = s_st[par][block, :n], dp_st[par][block, :n]
        top = jnp.max(s, axis=1, keepdims=True)
        e = jnp.exp2((s - top) * EXP_SCALE)
        inv = 1.0 / jnp.sum(e, axis=1, keepdims=True)
        delta = jnp.sum(e * dp, axis=1, keepdims=True) * inv
        p = e * inv
        p_st[par][block, :n] = p.astype(jnp.bfloat16)
        d_st[par][block, :n] = (p * (dp - delta)).astype(jnp.bfloat16)
        if n < lanes:
            d_st[par][block, n:] = jnp.zeros((size, lanes - n), jnp.bfloat16)

    def turned(ref, j):
        blocks = [ref[pl.ds(pair * tok + j * sub, sub), :seen_lanes(j)] for pair in range(PAIRS)]
        return jnp.concatenate(blocks, axis=0).T[:seen(j)]

    def grad_values(par, j):
        toks = pl.ds(j * sub, sub)
        acc_v[:seen(j), :] += mm(turned(p_st[par], j), stacked(head_grads, par, toks), NN)

    def grad_keys(par, j):
        toks = pl.ds(j * sub, sub)
        accs[par][:seen(j), :] += mm(turned(d_st[par], j), stacked(head_queries, par, toks), NN)

    def scores(par):
        jobs = []
        for piece in pieces(lanes, 256):
            jobs += [functools.partial(score, par, *piece), functools.partial(prob, par, *piece)]
        return jobs

    def softs(par):
        blocks = [(pair, j, half) for pair in range(PAIRS) for j in range(parts) for half in range(2)]
        return [functools.partial(soft, par, *block) for block in blocks]

    def grads(par):
        jobs = []
        for j in range(parts):
            jobs += [functools.partial(grad_values, par, j), functools.partial(grad_keys, par, j)]
        return jobs

    def together(*groups):
        order = [
            (k / len(group), g, job) for g, group in enumerate(groups) for k, job in enumerate(group)
        ]
        for _, _, job in sorted(order, key=lambda item: item[:2]):
            job()

    together(scores(0))
    together(scores(1), softs(0))
    together(grads(0), softs(1))
    together(grads(1))

    @pl.when(step < ahead)
    def _():
        put_queries(dq, d_e[...], d_o[...], keys_e[...], keys_o[...])

    @pl.when(step >= ahead)
    def _():
        ds[0, 0] = d_e[...]
        ds[0, 1] = d_o[...]

    @pl.when(step == pl.num_programs(0) - 1)
    def _():
        shifted = pltpu.roll(acc_o[...], WIDTH - HALF, axis=1)
        acc_e[...] = (acc_e[...] + shifted) * SCALE
        acc_e[:, :RANK] += acc_v[...]
        part_rows = BLK // head_parts
        row, owner, second = slot_places(ancestors, owned)
        inner = mod(row, BLK)
        place = (owner * head_parts + div(inner, part_rows)) * CAP + second
        place = place * part_rows + mod(inner, part_rows)
        sel = one_hot(place, sent.shape[0])
        far = acc_e[:far_rows, :LATENT].astype(jnp.bfloat16)
        sent[...] = mm(sel, far, TN).astype(sent.dtype)
        own_rows = tok // head_parts
        for hop, out in enumerate(own_parts):
            part = lax.rem(lax.axis_index("head") + hop, head_parts)
            at = pl.multiple_of(far_rows + part * own_rows, 8)
            out[...] = acc_e[pl.ds(at, own_rows), :LATENT]


def put_queries(dq, even, odd, keys_e, keys_o):
    tok = dq.shape[0]
    low = LATENT - HALF
    even = mm(even, keys_e, NN) * SCALE
    odd = mm(odd, keys_o, NN) * SCALE
    for pair in range(PAIRS):
        at, part = pair * 2 * LATENT, slice(pair * tok, (pair + 1) * tok)
        dq[:, at:at + low] = even[part, :low].astype(dq.dtype)
        joint = even[part, low:] + odd[part, :2 * HALF]
        dq[:, at + low:at + low + 2 * HALF] = joint.astype(dq.dtype)
        dq[:, at + low + 2 * HALF:at + 2 * LATENT] = odd[part, 2 * HALF:].astype(dq.dtype)


def steps_ahead(steps):
    return steps * 3 // 8


def attention(owned, head_parts, anc_count, ancestors, incoming, own, queries, d_out):
    tok = queries.shape[0]
    heads = queries.shape[1] // LATENT
    steps = heads // (2 * PAIRS)
    ahead = steps_ahead(steps)
    far_rows, rows = ANC * BLK, ANC * BLK + tok
    lanes = -(-rows // LANES) * LANES
    toks = PAIRS * tok
    bf16, f32 = jnp.bfloat16, jnp.float32

    def whole(i):
        return (0, 0)

    def along(i):
        return (0, i)

    own_part = (tok // head_parts, LATENT)
    pair_of = lambda shape, dtype: [pltpu.VMEM(shape, dtype)] * 2
    return pl.pallas_call(
        functools.partial(attn_kernel, owned, head_parts, ahead),
        grid=(steps,),
        in_specs=[
            pl.BlockSpec(memory_space=pltpu.SMEM),
            pl.BlockSpec(ancestors.shape, whole),
            pl.BlockSpec(incoming.shape, whole),
            pl.BlockSpec(own.shape, whole),
            pl.BlockSpec((tok, 2 * PAIRS * LATENT), along),
            pl.BlockSpec((tok, 2 * PAIRS * RANK), along),
        ],
        out_specs=[
            pl.BlockSpec(
                (tok, 2 * PAIRS * LATENT), lambda i: (0, jnp.minimum(i, max(ahead - 1, 0)))
            ),
            pl.BlockSpec((1, 2, toks, lanes), lambda i: (jnp.maximum(i - ahead, 0), 0, 0, 0)),
            pl.BlockSpec((lanes, WIDTH), whole),
            pl.BlockSpec((lanes, WIDTH), whole),
            pl.BlockSpec(incoming.shape, whole),
        ] + [pl.BlockSpec(own_part, whole)] * head_parts,
        out_shape=[
            jax.ShapeDtypeStruct(queries.shape, bf16),
            jax.ShapeDtypeStruct((steps - ahead, 2, toks, lanes), bf16),
            jax.ShapeDtypeStruct((lanes, WIDTH), bf16),
            jax.ShapeDtypeStruct((lanes, WIDTH), bf16),
            jax.ShapeDtypeStruct(incoming.shape, bf16),
        ] + [jax.ShapeDtypeStruct(own_part, f32)] * head_parts,
        scratch_shapes=[pltpu.VMEM((tok, lanes), f32)]
        + pair_of((WIDTH, lanes), bf16)
        + pair_of((toks, lanes), f32)
        + pair_of((toks, lanes), f32)
        + pair_of((toks, lanes), bf16)
        + pair_of((toks, lanes), bf16)
        + pair_of((rows, WIDTH), f32)
        + [pltpu.VMEM((rows, RANK), f32)],
        compiler_params=pltpu.CompilerParams(vmem_limit_bytes=60 * MIB),
        cost_estimate=pl.CostEstimate(
            flops=2 * tok * heads * rows * (2 * LATENT + 2 * RANK),
            bytes_accessed=2 * tok * heads * (LATENT + RANK + rows),
            transcendentals=tok * heads * rows,
        ),
        name="score_gradients",
    )(anc_count, ancestors, incoming, own, queries, d_out)


def query_kernel(keys_e, keys_o, ds, started, dq):
    put_queries(dq, ds[0, 0], ds[0, 1], keys_e[...], keys_o[...])


def query_gradients(keys_e, keys_o, ds, started):
    tok = started.shape[0]
    steps = ds.shape[0]
    ahead = started.shape[1] // (2 * PAIRS * LATENT) - steps
    rows = ds.shape[3]
    return pl.pallas_call(
        query_kernel,
        grid=(steps,),
        in_specs=[
            pl.BlockSpec(keys_e.shape, lambda i: (0, 0)),
            pl.BlockSpec(keys_o.shape, lambda i: (0, 0)),
            pl.BlockSpec((1,) + ds.shape[1:], lambda i: (i, 0, 0, 0)),
            pl.BlockSpec(memory_space=pl.ANY),
        ],
        out_specs=pl.BlockSpec((tok, 2 * PAIRS * LATENT), lambda i: (0, i + ahead)),
        out_shape=jax.ShapeDtypeStruct(started.shape, started.dtype),
        input_output_aliases={3: 0},
        compiler_params=pltpu.CompilerParams(vmem_limit_bytes=60 * MIB),
        cost_estimate=pl.CostEstimate(
            flops=4 * tok * steps * PAIRS * rows * LATENT,
            bytes_accessed=4 * tok * steps * PAIRS * (LATENT + rows),
            transcendentals=0,
        ),
        name="query_gradients",
    )(keys_e, keys_o, ds, started)


def local(queries, d_out, branch_latent, trunk_latent, ancestors, anc_count):
    leafs = lax.axis_size("leaf")
    head_parts = lax.axis_size("head")
    owned = trunk_latent.shape[0]
    part_rows = BLK // head_parts

    outgoing = pick(ancestors, trunk_latent.reshape(owned * BLK, LATENT))
    incoming = lax.all_to_all(
        outgoing.reshape(leafs, CAP * BLK, LATENT), "leaf", split_axis=0, concat_axis=0, tiled=True
    ).reshape(leafs * CAP * BLK, LATENT)

    started, ds, keys_e, keys_o, sent, mine, *others = attention(
        owned, head_parts, anc_count, ancestors, incoming, branch_latent, queries, d_out
    )

    got = lax.all_to_all(
        sent.reshape(leafs * head_parts, CAP * part_rows, LATENT),
        ("leaf", "head"), split_axis=0, concat_axis=0, tiled=True,
    ).reshape(leafs * CAP * BLK, LATENT)
    theirs = []
    for hop, part in enumerate(others, 1):
        route = [(i, (i + hop) % head_parts) for i in range(head_parts)]
        theirs.append(lax.ppermute(part, "head", route))

    d_queries = query_gradients(keys_e, keys_o, ds, started)
    d_branch, d_trunk = finish(ancestors, got, mine, theirs, owned, part_rows)
    return d_queries, d_branch, d_trunk


def solution(mesh):
    return jax.shard_map(
        local,
        mesh=mesh,
        in_specs=(
            P("leaf", "head"),
            P("leaf", "head"),
            P("leaf", None),
            P("leaf", None, None),
            P(),
            P(),
        ),
        out_specs=(P("leaf", "head"), P(("leaf", "head"), None), P("leaf", "head", None)),
        check_vma=False,
    )
```

```python
import functools
import math

import jax
import jax.numpy as jnp
from jax import lax
from jax.experimental import pallas as pl
from jax.experimental.pallas import tpu as pltpu
from jax.sharding import PartitionSpec as P

RANK = 512
QK_HEAD = 192
LATENT = 576
BLK = 8
CAP = 2
ANC = 32
LEAST_LIVE = 24
LANES = 128
WIDTH = 640
HALF = WIDTH - LATENT
PAIRS = 4
MASKED = -1e30
FAR_OFF = 1 << 20
SCALE = float(QK_HEAD) ** -0.5
EXP_SCALE = SCALE * math.log2(math.e)
MIB = 1024 * 1024
NT = (((1,), (1,)), ((), ()))
NN = (((1,), (0,)), ((), ()))
TN = (((0,), (0,)), ((), ()))


def mm(a, b, dims):
    return lax.dot_general(a, b, dims, preferred_element_type=jnp.float32)


def pieces(total, size):
    return [(at, min(size, total - at)) for at in range(0, total, size)]


def div(x, n):
    return x >> (n.bit_length() - 1) if n & (n - 1) == 0 else lax.div(x, jnp.full_like(x, n))


def mod(x, n):
    return x - div(x, n) * n


def column(rows):
    return lax.broadcasted_iota(jnp.int32, (rows, 1), 0)


def one_hot(place, size):
    lane = lax.broadcasted_iota(jnp.int32, (place.shape[0], size), 1)
    return jnp.where(lane == place, 1.0, 0.0).astype(jnp.bfloat16)


def token_part(tok):
    return 64 if tok % 64 == 0 else tok


def listed_blocks(ancestors, owned, second):
    leafs = ancestors.shape[0]
    rows = leafs * CAP * BLK
    named = ancestors[...].astype(jnp.float32)
    named = jnp.broadcast_to(named[:, None, :], (leafs, CAP * BLK, ANC)).reshape(rows, ANC)
    first = lax.axis_index("leaf") * owned
    low_end = first.astype(jnp.float32)
    mine = (named >= low_end) & (named < low_end + owned)
    low = jnp.min(jnp.where(mine, named, float(FAR_OFF)), axis=1, keepdims=True)
    high = jnp.max(jnp.where(mine, named, -1.0), axis=1, keepdims=True)
    return jnp.where(second, high, low).astype(jnp.int32) - first


def pick_kernel(ancestors, trunk, out):
    owned = trunk.shape[0] // BLK
    row = column(out.shape[0])
    block = listed_blocks(ancestors, owned, mod(div(row, BLK), CAP) == 1)
    sel = one_hot(block * BLK + mod(row, BLK), trunk.shape[0])
    out[...] = mm(sel, trunk[...], NN).astype(out.dtype)


def pick(ancestors, trunk):
    rows = ancestors.shape[0] * CAP * BLK
    return pl.pallas_call(
        pick_kernel,
        out_shape=jax.ShapeDtypeStruct((rows, LATENT), trunk.dtype),
        name="pick_blocks",
    )(ancestors, trunk)


def finish_kernel(ancestors, got, mine, *rest):
    theirs, (d_branch, d_trunk) = rest[:-2], rest[-2:]
    owned, part_rows = d_trunk.shape[0], d_trunk.shape[1]
    row = column(got.shape[0])
    block = listed_blocks(ancestors, owned, mod(div(row, part_rows), CAP) == 1)
    sel = one_hot(block * part_rows + mod(row, part_rows), owned * part_rows)
    total = mm(sel, got[...], TN)
    for b in range(owned):
        d_trunk[b] = total[b * part_rows:(b + 1) * part_rows]
    own = mine[...]
    for other in theirs:
        own = own + other[...]
    d_branch[...] = own


def finish(ancestors, got, mine, theirs, owned, part_rows):
    return pl.pallas_call(
        finish_kernel,
        out_shape=[
            jax.ShapeDtypeStruct(mine.shape, jnp.float32),
            jax.ShapeDtypeStruct((owned, part_rows, LATENT), jnp.float32),
        ],
        compiler_params=pltpu.CompilerParams(vmem_limit_bytes=8 * MIB),
        name="sum_gradients",
    )(ancestors, got, mine, *theirs)


def slot_places(ancestors, owned):
    row = column(ANC * BLK)
    mine = ancestors[pl.ds(lax.axis_index("leaf"), 1), :].astype(jnp.float32)
    mine = jnp.broadcast_to(mine, (ANC * BLK, ANC))
    lane = lax.broadcasted_iota(jnp.int32, (ANC * BLK, ANC), 1)
    block = jnp.max(jnp.where(lane == div(row, BLK), mine, -1.0), axis=1, keepdims=True)
    owner = div(block.astype(jnp.int32), owned)
    low_end = (owner * owned).astype(jnp.float32)
    below = (mine >= low_end) & (mine < block)
    second = jnp.max(jnp.where(below, 1.0, 0.0), axis=1, keepdims=True).astype(jnp.int32)
    return row, owner, second


def attn_kernel(
    owned, head_parts, ahead, anc_count, ancestors, incoming, own, q, do, dq, ds, keys_e, keys_o, sent,
    *rest
):
    own_parts = rest[:head_parts]
    far_bias, causal, q_st, s, dp, p_low, tops, acc_k, acc_v = rest[head_parts:]
    tok = q.shape[0]
    far_rows, rows = ANC * BLK, ANC * BLK + tok
    sub = token_part(tok)
    parts = tok // sub
    stack = 2 * PAIRS * sub
    least = LEAST_LIVE * BLK
    step = pl.program_id(0)

    @pl.when(step == 0)
    def _():
        row, owner, second = slot_places(ancestors, owned)
        sel = one_hot((owner * CAP + second) * BLK + mod(row, BLK), incoming.shape[0])
        far = mm(sel, incoming[...], NN)
        joined = jnp.concatenate([far, own[...].astype(jnp.float32)], axis=0)
        padded = jnp.concatenate([joined, jnp.zeros((rows, HALF), jnp.float32)], axis=1)
        keys_e[...] = padded.astype(jnp.bfloat16)
        keys_o[...] = pltpu.roll(padded, HALF, axis=1).astype(jnp.bfloat16)
        live = anc_count[lax.axis_index("leaf")]
        slot = div(lax.broadcasted_iota(jnp.int32, far_bias.shape, 0) + least, BLK)
        far_bias[...] = jnp.where(slot < live, 0.0, MASKED)
        key_at = lax.broadcasted_iota(jnp.int32, causal.shape, 0)
        tok_at = mod(lax.broadcasted_iota(jnp.int32, causal.shape, 1), sub)
        causal[...] = jnp.where(key_at <= tok_at, 0.0, MASKED)
        acc_k[...] = jnp.zeros_like(acc_k)
        acc_v[...] = jnp.zeros_like(acc_v)

    def seen(j):
        return far_rows + (j + 1) * sub

    def lanes(j):
        return pl.ds(j * stack, stack)

    def fill(j):
        toks = pl.ds(j * sub, sub)
        for i in range(PAIRS):
            at = i * 2 * LATENT
            q_st[pl.ds(j * stack + i * sub, sub), :] = q[toks, at:at + WIDTH]
            odd = q[toks, at + LATENT - HALF:at + 2 * LATENT]
            odd = pltpu.roll(odd, WIDTH - HALF, axis=1)
            q_st[pl.ds(j * stack + (PAIRS + i) * sub, sub), :] = odd

    heads = list(range(0, 2 * PAIRS, 2)) + list(range(1, 2 * PAIRS, 2))

    def grads(j, first, count, at=0, size=RANK):
        toks = pl.ds(j * sub, sub)
        cols = [pl.ds(h * RANK + at, size) for h in heads[first:first + count]]
        return jnp.concatenate([do[toks, c] for c in cols], axis=0)

    def fold(x):
        return x.reshape(-1, 8, x.shape[1])

    def score(j, at):
        n, cols = seen(j), pl.ds(j * stack + at, stack // 2)
        out = mm(keys_e[:n, :], q_st[cols, :].T, NN)
        near = [(0, out[:least]), (least, out[least:far_rows] + far_bias[...])]
        if j > 0:
            near.append((far_rows, out[far_rows:n - sub]))
        near.append((n - sub, out[n - sub:] + causal[...]))
        top = None
        for r, part in near:
            s[pl.ds(r, part.shape[0]), cols] = part
            part = jnp.max(fold(part), axis=0)
            top = part if top is None else jnp.maximum(top, part)
        tops[:, cols] = top

    def prob(j, at):
        n, cols = seen(j), pl.ds(j * stack + at, stack // 2)
        dp[:n, cols] = mm(keys_e[:n, :RANK], grads(j, at // sub, PAIRS).T, NN)

    state = {}

    def soft_sums(j, at):
        lane = pl.ds(j * stack + at, LANES)
        top = jnp.max(tops[:, lane], axis=0, keepdims=True)
        total = jnp.zeros((8, LANES), jnp.float32)
        delta = jnp.zeros((8, LANES), jnp.float32)
        for r, n in pieces(seen(j), 64):
            e = jnp.exp2((s[pl.ds(r, n), lane] - top) * EXP_SCALE)
            s[pl.ds(r, n), lane] = e
            total += jnp.sum(fold(e), axis=0)
            delta += jnp.sum(fold(e * dp[pl.ds(r, n), lane]), axis=0)
        inv = 1.0 / jnp.sum(total, axis=0, keepdims=True)
        state[j, at] = inv, jnp.sum(delta, axis=0, keepdims=True) * inv

    def soft_outs(j, at):
        lane = pl.ds(j * stack + at, LANES)
        inv, delta = state.pop((j, at))
        for r, n in pieces(seen(j), 64):
            p = s[pl.ds(r, n), lane] * inv
            p_low[pl.ds(r, n), lane] = p.astype(jnp.bfloat16)
            ds[0, pl.ds(r, n), lane] = (p * (dp[pl.ds(r, n), lane] - delta)).astype(ds.dtype)

    def grad_values(j, at, size):
        n, cols = seen(j), pl.ds(at, size)
        acc_v[:n, cols] += mm(p_low[:n, lanes(j)], grads(j, 0, 2 * PAIRS, at, size), NN)

    def grad_keys(j, at, size):
        n, cols = seen(j), pl.ds(at, size)
        acc_k[:n, cols] += mm(ds[0, :n, lanes(j)], q_st[lanes(j), cols], NN)

    def jobs_of(i):
        products, passes = [], []
        if i < parts:
            products += [functools.partial(fill, i)]
            for at in (0, stack // 2):
                products += [functools.partial(score, i, at), functools.partial(prob, i, at)]
        if 0 <= i - 2 < parts:
            products += [functools.partial(grad_values, i - 2, *c) for c in pieces(RANK, 256)]
            products += [functools.partial(grad_keys, i - 2, *c) for c in pieces(WIDTH, 256)]
        if 0 <= i - 1 < parts:
            for at in range(0, stack, LANES):
                passes += [functools.partial(job, i - 1, at) for job in (soft_sums, soft_outs)]
        order = [
            (k / len(group), g, job)
            for g, group in enumerate((products, passes)) for k, job in enumerate(group)
        ]
        return [job for _, _, job in sorted(order, key=lambda item: item[:2])]

    for i in range(parts + 2):
        for job in jobs_of(i):
            job()

    @pl.when(step < ahead)
    def _():
        put_queries(dq, ds, keys_e, keys_o)

    @pl.when(step == pl.num_programs(0) - 1)
    def _():
        acc_k[...] = acc_k[...] * SCALE
        acc_k[:, :RANK] += acc_v[...]
        part_rows = BLK // head_parts
        row, owner, second = slot_places(ancestors, owned)
        inner = mod(row, BLK)
        place = (owner * head_parts + div(inner, part_rows)) * CAP + second
        place = place * part_rows + mod(inner, part_rows)
        sel = one_hot(place, sent.shape[0])
        far = acc_k[:far_rows, :LATENT].astype(jnp.bfloat16)
        sent[...] = mm(sel, far, TN).astype(sent.dtype)
        own_rows = tok // head_parts
        for hop, out in enumerate(own_parts):
            part = lax.rem(lax.axis_index("head") + hop, head_parts)
            at = pl.multiple_of(far_rows + part * own_rows, 8)
            out[...] = acc_k[pl.ds(at, own_rows), :LATENT]


def steps_ahead(steps):
    return steps * 3 // 8


def attention(owned, head_parts, anc_count, ancestors, incoming, own, queries, d_out):
    tok = queries.shape[0]
    heads = queries.shape[1] // LATENT
    steps = heads // (2 * PAIRS)
    ahead = steps_ahead(steps)
    far_rows, rows = ANC * BLK, ANC * BLK + tok
    toks = 2 * PAIRS * tok
    stack = 2 * PAIRS * token_part(tok)
    bf16, f32 = jnp.bfloat16, jnp.float32

    def whole(i):
        return (0, 0)

    def along(i):
        return (0, i)

    own_part = (tok // head_parts, LATENT)
    return pl.pallas_call(
        functools.partial(attn_kernel, owned, head_parts, ahead),
        grid=(steps,),
        in_specs=[
            pl.BlockSpec(memory_space=pltpu.SMEM),
            pl.BlockSpec(ancestors.shape, whole),
            pl.BlockSpec(incoming.shape, whole),
            pl.BlockSpec(own.shape, whole),
            pl.BlockSpec((tok, 2 * PAIRS * LATENT), along),
            pl.BlockSpec((tok, 2 * PAIRS * RANK), along),
        ],
        out_specs=[
            pl.BlockSpec(
                (tok, 2 * PAIRS * LATENT), lambda i: (0, jnp.minimum(i, max(ahead - 1, 0)))
            ),
            pl.BlockSpec((1, rows, toks), lambda i: (jnp.maximum(i - ahead, 0), 0, 0)),
            pl.BlockSpec((rows, WIDTH), whole),
            pl.BlockSpec((rows, WIDTH), whole),
            pl.BlockSpec(incoming.shape, whole),
        ] + [pl.BlockSpec(own_part, whole)] * head_parts,
        out_shape=[
            jax.ShapeDtypeStruct(queries.shape, bf16),
            jax.ShapeDtypeStruct((steps - ahead, rows, toks), bf16),
            jax.ShapeDtypeStruct((rows, WIDTH), bf16),
            jax.ShapeDtypeStruct((rows, WIDTH), bf16),
            jax.ShapeDtypeStruct(incoming.shape, bf16),
        ] + [jax.ShapeDtypeStruct(own_part, f32)] * head_parts,
        scratch_shapes=[
            pltpu.VMEM((far_rows - LEAST_LIVE * BLK, stack // 2), f32),
            pltpu.VMEM((token_part(tok), stack // 2), f32),
            pltpu.VMEM((toks, WIDTH), bf16),
            pltpu.VMEM((rows, toks), f32),
            pltpu.VMEM((rows, toks), f32),
            pltpu.VMEM((rows, toks), bf16),
            pltpu.VMEM((8, toks), f32),
            pltpu.VMEM((rows, WIDTH), f32),
            pltpu.VMEM((rows, RANK), f32),
        ],
        compiler_params=pltpu.CompilerParams(vmem_limit_bytes=60 * MIB),
        cost_estimate=pl.CostEstimate(
            flops=2 * tok * heads * rows * (2 * LATENT + 2 * RANK),
            bytes_accessed=2 * tok * heads * (LATENT + RANK + rows),
            transcendentals=tok * heads * rows,
        ),
        name="score_gradients",
    )(anc_count, ancestors, incoming, own, queries, d_out)


def put_queries(dq, ds, keys_e, keys_o):
    tok = dq.shape[0]
    rows = ds.shape[1]
    sub = token_part(tok)
    stack = PAIRS * sub
    low = LATENT - HALF
    for j in range(tok // sub):
        n = rows - tok + (j + 1) * sub
        even = mm(ds[0, :n, pl.ds(2 * j * stack, stack)], keys_e[:n, :], TN) * SCALE
        odd = mm(ds[0, :n, pl.ds((2 * j + 1) * stack, stack)], keys_o[:n, :], TN) * SCALE
        for i in range(PAIRS):
            at = i * 2 * LATENT
            part = slice(i * sub, (i + 1) * sub)
            toks = pl.ds(j * sub, sub)
            dq[toks, at:at + low] = even[part, :low].astype(dq.dtype)
            joint = even[part, low:] + odd[part, :2 * HALF]
            dq[toks, at + low:at + low + 2 * HALF] = joint.astype(dq.dtype)
            dq[toks, at + low + 2 * HALF:at + 2 * LATENT] = odd[part, 2 * HALF:].astype(dq.dtype)


def query_kernel(keys_e, keys_o, ds, started, dq):
    put_queries(dq, ds, keys_e, keys_o)


def query_gradients(keys_e, keys_o, ds, started):
    tok = started.shape[0]
    steps = ds.shape[0]
    ahead = started.shape[1] // (2 * PAIRS * LATENT) - steps
    rows = ds.shape[1]
    return pl.pallas_call(
        query_kernel,
        grid=(steps,),
        in_specs=[
            pl.BlockSpec(keys_e.shape, lambda i: (0, 0)),
            pl.BlockSpec(keys_o.shape, lambda i: (0, 0)),
            pl.BlockSpec((1,) + ds.shape[1:], lambda i: (i, 0, 0)),
            pl.BlockSpec(memory_space=pl.ANY),
        ],
        out_specs=pl.BlockSpec((tok, 2 * PAIRS * LATENT), lambda i: (0, i + ahead)),
        out_shape=jax.ShapeDtypeStruct(started.shape, started.dtype),
        input_output_aliases={3: 0},
        compiler_params=pltpu.CompilerParams(vmem_limit_bytes=60 * MIB),
        cost_estimate=pl.CostEstimate(
            flops=4 * tok * steps * PAIRS * rows * LATENT,
            bytes_accessed=4 * tok * steps * PAIRS * (LATENT + rows),
            transcendentals=0,
        ),
        name="query_gradients",
    )(keys_e, keys_o, ds, started)


def local(queries, d_out, branch_latent, trunk_latent, ancestors, anc_count):
    leafs = lax.axis_size("leaf")
    head_parts = lax.axis_size("head")
    owned = trunk_latent.shape[0]
    part_rows = BLK // head_parts

    outgoing = pick(ancestors, trunk_latent.reshape(owned * BLK, LATENT))
    incoming = lax.all_to_all(
        outgoing.reshape(leafs, CAP * BLK, LATENT), "leaf", split_axis=0, concat_axis=0, tiled=True
    ).reshape(leafs * CAP * BLK, LATENT)

    started, ds, keys_e, keys_o, sent, mine, *others = attention(
        owned, head_parts, anc_count, ancestors, incoming, branch_latent, queries, d_out
    )

    got = lax.all_to_all(
        sent.reshape(leafs * head_parts, CAP * part_rows, LATENT),
        ("leaf", "head"), split_axis=0, concat_axis=0, tiled=True,
    ).reshape(leafs * CAP * BLK, LATENT)
    theirs = []
    for hop, part in enumerate(others, 1):
        route = [(i, (i + hop) % head_parts) for i in range(head_parts)]
        theirs.append(lax.ppermute(part, "head", route))

    d_queries = query_gradients(keys_e, keys_o, ds, started)
    d_branch, d_trunk = finish(ancestors, got, mine, theirs, owned, part_rows)
    return d_queries, d_branch, d_trunk


def solution(mesh):
    return jax.shard_map(
        local,
        mesh=mesh,
        in_specs=(
            P("leaf", "head"),
            P("leaf", "head"),
            P("leaf", None),
            P("leaf", None, None),
            P(),
            P(),
        ),
        out_specs=(P("leaf", "head"), P(("leaf", "head"), None), P("leaf", "head", None)),
        check_vma=False,
    )
```

```python
import functools
import math

import jax
import jax.numpy as jnp
from jax import lax
from jax.experimental import pallas as pl
from jax.experimental.pallas import tpu as pltpu
from jax.sharding import PartitionSpec as P

RANK = 512
QK_HEAD = 192
LATENT = 576
BLK = 8
CAP = 2
ANC = 32
LEAST_LIVE = 24
LANES = 128
WIDTH = 640
HALF = WIDTH - LATENT
PAIRS = 4
MASKED = -1e30
FAR_OFF = 1 << 20
SCALE = float(QK_HEAD) ** -0.5
EXP_SCALE = SCALE * math.log2(math.e)
MIB = 1024 * 1024
NT = (((1,), (1,)), ((), ()))
NN = (((1,), (0,)), ((), ()))
TN = (((0,), (0,)), ((), ()))


def mm(a, b, dims):
    return lax.dot_general(a, b, dims, preferred_element_type=jnp.float32)


def pieces(total, size):
    return [(at, min(size, total - at)) for at in range(0, total, size)]


def div(x, n):
    return x >> (n.bit_length() - 1) if n & (n - 1) == 0 else lax.div(x, jnp.full_like(x, n))


def mod(x, n):
    return x - div(x, n) * n


def column(rows):
    return lax.broadcasted_iota(jnp.int32, (rows, 1), 0)


def one_hot(place, size):
    lane = lax.broadcasted_iota(jnp.int32, (place.shape[0], size), 1)
    return jnp.where(lane == place, 1.0, 0.0).astype(jnp.bfloat16)


def token_part(tok):
    return 64 if tok % 64 == 0 else tok


def listed_blocks(ancestors, owned, second):
    leafs = ancestors.shape[0]
    rows = leafs * CAP * BLK
    named = ancestors[...].astype(jnp.float32)
    named = jnp.broadcast_to(named[:, None, :], (leafs, CAP * BLK, ANC)).reshape(rows, ANC)
    first = lax.axis_index("leaf") * owned
    low_end = first.astype(jnp.float32)
    mine = (named >= low_end) & (named < low_end + owned)
    low = jnp.min(jnp.where(mine, named, float(FAR_OFF)), axis=1, keepdims=True)
    high = jnp.max(jnp.where(mine, named, -1.0), axis=1, keepdims=True)
    return jnp.where(second, high, low).astype(jnp.int32) - first


def pick_kernel(ancestors, trunk, out):
    owned = trunk.shape[0] // BLK
    row = column(out.shape[0])
    block = listed_blocks(ancestors, owned, mod(div(row, BLK), CAP) == 1)
    sel = one_hot(block * BLK + mod(row, BLK), trunk.shape[0])
    out[...] = mm(sel, trunk[...], NN).astype(out.dtype)


def pick(ancestors, trunk):
    rows = ancestors.shape[0] * CAP * BLK
    return pl.pallas_call(
        pick_kernel,
        out_shape=jax.ShapeDtypeStruct((rows, LATENT), trunk.dtype),
        name="pick_blocks",
    )(ancestors, trunk)


def finish_kernel(ancestors, got, mine, *rest):
    theirs, (d_branch, d_trunk) = rest[:-2], rest[-2:]
    owned, part_rows = d_trunk.shape[0], d_trunk.shape[1]
    row = column(got.shape[0])
    block = listed_blocks(ancestors, owned, mod(div(row, part_rows), CAP) == 1)
    sel = one_hot(block * part_rows + mod(row, part_rows), owned * part_rows)
    total = mm(sel, got[...], TN)
    for b in range(owned):
        d_trunk[b] = total[b * part_rows:(b + 1) * part_rows]
    own = mine[...]
    for other in theirs:
        own = own + other[...]
    d_branch[...] = own


def finish(ancestors, got, mine, theirs, owned, part_rows):
    return pl.pallas_call(
        finish_kernel,
        out_shape=[
            jax.ShapeDtypeStruct(mine.shape, jnp.float32),
            jax.ShapeDtypeStruct((owned, part_rows, LATENT), jnp.float32),
        ],
        compiler_params=pltpu.CompilerParams(vmem_limit_bytes=8 * MIB),
        name="sum_gradients",
    )(ancestors, got, mine, *theirs)


def slot_places(ancestors, owned):
    row = column(ANC * BLK)
    mine = ancestors[pl.ds(lax.axis_index("leaf"), 1), :].astype(jnp.float32)
    mine = jnp.broadcast_to(mine, (ANC * BLK, ANC))
    lane = lax.broadcasted_iota(jnp.int32, (ANC * BLK, ANC), 1)
    block = jnp.max(jnp.where(lane == div(row, BLK), mine, -1.0), axis=1, keepdims=True)
    owner = div(block.astype(jnp.int32), owned)
    low_end = (owner * owned).astype(jnp.float32)
    below = (mine >= low_end) & (mine < block)
    second = jnp.max(jnp.where(below, 1.0, 0.0), axis=1, keepdims=True).astype(jnp.int32)
    return row, owner, second


def attn_kernel(
    owned, head_parts, ahead, anc_count, ancestors, incoming, own, q, do, dq, ds, keys_e, keys_o, sent,
    *rest
):
    own_parts = rest[:head_parts]
    scratch = rest[head_parts:]
    k_e, k_o, far_bias, causal, q_st, do_st, s, dp, p_low, d_low, tops, acc_k, acc_v = scratch
    tok = q.shape[0]
    far_rows, rows = ANC * BLK, ANC * BLK + tok
    sub = token_part(tok)
    parts = tok // sub
    stack = 2 * PAIRS * sub
    least = LEAST_LIVE * BLK
    step = pl.program_id(0)

    @pl.when(step == 0)
    def _():
        row, owner, second = slot_places(ancestors, owned)
        sel = one_hot((owner * CAP + second) * BLK + mod(row, BLK), incoming.shape[0])
        far = mm(sel, incoming[...], NN)
        joined = jnp.concatenate([far, own[...].astype(jnp.float32)], axis=0)
        padded = jnp.concatenate([joined, jnp.zeros((rows, HALF), jnp.float32)], axis=1)
        k_e[...] = padded.astype(jnp.bfloat16)
        k_o[...] = pltpu.roll(padded, HALF, axis=1).astype(jnp.bfloat16)
        keys_e[...] = k_e[...]
        keys_o[...] = k_o[...]
        live = anc_count[lax.axis_index("leaf")]
        slot = div(lax.broadcasted_iota(jnp.int32, far_bias.shape, 0) + least, BLK)
        far_bias[...] = jnp.where(slot < live, 0.0, MASKED)
        key_at = lax.broadcasted_iota(jnp.int32, causal.shape, 0)
        tok_at = mod(lax.broadcasted_iota(jnp.int32, causal.shape, 1), sub)
        causal[...] = jnp.where(key_at <= tok_at, 0.0, MASKED)
        acc_k[...] = jnp.zeros_like(acc_k)
        acc_v[...] = jnp.zeros_like(acc_v)

    def seen(j):
        return far_rows + (j + 1) * sub

    def lanes(j):
        return pl.ds(j * stack, stack)

    def fill(j):
        toks = pl.ds(j * sub, sub)
        for i in range(PAIRS):
            at = i * 2 * LATENT
            q_st[pl.ds(j * stack + i * sub, sub), :] = q[toks, at:at + WIDTH]
            odd = q[toks, at + LATENT - HALF:at + 2 * LATENT]
            odd = pltpu.roll(odd, WIDTH - HALF, axis=1)
            q_st[pl.ds(j * stack + (PAIRS + i) * sub, sub), :] = odd
            for par in range(2):
                block = do[toks, pl.ds((2 * i + par) * RANK, RANK)]
                do_st[pl.ds(j * stack + (par * PAIRS + i) * sub, sub), :] = block

    def fold(x):
        return x.reshape(-1, 8, x.shape[1])

    def score(j, at):
        n, cols = seen(j), pl.ds(j * stack + at, stack // 2)
        out = mm(k_e[:n, :], q_st[cols, :], NT)
        near = [(0, out[:least]), (least, out[least:far_rows] + far_bias[...])]
        if j > 0:
            near.append((far_rows, out[far_rows:n - sub]))
        near.append((n - sub, out[n - sub:] + causal[...]))
        top = None
        for r, part in near:
            s[pl.ds(r, part.shape[0]), cols] = part
            part = jnp.max(fold(part), axis=0)
            top = part if top is None else jnp.maximum(top, part)
        tops[:, cols] = top

    def prob(j, at):
        n, cols = seen(j), pl.ds(j * stack + at, stack // 2)
        dp[:n, cols] = mm(k_e[:n, :RANK], do_st[cols, :], NT)

    state = {}

    def soft_sums(j, at):
        lane = pl.ds(j * stack + at, LANES)
        top = jnp.max(tops[:, lane], axis=0, keepdims=True)
        total = jnp.zeros((8, LANES), jnp.float32)
        delta = jnp.zeros((8, LANES), jnp.float32)
        for r, n in pieces(seen(j), 64):
            e = jnp.exp2((s[pl.ds(r, n), lane] - top) * EXP_SCALE)
            s[pl.ds(r, n), lane] = e
            total += jnp.sum(fold(e), axis=0)
            delta += jnp.sum(fold(e * dp[pl.ds(r, n), lane]), axis=0)
        inv = 1.0 / jnp.sum(total, axis=0, keepdims=True)
        state[j, at] = inv, jnp.sum(delta, axis=0, keepdims=True) * inv

    def soft_outs(j, at):
        lane = pl.ds(j * stack + at, LANES)
        inv, delta = state.pop((j, at))
        for r, n in pieces(seen(j), 64):
            p = s[pl.ds(r, n), lane] * inv
            p_low[pl.ds(r, n), lane] = p.astype(jnp.bfloat16)
            d_low[pl.ds(r, n), lane] = (p * (dp[pl.ds(r, n), lane] - delta)).astype(ds.dtype)

    def grad_values(j, at, size):
        n, cols = seen(j), pl.ds(at, size)
        acc_v[:n, cols] += mm(p_low[:n, lanes(j)], do_st[lanes(j), cols], NN)

    def grad_keys(j, at, size):
        n, cols = seen(j), pl.ds(at, size)
        acc_k[:n, cols] += mm(d_low[:n, lanes(j)], q_st[lanes(j), cols], NN)

    def jobs_of(i):
        products, passes = [], []
        if i < parts:
            products += [functools.partial(fill, i)]
            for at in (0, stack // 2):
                products += [functools.partial(score, i, at), functools.partial(prob, i, at)]
        if 0 <= i - 2 < parts:
            products += [functools.partial(grad_values, i - 2, *c) for c in pieces(RANK, 256)]
            products += [functools.partial(grad_keys, i - 2, *c) for c in pieces(WIDTH, 256)]
        if 0 <= i - 1 < parts:
            for at in range(0, stack, LANES):
                passes += [functools.partial(job, i - 1, at) for job in (soft_sums, soft_outs)]
        order = [
            (k / len(group), g, job)
            for g, group in enumerate((products, passes)) for k, job in enumerate(group)
        ]
        return [job for _, _, job in sorted(order, key=lambda item: item[:2])]

    for i in range(parts + 2):
        for job in jobs_of(i):
            job()

    @pl.when(step < ahead)
    def _():
        put_queries(dq, d_low, k_e, k_o)

    @pl.when(step >= ahead)
    def _():
        for j in range(parts):
            ds[0, :seen(j), lanes(j)] = d_low[:seen(j), lanes(j)]

    @pl.when(step == pl.num_programs(0) - 1)
    def _():
        acc_k[...] = acc_k[...] * SCALE
        acc_k[:, :RANK] += acc_v[...]
        part_rows = BLK // head_parts
        row, owner, second = slot_places(ancestors, owned)
        inner = mod(row, BLK)
        place = (owner * head_parts + div(inner, part_rows)) * CAP + second
        place = place * part_rows + mod(inner, part_rows)
        sel = one_hot(place, sent.shape[0])
        far = acc_k[:far_rows, :LATENT].astype(jnp.bfloat16)
        sent[...] = mm(sel, far, TN).astype(sent.dtype)
        own_rows = tok // head_parts
        for hop, out in enumerate(own_parts):
            part = lax.rem(lax.axis_index("head") + hop, head_parts)
            at = pl.multiple_of(far_rows + part * own_rows, 8)
            out[...] = acc_k[pl.ds(at, own_rows), :LATENT]


def steps_ahead(steps):
    return steps * 3 // 8


def attention(owned, head_parts, anc_count, ancestors, incoming, own, queries, d_out):
    tok = queries.shape[0]
    heads = queries.shape[1] // LATENT
    steps = heads // (2 * PAIRS)
    ahead = steps_ahead(steps)
    far_rows, rows = ANC * BLK, ANC * BLK + tok
    toks = 2 * PAIRS * tok
    stack = 2 * PAIRS * token_part(tok)
    bf16, f32 = jnp.bfloat16, jnp.float32

    def whole(i):
        return (0, 0)

    def along(i):
        return (0, i)

    own_part = (tok // head_parts, LATENT)
    return pl.pallas_call(
        functools.partial(attn_kernel, owned, head_parts, ahead),
        grid=(steps,),
        in_specs=[
            pl.BlockSpec(memory_space=pltpu.SMEM),
            pl.BlockSpec(ancestors.shape, whole),
            pl.BlockSpec(incoming.shape, whole),
            pl.BlockSpec(own.shape, whole),
            pl.BlockSpec((tok, 2 * PAIRS * LATENT), along),
            pl.BlockSpec((tok, 2 * PAIRS * RANK), along),
        ],
        out_specs=[
            pl.BlockSpec(
                (tok, 2 * PAIRS * LATENT), lambda i: (0, jnp.minimum(i, max(ahead - 1, 0)))
            ),
            pl.BlockSpec((1, rows, toks), lambda i: (jnp.maximum(i - ahead, 0), 0, 0)),
            pl.BlockSpec((rows, WIDTH), whole),
            pl.BlockSpec((rows, WIDTH), whole),
            pl.BlockSpec(incoming.shape, whole),
        ] + [pl.BlockSpec(own_part, whole)] * head_parts,
        out_shape=[
            jax.ShapeDtypeStruct(queries.shape, bf16),
            jax.ShapeDtypeStruct((steps - ahead, rows, toks), bf16),
            jax.ShapeDtypeStruct((rows, WIDTH), bf16),
            jax.ShapeDtypeStruct((rows, WIDTH), bf16),
            jax.ShapeDtypeStruct(incoming.shape, bf16),
        ] + [jax.ShapeDtypeStruct(own_part, f32)] * head_parts,
        scratch_shapes=[
            pltpu.VMEM((rows, WIDTH), bf16),
            pltpu.VMEM((rows, WIDTH), bf16),
            pltpu.VMEM((far_rows - LEAST_LIVE * BLK, stack // 2), f32),
            pltpu.VMEM((token_part(tok), stack // 2), f32),
            pltpu.VMEM((toks, WIDTH), bf16),
            pltpu.VMEM((toks, RANK), bf16),
            pltpu.VMEM((rows, toks), f32),
            pltpu.VMEM((rows, toks), f32),
            pltpu.VMEM((rows, toks), bf16),
            pltpu.VMEM((rows, toks), bf16),
            pltpu.VMEM((8, toks), f32),
            pltpu.VMEM((rows, WIDTH), f32),
            pltpu.VMEM((rows, RANK), f32),
        ],
        compiler_params=pltpu.CompilerParams(vmem_limit_bytes=60 * MIB),
        cost_estimate=pl.CostEstimate(
            flops=2 * tok * heads * rows * (2 * LATENT + 2 * RANK),
            bytes_accessed=2 * tok * heads * (LATENT + RANK + rows),
            transcendentals=tok * heads * rows,
        ),
        name="score_gradients",
    )(anc_count, ancestors, incoming, own, queries, d_out)


def put_queries(dq, ds, keys_e, keys_o):
    tok = dq.shape[0]
    rows = ds.shape[0]
    sub = token_part(tok)
    stack = PAIRS * sub
    low = LATENT - HALF
    for j in range(tok // sub):
        n = rows - tok + (j + 1) * sub
        even = mm(ds[:n, pl.ds(2 * j * stack, stack)], keys_e[:n, :], TN) * SCALE
        odd = mm(ds[:n, pl.ds((2 * j + 1) * stack, stack)], keys_o[:n, :], TN) * SCALE
        for i in range(PAIRS):
            at = i * 2 * LATENT
            part = slice(i * sub, (i + 1) * sub)
            toks = pl.ds(j * sub, sub)
            dq[toks, at:at + low] = even[part, :low].astype(dq.dtype)
            joint = even[part, low:] + odd[part, :2 * HALF]
            dq[toks, at + low:at + low + 2 * HALF] = joint.astype(dq.dtype)
            dq[toks, at + low + 2 * HALF:at + 2 * LATENT] = odd[part, 2 * HALF:].astype(dq.dtype)


def query_kernel(keys_e, keys_o, ds, started, dq):
    put_queries(dq, ds.at[0], keys_e, keys_o)


def query_gradients(keys_e, keys_o, ds, started):
    tok = started.shape[0]
    steps = ds.shape[0]
    ahead = started.shape[1] // (2 * PAIRS * LATENT) - steps
    rows = ds.shape[1]
    return pl.pallas_call(
        query_kernel,
        grid=(steps,),
        in_specs=[
            pl.BlockSpec(keys_e.shape, lambda i: (0, 0)),
            pl.BlockSpec(keys_o.shape, lambda i: (0, 0)),
            pl.BlockSpec((1,) + ds.shape[1:], lambda i: (i, 0, 0)),
            pl.BlockSpec(memory_space=pl.ANY),
        ],
        out_specs=pl.BlockSpec((tok, 2 * PAIRS * LATENT), lambda i: (0, i + ahead)),
        out_shape=jax.ShapeDtypeStruct(started.shape, started.dtype),
        input_output_aliases={3: 0},
        compiler_params=pltpu.CompilerParams(vmem_limit_bytes=60 * MIB),
        cost_estimate=pl.CostEstimate(
            flops=4 * tok * steps * PAIRS * rows * LATENT,
            bytes_accessed=4 * tok * steps * PAIRS * (LATENT + rows),
            transcendentals=0,
        ),
        name="query_gradients",
    )(keys_e, keys_o, ds, started)


def local(queries, d_out, branch_latent, trunk_latent, ancestors, anc_count):
    leafs = lax.axis_size("leaf")
    head_parts = lax.axis_size("head")
    owned = trunk_latent.shape[0]
    part_rows = BLK // head_parts

    outgoing = pick(ancestors, trunk_latent.reshape(owned * BLK, LATENT))
    incoming = lax.all_to_all(
        outgoing.reshape(leafs, CAP * BLK, LATENT), "leaf", split_axis=0, concat_axis=0, tiled=True
    ).reshape(leafs * CAP * BLK, LATENT)

    started, ds, keys_e, keys_o, sent, mine, *others = attention(
        owned, head_parts, anc_count, ancestors, incoming, branch_latent, queries, d_out
    )

    got = lax.all_to_all(
        sent.reshape(leafs * head_parts, CAP * part_rows, LATENT),
        ("leaf", "head"), split_axis=0, concat_axis=0, tiled=True,
    ).reshape(leafs * CAP * BLK, LATENT)
    theirs = []
    for hop, part in enumerate(others, 1):
        route = [(i, (i + hop) % head_parts) for i in range(head_parts)]
        theirs.append(lax.ppermute(part, "head", route))

    d_queries = query_gradients(keys_e, keys_o, ds, started)
    d_branch, d_trunk = finish(ancestors, got, mine, theirs, owned, part_rows)
    return d_queries, d_branch, d_trunk


def solution(mesh):
    return jax.shard_map(
        local,
        mesh=mesh,
        in_specs=(
            P("leaf", "head"),
            P("leaf", "head"),
            P("leaf", None),
            P("leaf", None, None),
            P(),
            P(),
        ),
        out_specs=(P("leaf", "head"), P(("leaf", "head"), None), P("leaf", "head", None)),
        check_vma=False,
    )
```

```python
import functools
import math

import jax
import jax.numpy as jnp
from jax import lax
from jax.experimental import pallas as pl
from jax.experimental.pallas import tpu as pltpu
from jax.sharding import PartitionSpec as P

RANK = 512
QK_HEAD = 192
LATENT = 576
BLK = 8
CAP = 2
ANC = 32
LEAST_LIVE = 24
LANES = 128
WIDTH = 640
HALF = WIDTH - LATENT
PAIRS = 4
MASKED = -1e30
FAR_OFF = 1 << 20
SCALE = float(QK_HEAD) ** -0.5
EXP_SCALE = SCALE * math.log2(math.e)
MIB = 1024 * 1024
NT = (((1,), (1,)), ((), ()))
NN = (((1,), (0,)), ((), ()))
TN = (((0,), (0,)), ((), ()))


def mm(a, b, dims):
    return lax.dot_general(a, b, dims, preferred_element_type=jnp.float32)


def pieces(total, size):
    return [(at, min(size, total - at)) for at in range(0, total, size)]


def div(x, n):
    return x >> (n.bit_length() - 1) if n & (n - 1) == 0 else lax.div(x, jnp.full_like(x, n))


def mod(x, n):
    return x - div(x, n) * n


def column(rows):
    return lax.broadcasted_iota(jnp.int32, (rows, 1), 0)


def one_hot(place, size):
    lane = lax.broadcasted_iota(jnp.int32, (place.shape[0], size), 1)
    return jnp.where(lane == place, 1.0, 0.0).astype(jnp.bfloat16)


def build_keys(k_e, k_o, ancestors, incoming, own, owned):
    rows = k_e.shape[0]
    row, owner, second = slot_places(ancestors, owned)
    sel = one_hot((owner * CAP + second) * BLK + mod(row, BLK), incoming.shape[0])
    far = mm(sel, incoming[...], NN)
    joined = jnp.concatenate([far, own[...].astype(jnp.float32)], axis=0)
    padded = jnp.concatenate([joined, jnp.zeros((rows, HALF), jnp.float32)], axis=1)
    k_e[...] = padded.astype(jnp.bfloat16)
    k_o[...] = pltpu.roll(padded, HALF, axis=1).astype(jnp.bfloat16)


def token_part(tok):
    return 64 if tok % 64 == 0 else tok


def listed_blocks(ancestors, owned, second):
    leafs = ancestors.shape[0]
    rows = leafs * CAP * BLK
    named = ancestors[...].astype(jnp.float32)
    named = jnp.broadcast_to(named[:, None, :], (leafs, CAP * BLK, ANC)).reshape(rows, ANC)
    first = lax.axis_index("leaf") * owned
    low_end = first.astype(jnp.float32)
    mine = (named >= low_end) & (named < low_end + owned)
    low = jnp.min(jnp.where(mine, named, float(FAR_OFF)), axis=1, keepdims=True)
    high = jnp.max(jnp.where(mine, named, -1.0), axis=1, keepdims=True)
    return jnp.where(second, high, low).astype(jnp.int32) - first


def pick_kernel(ancestors, trunk, out):
    owned = trunk.shape[0] // BLK
    row = column(out.shape[0])
    block = listed_blocks(ancestors, owned, mod(div(row, BLK), CAP) == 1)
    sel = one_hot(block * BLK + mod(row, BLK), trunk.shape[0])
    out[...] = mm(sel, trunk[...], NN).astype(out.dtype)


def pick(ancestors, trunk):
    rows = ancestors.shape[0] * CAP * BLK
    return pl.pallas_call(
        pick_kernel,
        out_shape=jax.ShapeDtypeStruct((rows, LATENT), trunk.dtype),
        name="pick_blocks",
    )(ancestors, trunk)


def finish_kernel(ancestors, got, mine, *rest):
    theirs, (d_branch, d_trunk) = rest[:-2], rest[-2:]
    owned, part_rows = d_trunk.shape[0], d_trunk.shape[1]
    row = column(got.shape[0])
    block = listed_blocks(ancestors, owned, mod(div(row, part_rows), CAP) == 1)
    sel = one_hot(block * part_rows + mod(row, part_rows), owned * part_rows)
    total = mm(sel, got[...], TN)
    for b in range(owned):
        d_trunk[b] = total[b * part_rows:(b + 1) * part_rows]
    own = mine[...]
    for other in theirs:
        own = own + other[...]
    d_branch[...] = own


def finish(ancestors, got, mine, theirs, owned, part_rows):
    return pl.pallas_call(
        finish_kernel,
        out_shape=[
            jax.ShapeDtypeStruct(mine.shape, jnp.float32),
            jax.ShapeDtypeStruct((owned, part_rows, LATENT), jnp.float32),
        ],
        compiler_params=pltpu.CompilerParams(vmem_limit_bytes=8 * MIB),
        name="sum_gradients",
    )(ancestors, got, mine, *theirs)


def slot_places(ancestors, owned):
    row = column(ANC * BLK)
    mine = ancestors[pl.ds(lax.axis_index("leaf"), 1), :].astype(jnp.float32)
    mine = jnp.broadcast_to(mine, (ANC * BLK, ANC))
    lane = lax.broadcasted_iota(jnp.int32, (ANC * BLK, ANC), 1)
    block = jnp.max(jnp.where(lane == div(row, BLK), mine, -1.0), axis=1, keepdims=True)
    owner = div(block.astype(jnp.int32), owned)
    low_end = (owner * owned).astype(jnp.float32)
    below = (mine >= low_end) & (mine < block)
    second = jnp.max(jnp.where(below, 1.0, 0.0), axis=1, keepdims=True).astype(jnp.int32)
    return row, owner, second


def attn_kernel(
    owned, head_parts, ahead, anc_count, ancestors, incoming, own, q, do, dq, ds, sent, *rest
):
    own_parts = rest[:head_parts]
    scratch = rest[head_parts:]
    k_e, k_o, far_bias, causal, q_st, do_st, s, dp, p_low, d_low, tops, acc_k, acc_v = scratch
    tok = q.shape[0]
    far_rows, rows = ANC * BLK, ANC * BLK + tok
    sub = token_part(tok)
    parts = tok // sub
    stack = 2 * PAIRS * sub
    least = LEAST_LIVE * BLK
    step = pl.program_id(0)

    @pl.when(step == 0)
    def _():
        build_keys(k_e, k_o, ancestors, incoming, own, owned)
        live = anc_count[lax.axis_index("leaf")]
        slot = div(lax.broadcasted_iota(jnp.int32, far_bias.shape, 0) + least, BLK)
        far_bias[...] = jnp.where(slot < live, 0.0, MASKED)
        key_at = lax.broadcasted_iota(jnp.int32, causal.shape, 0)
        tok_at = mod(lax.broadcasted_iota(jnp.int32, causal.shape, 1), sub)
        causal[...] = jnp.where(key_at <= tok_at, 0.0, MASKED)
        acc_k[...] = jnp.zeros_like(acc_k)
        acc_v[...] = jnp.zeros_like(acc_v)

    def seen(j):
        return far_rows + (j + 1) * sub

    def lanes(j):
        return pl.ds(j * stack, stack)

    def fill(j):
        toks = pl.ds(j * sub, sub)
        for i in range(PAIRS):
            at = i * 2 * LATENT
            half, pair = divmod(i, PAIRS // 2)
            even, odd = [j * stack + (half * PAIRS + par * PAIRS // 2 + pair) * sub for par in range(2)]
            q_st[pl.ds(even, sub), :] = q[toks, at:at + WIDTH]
            moved = pltpu.roll(q[toks, at + LATENT - HALF:at + 2 * LATENT], WIDTH - HALF, axis=1)
            q_st[pl.ds(odd, sub), :] = moved
            do_st[pl.ds(even, sub), :] = do[toks, pl.ds(2 * i * RANK, RANK)]
            do_st[pl.ds(odd, sub), :] = do[toks, pl.ds((2 * i + 1) * RANK, RANK)]

    def fold(x):
        return x.reshape(-1, 8, x.shape[1])

    def score(j, at):
        n, cols = seen(j), pl.ds(j * stack + at, stack // 2)
        out = mm(k_e[:n, :], q_st[cols, :], NT)
        near = [(0, out[:least]), (least, out[least:far_rows] + far_bias[...])]
        if j > 0:
            near.append((far_rows, out[far_rows:n - sub]))
        near.append((n - sub, out[n - sub:] + causal[...]))
        top = None
        for r, part in near:
            s[pl.ds(r, part.shape[0]), cols] = part
            part = jnp.max(fold(part), axis=0)
            top = part if top is None else jnp.maximum(top, part)
        tops[:, cols] = top

    def prob(j, at):
        n, cols = seen(j), pl.ds(j * stack + at, stack // 2)
        dp[:n, cols] = mm(k_e[:n, :RANK], do_st[cols, :], NT)

    state = {}

    def soft_sums(j, at):
        lane = pl.ds(j * stack + at, LANES)
        top = jnp.max(tops[:, lane], axis=0, keepdims=True)
        total = jnp.zeros((8, LANES), jnp.float32)
        delta = jnp.zeros((8, LANES), jnp.float32)
        for r, n in pieces(seen(j), 64):
            e = jnp.exp2((s[pl.ds(r, n), lane] - top) * EXP_SCALE)
            s[pl.ds(r, n), lane] = e
            total += jnp.sum(fold(e), axis=0)
            delta += jnp.sum(fold(e * dp[pl.ds(r, n), lane]), axis=0)
        inv = 1.0 / jnp.sum(total, axis=0, keepdims=True)
        state[j, at] = inv, jnp.sum(delta, axis=0, keepdims=True) * inv

    def soft_outs(j, at):
        lane = pl.ds(j * stack + at, LANES)
        inv, delta = state.pop((j, at))
        for r, n in pieces(seen(j), 64):
            p = s[pl.ds(r, n), lane] * inv
            p_low[pl.ds(r, n), lane] = p.astype(jnp.bfloat16)
            d_low[pl.ds(r, n), lane] = (p * (dp[pl.ds(r, n), lane] - delta)).astype(ds.dtype)

    def grad_values(j, at, size):
        n, cols = seen(j), pl.ds(at, size)
        acc_v[:n, cols] += mm(p_low[:n, lanes(j)], do_st[lanes(j), cols], NN)

    def grad_keys(j, at, size):
        n, cols = seen(j), pl.ds(at, size)
        acc_k[:n, cols] += mm(d_low[:n, lanes(j)], q_st[lanes(j), cols], NN)

    def jobs_of(i):
        products, passes = [], []
        if i < parts:
            products += [functools.partial(fill, i)]
            for at in (0, stack // 2):
                products += [functools.partial(score, i, at), functools.partial(prob, i, at)]
        if 0 <= i - 2 < parts:
            products += [functools.partial(grad_values, i - 2, *c) for c in pieces(RANK, 256)]
            products += [functools.partial(grad_keys, i - 2, *c) for c in pieces(WIDTH, 256)]
        if 0 <= i - 1 < parts:
            for at in range(0, stack, LANES):
                passes += [functools.partial(job, i - 1, at) for job in (soft_sums, soft_outs)]
        order = [
            (k / len(group), g, job)
            for g, group in enumerate((products, passes)) for k, job in enumerate(group)
        ]
        return [job for _, _, job in sorted(order, key=lambda item: item[:2])]

    for i in range(parts + 2):
        for job in jobs_of(i):
            job()

    wide = stack // 4
    for half in range(2):
        for j in range(parts):
            for par in range(2):
                n = seen(j)
                to = pl.ds((par * parts + j) * wide, wide)
                at = pl.ds(j * stack + (2 * half + par) * wide, wide)
                ds[half, :n, to] = d_low[:n, at]
                if n < rows:
                    ds[half, n:, to] = jnp.zeros((rows - n, wide), ds.dtype)

    @pl.when(step < ahead)
    def _():
        for half in range(2):
            put_queries(dq, half * PAIRS * LATENT, ds[half], k_e[...], k_o[...])

    @pl.when(step == pl.num_programs(0) - 1)
    def _():
        acc_k[...] = acc_k[...] * SCALE
        acc_k[:, :RANK] += acc_v[...]
        part_rows = BLK // head_parts
        row, owner, second = slot_places(ancestors, owned)
        inner = mod(row, BLK)
        place = (owner * head_parts + div(inner, part_rows)) * CAP + second
        place = place * part_rows + mod(inner, part_rows)
        sel = one_hot(place, sent.shape[0])
        far = acc_k[:far_rows, :LATENT].astype(jnp.bfloat16)
        sent[...] = mm(sel, far, TN).astype(sent.dtype)
        own_rows = tok // head_parts
        for hop, out in enumerate(own_parts):
            part = lax.rem(lax.axis_index("head") + hop, head_parts)
            at = pl.multiple_of(far_rows + part * own_rows, 8)
            out[...] = acc_k[pl.ds(at, own_rows), :LATENT]


def steps_ahead(steps):
    return steps * 3 // 8


def attention(owned, head_parts, anc_count, ancestors, incoming, own, queries, d_out):
    tok = queries.shape[0]
    heads = queries.shape[1] // LATENT
    steps = heads // (2 * PAIRS)
    ahead = steps_ahead(steps)
    far_rows, rows = ANC * BLK, ANC * BLK + tok
    toks = 2 * PAIRS * tok
    stack = 2 * PAIRS * token_part(tok)
    bf16, f32 = jnp.bfloat16, jnp.float32

    def whole(i):
        return (0, 0)

    def along(i):
        return (0, i)

    own_part = (tok // head_parts, LATENT)
    return pl.pallas_call(
        functools.partial(attn_kernel, owned, head_parts, ahead),
        grid=(steps,),
        in_specs=[
            pl.BlockSpec(memory_space=pltpu.SMEM),
            pl.BlockSpec(ancestors.shape, whole),
            pl.BlockSpec(incoming.shape, whole),
            pl.BlockSpec(own.shape, whole),
            pl.BlockSpec((tok, 2 * PAIRS * LATENT), along),
            pl.BlockSpec((tok, 2 * PAIRS * RANK), along),
        ],
        out_specs=[
            pl.BlockSpec(
                (tok, 2 * PAIRS * LATENT), lambda i: (0, jnp.minimum(i, max(ahead - 1, 0)))
            ),
            pl.BlockSpec((2, rows, toks // 2), lambda i: (jnp.maximum(i - ahead, 0), 0, 0)),
            pl.BlockSpec(incoming.shape, whole),
        ] + [pl.BlockSpec(own_part, whole)] * head_parts,
        out_shape=[
            jax.ShapeDtypeStruct(queries.shape, bf16),
            jax.ShapeDtypeStruct((2 * (steps - ahead), rows, toks // 2), bf16),
            jax.ShapeDtypeStruct(incoming.shape, bf16),
        ] + [jax.ShapeDtypeStruct(own_part, f32)] * head_parts,
        scratch_shapes=[
            pltpu.VMEM((rows, WIDTH), bf16),
            pltpu.VMEM((rows, WIDTH), bf16),
            pltpu.VMEM((far_rows - LEAST_LIVE * BLK, stack // 2), f32),
            pltpu.VMEM((token_part(tok), stack // 2), f32),
            pltpu.VMEM((toks, WIDTH), bf16),
            pltpu.VMEM((toks, RANK), bf16),
            pltpu.VMEM((rows, toks), f32),
            pltpu.VMEM((rows, toks), f32),
            pltpu.VMEM((rows, toks), bf16),
            pltpu.VMEM((rows, toks), bf16),
            pltpu.VMEM((8, toks), f32),
            pltpu.VMEM((rows, WIDTH), f32),
            pltpu.VMEM((rows, RANK), f32),
        ],
        compiler_params=pltpu.CompilerParams(vmem_limit_bytes=60 * MIB),
        cost_estimate=pl.CostEstimate(
            flops=2 * tok * heads * rows * (2 * LATENT + 2 * RANK),
            bytes_accessed=2 * tok * heads * (LATENT + RANK + rows),
            transcendentals=tok * heads * rows,
        ),
        name="score_gradients",
    )(anc_count, ancestors, incoming, own, queries, d_out)


def put_queries(dq, first, ds, keys_e, keys_o):
    tok = dq.shape[0]
    sub = token_part(tok)
    pairs = PAIRS // 2
    toks = pairs * tok
    low = LATENT - HALF
    even = mm(ds[:, :toks], keys_e, TN) * SCALE
    odd = mm(ds[:, toks:], keys_o, TN) * SCALE
    for j in range(tok // sub):
        for i in range(pairs):
            at = first + i * 2 * LATENT
            part = slice((j * pairs + i) * sub, (j * pairs + i + 1) * sub)
            to = pl.ds(j * sub, sub)
            dq[to, at:at + low] = even[part, :low].astype(dq.dtype)
            joint = even[part, low:] + odd[part, :2 * HALF]
            dq[to, at + low:at + low + 2 * HALF] = joint.astype(dq.dtype)
            dq[to, at + low + 2 * HALF:at + 2 * LATENT] = odd[part, 2 * HALF:].astype(dq.dtype)


def query_kernel(owned, ancestors, incoming, own, ds, started, dq, k_e, k_o):
    @pl.when(pl.program_id(0) == 0)
    def _():
        build_keys(k_e, k_o, ancestors, incoming, own, owned)

    put_queries(dq, 0, ds[0], k_e[...], k_o[...])


def query_gradients(owned, ancestors, incoming, own, ds, started):
    tok = started.shape[0]
    steps, rows = ds.shape[0], ds.shape[1]
    ahead = started.shape[1] // (PAIRS * LATENT) - steps

    def whole(i):
        return (0, 0)

    return pl.pallas_call(
        functools.partial(query_kernel, owned),
        grid=(steps,),
        in_specs=[
            pl.BlockSpec(ancestors.shape, whole),
            pl.BlockSpec(incoming.shape, whole),
            pl.BlockSpec(own.shape, whole),
            pl.BlockSpec((1,) + ds.shape[1:], lambda i: (i, 0, 0)),
            pl.BlockSpec(memory_space=pl.ANY),
        ],
        out_specs=pl.BlockSpec((tok, PAIRS * LATENT), lambda i: (0, i + ahead)),
        out_shape=jax.ShapeDtypeStruct(started.shape, started.dtype),
        scratch_shapes=[pltpu.VMEM((rows, WIDTH), jnp.bfloat16)] * 2,
        input_output_aliases={4: 0},
        compiler_params=pltpu.CompilerParams(vmem_limit_bytes=60 * MIB),
        cost_estimate=pl.CostEstimate(
            flops=2 * tok * steps * PAIRS * rows * LATENT,
            bytes_accessed=2 * tok * steps * PAIRS * (LATENT + rows),
            transcendentals=0,
        ),
        name="query_gradients",
    )(ancestors, incoming, own, ds, started)


def local(queries, d_out, branch_latent, trunk_latent, ancestors, anc_count):
    leafs = lax.axis_size("leaf")
    head_parts = lax.axis_size("head")
    owned = trunk_latent.shape[0]
    part_rows = BLK // head_parts

    outgoing = pick(ancestors, trunk_latent.reshape(owned * BLK, LATENT))
    incoming = lax.all_to_all(
        outgoing.reshape(leafs, CAP * BLK, LATENT), "leaf", split_axis=0, concat_axis=0, tiled=True
    ).reshape(leafs * CAP * BLK, LATENT)

    started, ds, sent, mine, *others = attention(
        owned, head_parts, anc_count, ancestors, incoming, branch_latent, queries, d_out
    )

    got = lax.all_to_all(
        sent.reshape(leafs * head_parts, CAP * part_rows, LATENT),
        ("leaf", "head"), split_axis=0, concat_axis=0, tiled=True,
    ).reshape(leafs * CAP * BLK, LATENT)
    theirs = []
    for hop, part in enumerate(others, 1):
        route = [(i, (i + hop) % head_parts) for i in range(head_parts)]
        theirs.append(lax.ppermute(part, "head", route))

    d_queries = query_gradients(owned, ancestors, incoming, branch_latent, ds, started)
    d_branch, d_trunk = finish(ancestors, got, mine, theirs, owned, part_rows)
    return d_queries, d_branch, d_trunk


def solution(mesh):
    return jax.shard_map(
        local,
        mesh=mesh,
        in_specs=(
            P("leaf", "head"),
            P("leaf", "head"),
            P("leaf", None),
            P("leaf", None, None),
            P(),
            P(),
        ),
        out_specs=(P("leaf", "head"), P(("leaf", "head"), None), P("leaf", "head", None)),
        check_vma=False,
    )
```

```python
import functools
import math

import jax
import jax.numpy as jnp
from jax import lax
from jax.experimental import pallas as pl
from jax.experimental.pallas import tpu as pltpu
from jax.sharding import PartitionSpec as P

RANK = 512
QK_HEAD = 192
LATENT = 576
BLK = 8
CAP = 2
ANC = 32
LEAST_LIVE = 24
LANES = 128
WIDTH = 640
HALF = WIDTH - LATENT
PAIRS = 4
MASKED = -1e30
FAR_OFF = 1 << 20
SCALE = float(QK_HEAD) ** -0.5
EXP_SCALE = SCALE * math.log2(math.e)
MIB = 1024 * 1024
NT = (((1,), (1,)), ((), ()))
NN = (((1,), (0,)), ((), ()))
TN = (((0,), (0,)), ((), ()))


def mm(a, b, dims):
    return lax.dot_general(a, b, dims, preferred_element_type=jnp.float32)


def pieces(total, size):
    return [(at, min(size, total - at)) for at in range(0, total, size)]


def div(x, n):
    return x >> (n.bit_length() - 1) if n & (n - 1) == 0 else lax.div(x, jnp.full_like(x, n))


def mod(x, n):
    return x - div(x, n) * n


def column(rows):
    return lax.broadcasted_iota(jnp.int32, (rows, 1), 0)


def one_hot(place, size):
    lane = lax.broadcasted_iota(jnp.int32, (place.shape[0], size), 1)
    return jnp.where(lane == place, 1.0, 0.0).astype(jnp.bfloat16)


def token_part(tok):
    return 64 if tok % 64 == 0 else tok


def listed_blocks(ancestors, owned, second):
    leafs = ancestors.shape[0]
    rows = leafs * CAP * BLK
    named = ancestors[...].astype(jnp.float32)
    named = jnp.broadcast_to(named[:, None, :], (leafs, CAP * BLK, ANC)).reshape(rows, ANC)
    first = lax.axis_index("leaf") * owned
    low_end = first.astype(jnp.float32)
    mine = (named >= low_end) & (named < low_end + owned)
    low = jnp.min(jnp.where(mine, named, float(FAR_OFF)), axis=1, keepdims=True)
    high = jnp.max(jnp.where(mine, named, -1.0), axis=1, keepdims=True)
    return jnp.where(second, high, low).astype(jnp.int32) - first


def pick_kernel(ancestors, trunk, out):
    owned = trunk.shape[0] // BLK
    row = column(out.shape[0])
    block = listed_blocks(ancestors, owned, mod(div(row, BLK), CAP) == 1)
    sel = one_hot(block * BLK + mod(row, BLK), trunk.shape[0])
    out[...] = mm(sel, trunk[...], NN).astype(out.dtype)


def pick(ancestors, trunk):
    rows = ancestors.shape[0] * CAP * BLK
    return pl.pallas_call(
        pick_kernel,
        out_shape=jax.ShapeDtypeStruct((rows, LATENT), trunk.dtype),
        name="pick_blocks",
    )(ancestors, trunk)


def finish_kernel(ancestors, got, mine, *rest):
    theirs, (d_branch, d_trunk) = rest[:-2], rest[-2:]
    owned, part_rows = d_trunk.shape[0], d_trunk.shape[1]
    row = column(got.shape[0])
    block = listed_blocks(ancestors, owned, mod(div(row, part_rows), CAP) == 1)
    sel = one_hot(block * part_rows + mod(row, part_rows), owned * part_rows)
    total = mm(sel, got[...], TN)
    for b in range(owned):
        d_trunk[b] = total[b * part_rows:(b + 1) * part_rows]
    own = mine[...]
    for other in theirs:
        own = own + other[...]
    d_branch[...] = own


def finish(ancestors, got, mine, theirs, owned, part_rows):
    return pl.pallas_call(
        finish_kernel,
        out_shape=[
            jax.ShapeDtypeStruct(mine.shape, jnp.float32),
            jax.ShapeDtypeStruct((owned, part_rows, LATENT), jnp.float32),
        ],
        compiler_params=pltpu.CompilerParams(vmem_limit_bytes=8 * MIB),
        name="sum_gradients",
    )(ancestors, got, mine, *theirs)


def slot_places(ancestors, owned):
    row = column(ANC * BLK)
    mine = ancestors[pl.ds(lax.axis_index("leaf"), 1), :].astype(jnp.float32)
    mine = jnp.broadcast_to(mine, (ANC * BLK, ANC))
    lane = lax.broadcasted_iota(jnp.int32, (ANC * BLK, ANC), 1)
    block = jnp.max(jnp.where(lane == div(row, BLK), mine, -1.0), axis=1, keepdims=True)
    owner = div(block.astype(jnp.int32), owned)
    low_end = (owner * owned).astype(jnp.float32)
    below = (mine >= low_end) & (mine < block)
    second = jnp.max(jnp.where(below, 1.0, 0.0), axis=1, keepdims=True).astype(jnp.int32)
    return row, owner, second


def stack_heads(q, do, q_st, do_st, toks, to, heads):
    sub = toks.size
    pairs = heads // 2
    for i in range(pairs):
        at = i * 2 * LATENT
        even, odd = pl.ds(to + i * sub, sub), pl.ds(to + (pairs + i) * sub, sub)
        q_st[even, :] = q[toks, at:at + WIDTH]
        moved = q[toks, at + LATENT - HALF:at + 2 * LATENT]
        q_st[odd, :] = pltpu.roll(moved, WIDTH - HALF, axis=1)
        do_st[even, :] = do[toks, pl.ds(2 * i * RANK, RANK)]
        do_st[odd, :] = do[toks, pl.ds((2 * i + 1) * RANK, RANK)]


def causal_bias(shape, sub):
    key_at = lax.broadcasted_iota(jnp.int32, shape, 0)
    tok_at = mod(lax.broadcasted_iota(jnp.int32, shape, 1), sub)
    return jnp.where(key_at <= tok_at, 0.0, MASKED)


def own_kernel(own, q, do, s_own, dp_own, keys, causal, q_st, do_st):
    tok = own.shape[0]
    sub = q.shape[0]
    heads = 2 * PAIRS

    @pl.when(pl.program_id(0) == 0)
    def _():
        pad = jnp.zeros((tok, HALF), jnp.float32)
        padded = jnp.concatenate([own[...].astype(jnp.float32), pad], axis=1)
        keys[...] = padded.astype(jnp.bfloat16)
        causal[...] = causal_bias(causal.shape, sub)

    for group in range(s_own.shape[0]):
        cols = pl.ds(group * heads * LATENT, heads * LATENT)
        grad_cols = pl.ds(group * heads * RANK, heads * RANK)
        base = group * heads * sub
        block = pl.ds(base, heads * sub)
        stack_heads(
            q.at[:, cols], do.at[:, grad_cols], q_st, do_st, pl.ds(0, sub), base, heads
        )
        out = mm(keys[...], q_st[block, :], NT)
        s_own[group, :tok - sub] = out[:tok - sub]
        s_own[group, tok - sub:] = out[tok - sub:] + causal[...]
        dp_own[group] = mm(keys[:, :RANK], do_st[block, :], NT).astype(dp_own.dtype)


def own_scores(own, queries, d_out):
    tok = own.shape[0]
    heads = queries.shape[1] // LATENT
    steps = heads // (2 * PAIRS)
    sub = token_part(tok)
    parts = tok // sub
    unit = 2 * PAIRS * sub
    group = 2 if steps % 2 == 0 else 1
    bf16, f32 = jnp.bfloat16, jnp.float32
    return pl.pallas_call(
        own_kernel,
        grid=(steps // group,),
        in_specs=[
            pl.BlockSpec(own.shape, lambda i: (0, 0)),
            pl.BlockSpec((sub, group * 2 * PAIRS * LATENT), lambda i: (parts - 1, i)),
            pl.BlockSpec((sub, group * 2 * PAIRS * RANK), lambda i: (parts - 1, i)),
        ],
        out_specs=[pl.BlockSpec((group, tok, unit), lambda i: (i, 0, 0))] * 2,
        out_shape=[
            jax.ShapeDtypeStruct((steps, tok, unit), f32),
            jax.ShapeDtypeStruct((steps, tok, unit), bf16),
        ],
        scratch_shapes=[
            pltpu.VMEM((tok, WIDTH), bf16),
            pltpu.VMEM((sub, unit), f32),
            pltpu.VMEM((group * unit, WIDTH), bf16),
            pltpu.VMEM((group * unit, RANK), bf16),
        ],
        compiler_params=pltpu.CompilerParams(vmem_limit_bytes=60 * MIB),
        cost_estimate=pl.CostEstimate(
            flops=2 * sub * heads * tok * (LATENT + RANK),
            bytes_accessed=2 * sub * heads * (LATENT + RANK + 3 * tok),
            transcendentals=0,
        ),
        name="own_scores",
    )(own, queries, d_out)


def attn_kernel(
    owned, head_parts, ahead, anc_count, ancestors, incoming, own, s_own, dp_own, q, do,
    dq, ds, keys_e, keys_o, sent, *rest
):
    own_parts = rest[:head_parts]
    far_bias, causal, q_st, s, dp, p_low, tops, acc_k, acc_v = rest[head_parts:]
    tok = q.shape[0]
    far_rows, rows = ANC * BLK, ANC * BLK + tok
    sub = token_part(tok)
    parts = tok // sub
    stack = 2 * PAIRS * sub
    least = LEAST_LIVE * BLK
    step = pl.program_id(0)

    @pl.when(step == 0)
    def _():
        row, owner, second = slot_places(ancestors, owned)
        sel = one_hot((owner * CAP + second) * BLK + mod(row, BLK), incoming.shape[0])
        far = mm(sel, incoming[...], NN)
        joined = jnp.concatenate([far, own[...].astype(jnp.float32)], axis=0)
        padded = jnp.concatenate([joined, jnp.zeros((rows, HALF), jnp.float32)], axis=1)
        keys_e[...] = padded.astype(jnp.bfloat16)
        keys_o[...] = pltpu.roll(padded, HALF, axis=1).astype(jnp.bfloat16)
        live = anc_count[lax.axis_index("leaf")]
        slot = div(lax.broadcasted_iota(jnp.int32, far_bias.shape, 0) + least, BLK)
        far_bias[...] = jnp.where(slot < live, 0.0, MASKED)
        causal[...] = causal_bias(causal.shape, sub)
        acc_k[...] = jnp.zeros_like(acc_k)
        acc_v[...] = jnp.zeros_like(acc_v)

    def seen(j):
        return far_rows + (j + 1) * sub

    def lanes(j):
        return pl.ds(j * stack, stack)

    def fill(j):
        toks = pl.ds(j * sub, sub)
        for i in range(PAIRS):
            at = i * 2 * LATENT
            q_st[pl.ds(j * stack + i * sub, sub), :] = q[toks, at:at + WIDTH]
            odd = q[toks, at + LATENT - HALF:at + 2 * LATENT]
            odd = pltpu.roll(odd, WIDTH - HALF, axis=1)
            q_st[pl.ds(j * stack + (PAIRS + i) * sub, sub), :] = odd

    heads = list(range(0, 2 * PAIRS, 2)) + list(range(1, 2 * PAIRS, 2))

    def grads(j, first, count, at=0, size=RANK):
        toks = pl.ds(j * sub, sub)
        cols = [pl.ds(h * RANK + at, size) for h in heads[first:first + count]]
        return jnp.concatenate([do[toks, c] for c in cols], axis=0)

    def fold(x):
        return x.reshape(-1, 8, x.shape[1])

    def given(j):
        return j == parts - 1

    def score(j, at):
        n, cols = seen(j), pl.ds(j * stack + at, stack // 2)
        out = mm(keys_e[:far_rows if given(j) else n, :], q_st[cols, :].T, NN)
        near = [(0, out[:least]), (least, out[least:far_rows] + far_bias[...])]
        top = None
        if given(j):
            top = jnp.max(fold(s_own[0, :, pl.ds(at, stack // 2)]), axis=0)
        else:
            if j > 0:
                near.append((far_rows, out[far_rows:n - sub]))
            near.append((n - sub, out[n - sub:] + causal[...]))
        for r, part in near:
            s[pl.ds(r, part.shape[0]), cols] = part
            part = jnp.max(fold(part), axis=0)
            top = part if top is None else jnp.maximum(top, part)
        tops[:, cols] = top

    def prob(j, at):
        n, cols = far_rows if given(j) else seen(j), pl.ds(j * stack + at, stack // 2)
        dp[:n, cols] = mm(keys_e[:n, :RANK], grads(j, at // sub, PAIRS).T, NN)

    state = {}

    def scores_at(j, r, n, at):
        if given(j) and r >= far_rows:
            return s_own[0, pl.ds(r - far_rows, n), pl.ds(at, LANES)]
        return s[pl.ds(r, n), pl.ds(j * stack + at, LANES)]

    def probs_at(j, r, n, at):
        if given(j) and r >= far_rows:
            return dp_own[0, pl.ds(r - far_rows, n), pl.ds(at, LANES)].astype(jnp.float32)
        return dp[pl.ds(r, n), pl.ds(j * stack + at, LANES)]

    def soft_sums(j, at):
        lane = pl.ds(j * stack + at, LANES)
        top = jnp.max(tops[:, lane], axis=0, keepdims=True)
        total = jnp.zeros((8, LANES), jnp.float32)
        delta = jnp.zeros((8, LANES), jnp.float32)
        for r, n in pieces(seen(j), 64):
            e = jnp.exp2((scores_at(j, r, n, at) - top) * EXP_SCALE)
            s[pl.ds(r, n), lane] = e
            total += jnp.sum(fold(e), axis=0)
            delta += jnp.sum(fold(e * probs_at(j, r, n, at)), axis=0)
        inv = 1.0 / jnp.sum(total, axis=0, keepdims=True)
        state[j, at] = inv, jnp.sum(delta, axis=0, keepdims=True) * inv

    def soft_outs(j, at):
        lane = pl.ds(j * stack + at, LANES)
        inv, delta = state.pop((j, at))
        for r, n in pieces(seen(j), 64):
            p = s[pl.ds(r, n), lane] * inv
            p_low[pl.ds(r, n), lane] = p.astype(jnp.bfloat16)
            ds[0, pl.ds(r, n), lane] = (p * (probs_at(j, r, n, at) - delta)).astype(ds.dtype)

    def grad_values(j, at, size):
        n, cols = seen(j), pl.ds(at, size)
        acc_v[:n, cols] += mm(p_low[:n, lanes(j)], grads(j, 0, 2 * PAIRS, at, size), NN)

    def grad_keys(j, at, size):
        n, cols = seen(j), pl.ds(at, size)
        acc_k[:n, cols] += mm(ds[0, :n, lanes(j)], q_st[lanes(j), cols], NN)

    def jobs_of(i):
        products, passes = [], []
        if i < parts:
            products += [functools.partial(fill, i)]
            for at in (0, stack // 2):
                products += [functools.partial(score, i, at), functools.partial(prob, i, at)]
        if 0 <= i - 2 < parts:
            products += [functools.partial(grad_values, i - 2, *c) for c in pieces(RANK, 256)]
            products += [functools.partial(grad_keys, i - 2, *c) for c in pieces(WIDTH, 256)]
        if 0 <= i - 1 < parts:
            for at in range(0, stack, LANES):
                passes += [functools.partial(job, i - 1, at) for job in (soft_sums, soft_outs)]
        order = [
            (k / len(group), g, job)
            for g, group in enumerate((products, passes)) for k, job in enumerate(group)
        ]
        return [job for _, _, job in sorted(order, key=lambda item: item[:2])]

    for i in range(parts + 2):
        for job in jobs_of(i):
            job()

    @pl.when(step < ahead)
    def _():
        put_queries(dq, ds, keys_e, keys_o)

    @pl.when(step == pl.num_programs(0) - 1)
    def _():
        acc_k[...] = acc_k[...] * SCALE
        acc_k[:, :RANK] += acc_v[...]
        part_rows = BLK // head_parts
        row, owner, second = slot_places(ancestors, owned)
        inner = mod(row, BLK)
        place = (owner * head_parts + div(inner, part_rows)) * CAP + second
        place = place * part_rows + mod(inner, part_rows)
        sel = one_hot(place, sent.shape[0])
        far = acc_k[:far_rows, :LATENT].astype(jnp.bfloat16)
        sent[...] = mm(sel, far, TN).astype(sent.dtype)
        own_rows = tok // head_parts
        for hop, out in enumerate(own_parts):
            part = lax.rem(lax.axis_index("head") + hop, head_parts)
            at = pl.multiple_of(far_rows + part * own_rows, 8)
            out[...] = acc_k[pl.ds(at, own_rows), :LATENT]


def steps_ahead(steps):
    return steps * 3 // 8


def attention(
    owned, head_parts, anc_count, ancestors, incoming, own, s_own, dp_own, queries, d_out
):
    tok = queries.shape[0]
    heads = queries.shape[1] // LATENT
    steps = heads // (2 * PAIRS)
    ahead = steps_ahead(steps)
    far_rows, rows = ANC * BLK, ANC * BLK + tok
    toks = 2 * PAIRS * tok
    stack = 2 * PAIRS * token_part(tok)
    bf16, f32 = jnp.bfloat16, jnp.float32

    def whole(i):
        return (0, 0)

    def along(i):
        return (0, i)

    own_part = (tok // head_parts, LATENT)
    return pl.pallas_call(
        functools.partial(attn_kernel, owned, head_parts, ahead),
        grid=(steps,),
        in_specs=[
            pl.BlockSpec(memory_space=pltpu.SMEM),
            pl.BlockSpec(ancestors.shape, whole),
            pl.BlockSpec(incoming.shape, whole),
            pl.BlockSpec(own.shape, whole),
            pl.BlockSpec((1,) + s_own.shape[1:], lambda i: (i, 0, 0)),
            pl.BlockSpec((1,) + dp_own.shape[1:], lambda i: (i, 0, 0)),
            pl.BlockSpec((tok, 2 * PAIRS * LATENT), along),
            pl.BlockSpec((tok, 2 * PAIRS * RANK), along),
        ],
        out_specs=[
            pl.BlockSpec(
                (tok, 2 * PAIRS * LATENT), lambda i: (0, jnp.minimum(i, max(ahead - 1, 0)))
            ),
            pl.BlockSpec((1, rows, toks), lambda i: (jnp.maximum(i - ahead, 0), 0, 0)),
            pl.BlockSpec((rows, WIDTH), whole),
            pl.BlockSpec((rows, WIDTH), whole),
            pl.BlockSpec(incoming.shape, whole),
        ] + [pl.BlockSpec(own_part, whole)] * head_parts,
        out_shape=[
            jax.ShapeDtypeStruct(queries.shape, bf16),
            jax.ShapeDtypeStruct((steps - ahead, rows, toks), bf16),
            jax.ShapeDtypeStruct((rows, WIDTH), bf16),
            jax.ShapeDtypeStruct((rows, WIDTH), bf16),
            jax.ShapeDtypeStruct(incoming.shape, bf16),
        ] + [jax.ShapeDtypeStruct(own_part, f32)] * head_parts,
        scratch_shapes=[
            pltpu.VMEM((far_rows - LEAST_LIVE * BLK, stack // 2), f32),
            pltpu.VMEM((token_part(tok), stack // 2), f32),
            pltpu.VMEM((toks, WIDTH), bf16),
            pltpu.VMEM((rows, toks), f32),
            pltpu.VMEM((rows, toks), f32),
            pltpu.VMEM((rows, toks), bf16),
            pltpu.VMEM((8, toks), f32),
            pltpu.VMEM((rows, WIDTH), f32),
            pltpu.VMEM((rows, RANK), f32),
        ],
        compiler_params=pltpu.CompilerParams(vmem_limit_bytes=60 * MIB),
        cost_estimate=pl.CostEstimate(
            flops=2 * tok * heads * rows * (2 * LATENT + 2 * RANK),
            bytes_accessed=2 * tok * heads * (LATENT + RANK + rows),
            transcendentals=tok * heads * rows,
        ),
        name="score_gradients",
    )(anc_count, ancestors, incoming, own, s_own, dp_own, queries, d_out)


def put_queries(dq, ds, keys_e, keys_o):
    tok = dq.shape[0]
    rows = ds.shape[1]
    sub = token_part(tok)
    stack = PAIRS * sub
    low = LATENT - HALF
    for j in range(tok // sub):
        n = rows - tok + (j + 1) * sub
        even = mm(ds[0, :n, pl.ds(2 * j * stack, stack)], keys_e[:n, :], TN) * SCALE
        odd = mm(ds[0, :n, pl.ds((2 * j + 1) * stack, stack)], keys_o[:n, :], TN) * SCALE
        for i in range(PAIRS):
            at = i * 2 * LATENT
            part = slice(i * sub, (i + 1) * sub)
            toks = pl.ds(j * sub, sub)
            dq[toks, at:at + low] = even[part, :low].astype(dq.dtype)
            joint = even[part, low:] + odd[part, :2 * HALF]
            dq[toks, at + low:at + low + 2 * HALF] = joint.astype(dq.dtype)
            dq[toks, at + low + 2 * HALF:at + 2 * LATENT] = odd[part, 2 * HALF:].astype(dq.dtype)


def query_kernel(keys_e, keys_o, ds, started, dq):
    put_queries(dq, ds, keys_e, keys_o)


def query_gradients(keys_e, keys_o, ds, started):
    tok = started.shape[0]
    steps = ds.shape[0]
    ahead = started.shape[1] // (2 * PAIRS * LATENT) - steps
    rows = ds.shape[1]
    return pl.pallas_call(
        query_kernel,
        grid=(steps,),
        in_specs=[
            pl.BlockSpec(keys_e.shape, lambda i: (0, 0)),
            pl.BlockSpec(keys_o.shape, lambda i: (0, 0)),
            pl.BlockSpec((1,) + ds.shape[1:], lambda i: (i, 0, 0)),
            pl.BlockSpec(memory_space=pl.ANY),
        ],
        out_specs=pl.BlockSpec((tok, 2 * PAIRS * LATENT), lambda i: (0, i + ahead)),
        out_shape=jax.ShapeDtypeStruct(started.shape, started.dtype),
        input_output_aliases={3: 0},
        compiler_params=pltpu.CompilerParams(vmem_limit_bytes=60 * MIB),
        cost_estimate=pl.CostEstimate(
            flops=4 * tok * steps * PAIRS * rows * LATENT,
            bytes_accessed=4 * tok * steps * PAIRS * (LATENT + rows),
            transcendentals=0,
        ),
        name="query_gradients",
    )(keys_e, keys_o, ds, started)


def local(queries, d_out, branch_latent, trunk_latent, ancestors, anc_count):
    leafs = lax.axis_size("leaf")
    head_parts = lax.axis_size("head")
    owned = trunk_latent.shape[0]
    part_rows = BLK // head_parts

    outgoing = pick(ancestors, trunk_latent.reshape(owned * BLK, LATENT))
    incoming = lax.all_to_all(
        outgoing.reshape(leafs, CAP * BLK, LATENT), "leaf", split_axis=0, concat_axis=0, tiled=True
    ).reshape(leafs * CAP * BLK, LATENT)

    s_own, dp_own = own_scores(branch_latent, queries, d_out)

    started, ds, keys_e, keys_o, sent, mine, *others = attention(
        owned, head_parts, anc_count, ancestors, incoming, branch_latent, s_own, dp_own,
        queries, d_out,
    )

    got = lax.all_to_all(
        sent.reshape(leafs * head_parts, CAP * part_rows, LATENT),
        ("leaf", "head"), split_axis=0, concat_axis=0, tiled=True,
    ).reshape(leafs * CAP * BLK, LATENT)
    theirs = []
    for hop, part in enumerate(others, 1):
        route = [(i, (i + hop) % head_parts) for i in range(head_parts)]
        theirs.append(lax.ppermute(part, "head", route))

    d_queries = query_gradients(keys_e, keys_o, ds, started)
    d_branch, d_trunk = finish(ancestors, got, mine, theirs, owned, part_rows)
    return d_queries, d_branch, d_trunk


def solution(mesh):
    return jax.shard_map(
        local,
        mesh=mesh,
        in_specs=(
            P("leaf", "head"),
            P("leaf", "head"),
            P("leaf", None),
            P("leaf", None, None),
            P(),
            P(),
        ),
        out_specs=(P("leaf", "head"), P(("leaf", "head"), None), P("leaf", "head", None)),
        check_vma=False,
    )
```

```python
import functools
import math

import jax
import jax.numpy as jnp
from jax import lax
from jax.experimental import pallas as pl
from jax.experimental.pallas import tpu as pltpu
from jax.sharding import PartitionSpec as P

RANK = 512
QK_HEAD = 192
LATENT = 576
BLK = 8
CAP = 2
ANC = 32
LEAST_LIVE = 24
LANES = 128
WIDTH = 640
HALF = WIDTH - LATENT
PAIRS = 4
MASKED = -1e30
FAR_OFF = 1 << 20
SCALE = float(QK_HEAD) ** -0.5
EXP_SCALE = SCALE * math.log2(math.e)
MIB = 1024 * 1024
NT = (((1,), (1,)), ((), ()))
NN = (((1,), (0,)), ((), ()))
TN = (((0,), (0,)), ((), ()))


def mm(a, b, dims):
    return lax.dot_general(a, b, dims, preferred_element_type=jnp.float32)


def pieces(total, size):
    return [(at, min(size, total - at)) for at in range(0, total, size)]


def div(x, n):
    return x >> (n.bit_length() - 1) if n & (n - 1) == 0 else lax.div(x, jnp.full_like(x, n))


def mod(x, n):
    return x - div(x, n) * n


def column(rows):
    return lax.broadcasted_iota(jnp.int32, (rows, 1), 0)


def one_hot(place, size):
    lane = lax.broadcasted_iota(jnp.int32, (place.shape[0], size), 1)
    return jnp.where(lane == place, 1.0, 0.0).astype(jnp.bfloat16)


def token_part(tok):
    return 64 if tok % 64 == 0 else tok


def listed_blocks(ancestors, owned, second):
    leafs = ancestors.shape[0]
    rows = leafs * CAP * BLK
    named = ancestors[...].astype(jnp.float32)
    named = jnp.broadcast_to(named[:, None, :], (leafs, CAP * BLK, ANC)).reshape(rows, ANC)
    first = lax.axis_index("leaf") * owned
    low_end = first.astype(jnp.float32)
    mine = (named >= low_end) & (named < low_end + owned)
    low = jnp.min(jnp.where(mine, named, float(FAR_OFF)), axis=1, keepdims=True)
    high = jnp.max(jnp.where(mine, named, -1.0), axis=1, keepdims=True)
    return jnp.where(second, high, low).astype(jnp.int32) - first


def pick_kernel(head_parts, ancestors, trunk, out):
    owned = trunk.shape[0] // BLK
    share = CAP * BLK // head_parts
    row = lax.axis_index("head") * share + mod(column(out.shape[0]), share)
    block = listed_blocks(ancestors, owned, div(row, BLK) == 1)
    sel = one_hot(block * BLK + mod(row, BLK), trunk.shape[0])
    out[...] = mm(sel, trunk[...], NN).astype(out.dtype)


def pick(head_parts, ancestors, trunk):
    rows = ancestors.shape[0] * CAP * BLK
    return pl.pallas_call(
        functools.partial(pick_kernel, head_parts),
        out_shape=jax.ShapeDtypeStruct((rows, LATENT), trunk.dtype),
        name="pick_blocks",
    )(ancestors, trunk)


def finish_kernel(ancestors, got, mine, *rest):
    theirs, (d_branch, d_trunk) = rest[:-2], rest[-2:]
    owned, part_rows = d_trunk.shape[0], d_trunk.shape[1]
    row = column(got.shape[0])
    block = listed_blocks(ancestors, owned, mod(div(row, part_rows), CAP) == 1)
    sel = one_hot(block * part_rows + mod(row, part_rows), owned * part_rows)
    total = mm(sel, got[...], TN)
    for b in range(owned):
        d_trunk[b] = total[b * part_rows:(b + 1) * part_rows]
    own = mine[...]
    for other in theirs:
        own = own + other[...]
    d_branch[...] = own


def finish(ancestors, got, mine, theirs, owned, part_rows):
    return pl.pallas_call(
        finish_kernel,
        out_shape=[
            jax.ShapeDtypeStruct(mine.shape, jnp.float32),
            jax.ShapeDtypeStruct((owned, part_rows, LATENT), jnp.float32),
        ],
        compiler_params=pltpu.CompilerParams(vmem_limit_bytes=8 * MIB),
        name="sum_gradients",
    )(ancestors, got, mine, *theirs)


def slot_places(ancestors, owned):
    row = column(ANC * BLK)
    mine = ancestors[pl.ds(lax.axis_index("leaf"), 1), :].astype(jnp.float32)
    mine = jnp.broadcast_to(mine, (ANC * BLK, ANC))
    lane = lax.broadcasted_iota(jnp.int32, (ANC * BLK, ANC), 1)
    block = jnp.max(jnp.where(lane == div(row, BLK), mine, -1.0), axis=1, keepdims=True)
    owner = div(block.astype(jnp.int32), owned)
    low_end = (owner * owned).astype(jnp.float32)
    below = (mine >= low_end) & (mine < block)
    second = jnp.max(jnp.where(below, 1.0, 0.0), axis=1, keepdims=True).astype(jnp.int32)
    return row, owner, second


def stack_heads(q, do, q_st, do_st, toks, to, heads):
    sub = toks.size
    pairs = heads // 2
    for i in range(pairs):
        at = i * 2 * LATENT
        even, odd = pl.ds(to + i * sub, sub), pl.ds(to + (pairs + i) * sub, sub)
        q_st[even, :] = q[toks, at:at + WIDTH]
        moved = q[toks, at + LATENT - HALF:at + 2 * LATENT]
        q_st[odd, :] = pltpu.roll(moved, WIDTH - HALF, axis=1)
        do_st[even, :] = do[toks, pl.ds(2 * i * RANK, RANK)]
        do_st[odd, :] = do[toks, pl.ds((2 * i + 1) * RANK, RANK)]


def causal_bias(shape, sub):
    key_at = lax.broadcasted_iota(jnp.int32, shape, 0)
    tok_at = mod(lax.broadcasted_iota(jnp.int32, shape, 1), sub)
    return jnp.where(key_at <= tok_at, 0.0, MASKED)


def own_kernel(own, q, do, s_own, dp_own, keys, causal, q_st, do_st):
    tok = own.shape[0]
    sub = q.shape[0]
    heads = 2 * PAIRS

    @pl.when(pl.program_id(0) == 0)
    def _():
        pad = jnp.zeros((tok, HALF), jnp.float32)
        padded = jnp.concatenate([own[...].astype(jnp.float32), pad], axis=1)
        keys[...] = padded.astype(jnp.bfloat16)
        causal[...] = causal_bias(causal.shape, sub)

    for group in range(s_own.shape[0]):
        cols = pl.ds(group * heads * LATENT, heads * LATENT)
        grad_cols = pl.ds(group * heads * RANK, heads * RANK)
        base = group * heads * sub
        block = pl.ds(base, heads * sub)
        stack_heads(
            q.at[:, cols], do.at[:, grad_cols], q_st, do_st, pl.ds(0, sub), base, heads
        )
        out = mm(keys[...], q_st[block, :], NT)
        s_own[group, :tok - sub] = out[:tok - sub]
        s_own[group, tok - sub:] = out[tok - sub:] + causal[...]
        dp_own[group] = mm(keys[:, :RANK], do_st[block, :], NT).astype(dp_own.dtype)


def own_scores(own, queries, d_out):
    tok = own.shape[0]
    heads = queries.shape[1] // LATENT
    steps = heads // (2 * PAIRS)
    sub = token_part(tok)
    parts = tok // sub
    unit = 2 * PAIRS * sub
    group = 2 if steps % 2 == 0 else 1
    bf16, f32 = jnp.bfloat16, jnp.float32
    return pl.pallas_call(
        own_kernel,
        grid=(steps // group,),
        in_specs=[
            pl.BlockSpec(own.shape, lambda i: (0, 0)),
            pl.BlockSpec((sub, group * 2 * PAIRS * LATENT), lambda i: (parts - 1, i)),
            pl.BlockSpec((sub, group * 2 * PAIRS * RANK), lambda i: (parts - 1, i)),
        ],
        out_specs=[pl.BlockSpec((group, tok, unit), lambda i: (i, 0, 0))] * 2,
        out_shape=[
            jax.ShapeDtypeStruct((steps, tok, unit), f32),
            jax.ShapeDtypeStruct((steps, tok, unit), bf16),
        ],
        scratch_shapes=[
            pltpu.VMEM((tok, WIDTH), bf16),
            pltpu.VMEM((sub, unit), f32),
            pltpu.VMEM((group * unit, WIDTH), bf16),
            pltpu.VMEM((group * unit, RANK), bf16),
        ],
        compiler_params=pltpu.CompilerParams(vmem_limit_bytes=60 * MIB),
        cost_estimate=pl.CostEstimate(
            flops=2 * sub * heads * tok * (LATENT + RANK),
            bytes_accessed=2 * sub * heads * (LATENT + RANK + 3 * tok),
            transcendentals=0,
        ),
        name="own_scores",
    )(own, queries, d_out)


def attn_kernel(
    owned, head_parts, ahead, anc_count, ancestors, incoming, own, s_own, dp_own, q, do,
    dq, ds, keys_e, keys_o, sent, *rest
):
    own_parts = rest[:head_parts]
    far_bias, causal, q_st, s, dp, p_low, tops, acc_k, acc_v = rest[head_parts:]
    tok = q.shape[0]
    far_rows, rows = ANC * BLK, ANC * BLK + tok
    sub = token_part(tok)
    parts = tok // sub
    stack = 2 * PAIRS * sub
    least = LEAST_LIVE * BLK
    step = pl.program_id(0)

    @pl.when(step == 0)
    def _():
        row, owner, second = slot_places(ancestors, owned)
        sel = one_hot((owner * CAP + second) * BLK + mod(row, BLK), incoming.shape[0])
        far = mm(sel, incoming[...], NN)
        joined = jnp.concatenate([far, own[...].astype(jnp.float32)], axis=0)
        padded = jnp.concatenate([joined, jnp.zeros((rows, HALF), jnp.float32)], axis=1)
        keys_e[...] = padded.astype(jnp.bfloat16)
        keys_o[...] = pltpu.roll(padded, HALF, axis=1).astype(jnp.bfloat16)
        live = anc_count[lax.axis_index("leaf")]
        slot = div(lax.broadcasted_iota(jnp.int32, far_bias.shape, 0) + least, BLK)
        far_bias[...] = jnp.where(slot < live, 0.0, MASKED)
        causal[...] = causal_bias(causal.shape, sub)
        acc_k[...] = jnp.zeros_like(acc_k)
        acc_v[...] = jnp.zeros_like(acc_v)

    def seen(j):
        return far_rows + (j + 1) * sub

    def lanes(j):
        return pl.ds(j * stack, stack)

    def fill(j):
        toks = pl.ds(j * sub, sub)
        for i in range(PAIRS):
            at = i * 2 * LATENT
            q_st[pl.ds(j * stack + i * sub, sub), :] = q[toks, at:at + WIDTH]
            odd = q[toks, at + LATENT - HALF:at + 2 * LATENT]
            odd = pltpu.roll(odd, WIDTH - HALF, axis=1)
            q_st[pl.ds(j * stack + (PAIRS + i) * sub, sub), :] = odd

    heads = list(range(0, 2 * PAIRS, 2)) + list(range(1, 2 * PAIRS, 2))

    def grads(j, first, count, at=0, size=RANK):
        toks = pl.ds(j * sub, sub)
        cols = [pl.ds(h * RANK + at, size) for h in heads[first:first + count]]
        return jnp.concatenate([do[toks, c] for c in cols], axis=0)

    def fold(x):
        return x.reshape(-1, 8, x.shape[1])

    def given(j):
        return j == parts - 1

    def score(j, at):
        n, cols = seen(j), pl.ds(j * stack + at, stack // 2)
        out = mm(keys_e[:far_rows if given(j) else n, :], q_st[cols, :].T, NN)
        near = [(0, out[:least]), (least, out[least:far_rows] + far_bias[...])]
        top = None
        if given(j):
            top = jnp.max(fold(s_own[0, :, pl.ds(at, stack // 2)]), axis=0)
        else:
            if j > 0:
                near.append((far_rows, out[far_rows:n - sub]))
            near.append((n - sub, out[n - sub:] + causal[...]))
        for r, part in near:
            s[pl.ds(r, part.shape[0]), cols] = part
            part = jnp.max(fold(part), axis=0)
            top = part if top is None else jnp.maximum(top, part)
        tops[:, cols] = top

    def prob(j, at):
        n, cols = far_rows if given(j) else seen(j), pl.ds(j * stack + at, stack // 2)
        dp[:n, cols] = mm(keys_e[:n, :RANK], grads(j, at // sub, PAIRS).T, NN)

    state = {}

    def scores_at(j, r, n, at):
        if given(j) and r >= far_rows:
            return s_own[0, pl.ds(r - far_rows, n), pl.ds(at, LANES)]
        return s[pl.ds(r, n), pl.ds(j * stack + at, LANES)]

    def probs_at(j, r, n, at):
        if given(j) and r >= far_rows:
            return dp_own[0, pl.ds(r - far_rows, n), pl.ds(at, LANES)].astype(jnp.float32)
        return dp[pl.ds(r, n), pl.ds(j * stack + at, LANES)]

    def soft_sums(j, at):
        lane = pl.ds(j * stack + at, LANES)
        top = jnp.max(tops[:, lane], axis=0, keepdims=True)
        total = jnp.zeros((8, LANES), jnp.float32)
        delta = jnp.zeros((8, LANES), jnp.float32)
        for r, n in pieces(seen(j), 64):
            e = jnp.exp2((scores_at(j, r, n, at) - top) * EXP_SCALE)
            s[pl.ds(r, n), lane] = e
            total += jnp.sum(fold(e), axis=0)
            delta += jnp.sum(fold(e * probs_at(j, r, n, at)), axis=0)
        inv = 1.0 / jnp.sum(total, axis=0, keepdims=True)
        state[j, at] = inv, jnp.sum(delta, axis=0, keepdims=True) * inv

    def soft_outs(j, at):
        lane = pl.ds(j * stack + at, LANES)
        inv, delta = state.pop((j, at))
        for r, n in pieces(seen(j), 64):
            p = s[pl.ds(r, n), lane] * inv
            p_low[pl.ds(r, n), lane] = p.astype(jnp.bfloat16)
            ds[0, pl.ds(r, n), lane] = (p * (probs_at(j, r, n, at) - delta)).astype(ds.dtype)

    def grad_values(j, at, size):
        n, cols = seen(j), pl.ds(at, size)
        acc_v[:n, cols] += mm(p_low[:n, lanes(j)], grads(j, 0, 2 * PAIRS, at, size), NN)

    def grad_keys(j, at, size):
        n, cols = seen(j), pl.ds(at, size)
        acc_k[:n, cols] += mm(ds[0, :n, lanes(j)], q_st[lanes(j), cols], NN)

    def jobs_of(i):
        products, passes = [], []
        if i < parts:
            products += [functools.partial(fill, i)]
            for at in (0, stack // 2):
                products += [functools.partial(score, i, at), functools.partial(prob, i, at)]
        if 0 <= i - 2 < parts:
            products += [functools.partial(grad_values, i - 2, *c) for c in pieces(RANK, 256)]
            products += [functools.partial(grad_keys, i - 2, *c) for c in pieces(WIDTH, 256)]
        if 0 <= i - 1 < parts:
            for at in range(0, stack, LANES):
                passes += [functools.partial(job, i - 1, at) for job in (soft_sums, soft_outs)]
        order = [
            (k / len(group), g, job)
            for g, group in enumerate((products, passes)) for k, job in enumerate(group)
        ]
        return [job for _, _, job in sorted(order, key=lambda item: item[:2])]

    for i in range(parts + 2):
        for job in jobs_of(i):
            job()

    @pl.when(step < ahead)
    def _():
        put_queries(dq, ds, keys_e, keys_o)

    @pl.when(step == pl.num_programs(0) - 1)
    def _():
        acc_k[...] = acc_k[...] * SCALE
        acc_k[:, :RANK] += acc_v[...]
        part_rows = BLK // head_parts
        row, owner, second = slot_places(ancestors, owned)
        inner = mod(row, BLK)
        place = (owner * head_parts + div(inner, part_rows)) * CAP + second
        place = place * part_rows + mod(inner, part_rows)
        sel = one_hot(place, sent.shape[0])
        far = acc_k[:far_rows, :LATENT].astype(jnp.bfloat16)
        sent[...] = mm(sel, far, TN).astype(sent.dtype)
        own_rows = tok // head_parts
        for hop, out in enumerate(own_parts):
            part = lax.rem(lax.axis_index("head") + hop, head_parts)
            at = pl.multiple_of(far_rows + part * own_rows, 8)
            out[...] = acc_k[pl.ds(at, own_rows), :LATENT]


def steps_ahead(steps):
    return steps * 3 // 8


def attention(
    owned, head_parts, anc_count, ancestors, incoming, own, s_own, dp_own, queries, d_out
):
    tok = queries.shape[0]
    heads = queries.shape[1] // LATENT
    steps = heads // (2 * PAIRS)
    ahead = steps_ahead(steps)
    far_rows, rows = ANC * BLK, ANC * BLK + tok
    toks = 2 * PAIRS * tok
    stack = 2 * PAIRS * token_part(tok)
    bf16, f32 = jnp.bfloat16, jnp.float32

    def whole(i):
        return (0, 0)

    def along(i):
        return (0, i)

    own_part = (tok // head_parts, LATENT)
    return pl.pallas_call(
        functools.partial(attn_kernel, owned, head_parts, ahead),
        grid=(steps,),
        in_specs=[
            pl.BlockSpec(memory_space=pltpu.SMEM),
            pl.BlockSpec(ancestors.shape, whole),
            pl.BlockSpec(incoming.shape, whole),
            pl.BlockSpec(own.shape, whole),
            pl.BlockSpec((1,) + s_own.shape[1:], lambda i: (i, 0, 0)),
            pl.BlockSpec((1,) + dp_own.shape[1:], lambda i: (i, 0, 0)),
            pl.BlockSpec((tok, 2 * PAIRS * LATENT), along),
            pl.BlockSpec((tok, 2 * PAIRS * RANK), along),
        ],
        out_specs=[
            pl.BlockSpec(
                (tok, 2 * PAIRS * LATENT), lambda i: (0, jnp.minimum(i, max(ahead - 1, 0)))
            ),
            pl.BlockSpec((1, rows, toks), lambda i: (jnp.maximum(i - ahead, 0), 0, 0)),
            pl.BlockSpec((rows, WIDTH), whole),
            pl.BlockSpec((rows, WIDTH), whole),
            pl.BlockSpec(incoming.shape, whole),
        ] + [pl.BlockSpec(own_part, whole)] * head_parts,
        out_shape=[
            jax.ShapeDtypeStruct(queries.shape, bf16),
            jax.ShapeDtypeStruct((steps - ahead, rows, toks), bf16),
            jax.ShapeDtypeStruct((rows, WIDTH), bf16),
            jax.ShapeDtypeStruct((rows, WIDTH), bf16),
            jax.ShapeDtypeStruct(incoming.shape, bf16),
        ] + [jax.ShapeDtypeStruct(own_part, f32)] * head_parts,
        scratch_shapes=[
            pltpu.VMEM((far_rows - LEAST_LIVE * BLK, stack // 2), f32),
            pltpu.VMEM((token_part(tok), stack // 2), f32),
            pltpu.VMEM((toks, WIDTH), bf16),
            pltpu.VMEM((rows, toks), f32),
            pltpu.VMEM((rows, toks), f32),
            pltpu.VMEM((rows, toks), bf16),
            pltpu.VMEM((8, toks), f32),
            pltpu.VMEM((rows, WIDTH), f32),
            pltpu.VMEM((rows, RANK), f32),
        ],
        compiler_params=pltpu.CompilerParams(vmem_limit_bytes=60 * MIB),
        cost_estimate=pl.CostEstimate(
            flops=2 * tok * heads * rows * (2 * LATENT + 2 * RANK),
            bytes_accessed=2 * tok * heads * (LATENT + RANK + rows),
            transcendentals=tok * heads * rows,
        ),
        name="score_gradients",
    )(anc_count, ancestors, incoming, own, s_own, dp_own, queries, d_out)


def put_queries(dq, ds, keys_e, keys_o):
    tok = dq.shape[0]
    rows = ds.shape[1]
    sub = token_part(tok)
    stack = PAIRS * sub
    low = LATENT - HALF
    for j in range(tok // sub):
        n = rows - tok + (j + 1) * sub
        even = mm(ds[0, :n, pl.ds(2 * j * stack, stack)], keys_e[:n, :], TN) * SCALE
        odd = mm(ds[0, :n, pl.ds((2 * j + 1) * stack, stack)], keys_o[:n, :], TN) * SCALE
        for i in range(PAIRS):
            at = i * 2 * LATENT
            part = slice(i * sub, (i + 1) * sub)
            toks = pl.ds(j * sub, sub)
            dq[toks, at:at + low] = even[part, :low].astype(dq.dtype)
            joint = even[part, low:] + odd[part, :2 * HALF]
            dq[toks, at + low:at + low + 2 * HALF] = joint.astype(dq.dtype)
            dq[toks, at + low + 2 * HALF:at + 2 * LATENT] = odd[part, 2 * HALF:].astype(dq.dtype)


def query_kernel(keys_e, keys_o, ds, started, dq):
    put_queries(dq, ds, keys_e, keys_o)


def query_gradients(keys_e, keys_o, ds, started):
    tok = started.shape[0]
    steps = ds.shape[0]
    ahead = started.shape[1] // (2 * PAIRS * LATENT) - steps
    rows = ds.shape[1]
    return pl.pallas_call(
        query_kernel,
        grid=(steps,),
        in_specs=[
            pl.BlockSpec(keys_e.shape, lambda i: (0, 0)),
            pl.BlockSpec(keys_o.shape, lambda i: (0, 0)),
            pl.BlockSpec((1,) + ds.shape[1:], lambda i: (i, 0, 0)),
            pl.BlockSpec(memory_space=pl.ANY),
        ],
        out_specs=pl.BlockSpec((tok, 2 * PAIRS * LATENT), lambda i: (0, i + ahead)),
        out_shape=jax.ShapeDtypeStruct(started.shape, started.dtype),
        input_output_aliases={3: 0},
        compiler_params=pltpu.CompilerParams(vmem_limit_bytes=60 * MIB),
        cost_estimate=pl.CostEstimate(
            flops=4 * tok * steps * PAIRS * rows * LATENT,
            bytes_accessed=4 * tok * steps * PAIRS * (LATENT + rows),
            transcendentals=0,
        ),
        name="query_gradients",
    )(keys_e, keys_o, ds, started)


def local(queries, d_out, branch_latent, trunk_latent, ancestors, anc_count):
    leafs = lax.axis_size("leaf")
    head_parts = lax.axis_size("head")
    owned = trunk_latent.shape[0]
    part_rows = BLK // head_parts

    outgoing = pick(head_parts, ancestors, trunk_latent.reshape(owned * BLK, LATENT))
    incoming = lax.all_to_all(
        outgoing.reshape(leafs * head_parts, CAP * part_rows, LATENT),
        ("leaf", "head"), split_axis=0, concat_axis=0, tiled=True,
    ).reshape(leafs * CAP * BLK, LATENT)

    s_own, dp_own = own_scores(branch_latent, queries, d_out)

    started, ds, keys_e, keys_o, sent, mine, *others = attention(
        owned, head_parts, anc_count, ancestors, incoming, branch_latent, s_own, dp_own,
        queries, d_out,
    )

    got = lax.all_to_all(
        sent.reshape(leafs * head_parts, CAP * part_rows, LATENT),
        ("leaf", "head"), split_axis=0, concat_axis=0, tiled=True,
    ).reshape(leafs * CAP * BLK, LATENT)
    theirs = []
    for hop, part in enumerate(others, 1):
        route = [(i, (i + hop) % head_parts) for i in range(head_parts)]
        theirs.append(lax.ppermute(part, "head", route))

    d_queries = query_gradients(keys_e, keys_o, ds, started)
    d_branch, d_trunk = finish(ancestors, got, mine, theirs, owned, part_rows)
    return d_queries, d_branch, d_trunk


def solution(mesh):
    return jax.shard_map(
        local,
        mesh=mesh,
        in_specs=(
            P("leaf", "head"),
            P("leaf", "head"),
            P("leaf", None),
            P("leaf", None, None),
            P(),
            P(),
        ),
        out_specs=(P("leaf", "head"), P(("leaf", "head"), None), P("leaf", "head", None)),
        check_vma=False,
    )
```

```python
import functools
import math

import jax
import jax.numpy as jnp
from jax import lax
from jax.experimental import pallas as pl
from jax.experimental.pallas import tpu as pltpu
from jax.sharding import PartitionSpec as P

RANK = 512
QK_HEAD = 192
LATENT = 576
BLK = 8
CAP = 2
ANC = 32
LEAST_LIVE = 24
LANES = 128
WIDTH = 640
HALF = WIDTH - LATENT
PAIRS = 4
MASKED = -1e30
FAR_OFF = 1 << 20
SCALE = float(QK_HEAD) ** -0.5
EXP_SCALE = SCALE * math.log2(math.e)
MIB = 1024 * 1024
NT = (((1,), (1,)), ((), ()))
NN = (((1,), (0,)), ((), ()))
TN = (((0,), (0,)), ((), ()))


def mm(a, b, dims):
    return lax.dot_general(a, b, dims, preferred_element_type=jnp.float32)


def pieces(total, size):
    return [(at, min(size, total - at)) for at in range(0, total, size)]


def div(x, n):
    return x >> (n.bit_length() - 1) if n & (n - 1) == 0 else lax.div(x, jnp.full_like(x, n))


def mod(x, n):
    return x - div(x, n) * n


def column(rows):
    return lax.broadcasted_iota(jnp.int32, (rows, 1), 0)


def one_hot(place, size):
    lane = lax.broadcasted_iota(jnp.int32, (place.shape[0], size), 1)
    return jnp.where(lane == place, 1.0, 0.0).astype(jnp.bfloat16)


def seen_rows(rows, tok):
    sub = token_part(tok)
    seen = [rows - tok + (j + 1) * sub for j in range(tok // sub)]
    return seen, [sum(seen[:j]) for j in range(len(seen) + 1)]


def token_part(tok):
    return 64 if tok % 64 == 0 else tok


def listed_blocks(ancestors, owned, second):
    leafs = ancestors.shape[0]
    rows = leafs * CAP * BLK
    named = ancestors[...].astype(jnp.float32)
    named = jnp.broadcast_to(named[:, None, :], (leafs, CAP * BLK, ANC)).reshape(rows, ANC)
    first = lax.axis_index("leaf") * owned
    low_end = first.astype(jnp.float32)
    mine = (named >= low_end) & (named < low_end + owned)
    low = jnp.min(jnp.where(mine, named, float(FAR_OFF)), axis=1, keepdims=True)
    high = jnp.max(jnp.where(mine, named, -1.0), axis=1, keepdims=True)
    return jnp.where(second, high, low).astype(jnp.int32) - first


def pick_kernel(ancestors, trunk, out):
    owned = trunk.shape[0] // BLK
    row = column(out.shape[0])
    block = listed_blocks(ancestors, owned, mod(div(row, BLK), CAP) == 1)
    sel = one_hot(block * BLK + mod(row, BLK), trunk.shape[0])
    out[...] = mm(sel, trunk[...], NN).astype(out.dtype)


def pick(ancestors, trunk):
    rows = ancestors.shape[0] * CAP * BLK
    return pl.pallas_call(
        pick_kernel,
        out_shape=jax.ShapeDtypeStruct((rows, LATENT), trunk.dtype),
        compiler_params=pltpu.CompilerParams(vmem_limit_bytes=8 * MIB),
        name="pick_blocks",
    )(ancestors, trunk)


def finish_kernel(ancestors, got, mine, *rest):
    theirs, (d_branch, d_trunk) = rest[:-2], rest[-2:]
    owned, part_rows = d_trunk.shape[0], d_trunk.shape[1]
    row = column(got.shape[0])
    block = listed_blocks(ancestors, owned, mod(div(row, part_rows), CAP) == 1)
    sel = one_hot(block * part_rows + mod(row, part_rows), owned * part_rows)
    total = mm(sel, got[...], TN)
    for b in range(owned):
        d_trunk[b] = total[b * part_rows:(b + 1) * part_rows]
    own = mine[...]
    for other in theirs:
        own = own + other[...]
    d_branch[...] = own


def finish(ancestors, got, mine, theirs, owned, part_rows):
    return pl.pallas_call(
        finish_kernel,
        out_shape=[
            jax.ShapeDtypeStruct(mine.shape, jnp.float32),
            jax.ShapeDtypeStruct((owned, part_rows, LATENT), jnp.float32),
        ],
        compiler_params=pltpu.CompilerParams(vmem_limit_bytes=8 * MIB),
        name="sum_gradients",
    )(ancestors, got, mine, *theirs)


def slot_places(ancestors, owned):
    row = column(ANC * BLK)
    mine = ancestors[pl.ds(lax.axis_index("leaf"), 1), :].astype(jnp.float32)
    mine = jnp.broadcast_to(mine, (ANC * BLK, ANC))
    lane = lax.broadcasted_iota(jnp.int32, (ANC * BLK, ANC), 1)
    block = jnp.max(jnp.where(lane == div(row, BLK), mine, -1.0), axis=1, keepdims=True)
    owner = div(block.astype(jnp.int32), owned)
    low_end = (owner * owned).astype(jnp.float32)
    below = (mine >= low_end) & (mine < block)
    second = jnp.max(jnp.where(below, 1.0, 0.0), axis=1, keepdims=True).astype(jnp.int32)
    return row, owner, second


def stack_heads(q, do, q_st, do_st, toks, to, heads):
    sub = toks.size
    pairs = heads // 2
    for i in range(pairs):
        at = i * 2 * LATENT
        even, odd = pl.ds(to + i * sub, sub), pl.ds(to + (pairs + i) * sub, sub)
        q_st[even, :] = q[toks, at:at + WIDTH]
        moved = q[toks, at + LATENT - HALF:at + 2 * LATENT]
        q_st[odd, :] = pltpu.roll(moved, WIDTH - HALF, axis=1)
        do_st[even, :] = do[toks, pl.ds(2 * i * RANK, RANK)]
        do_st[odd, :] = do[toks, pl.ds((2 * i + 1) * RANK, RANK)]


def causal_bias(shape, sub):
    key_at = lax.broadcasted_iota(jnp.int32, shape, 0)
    tok_at = mod(lax.broadcasted_iota(jnp.int32, shape, 1), sub)
    return jnp.where(key_at <= tok_at, 0.0, MASKED)


def own_kernel(own, q, do, s_own, dp_own, keys, causal, q_st, do_st):
    tok = own.shape[0]
    sub = q.shape[0]
    heads = 2 * PAIRS

    @pl.when(pl.program_id(0) == 0)
    def _():
        pad = jnp.zeros((tok, HALF), jnp.float32)
        padded = jnp.concatenate([own[...].astype(jnp.float32), pad], axis=1)
        keys[...] = padded.astype(jnp.bfloat16)
        causal[...] = causal_bias(causal.shape, sub)

    for group in range(s_own.shape[0]):
        cols = pl.ds(group * heads * LATENT, heads * LATENT)
        grad_cols = pl.ds(group * heads * RANK, heads * RANK)
        base = group * heads * sub
        block = pl.ds(base, heads * sub)
        stack_heads(
            q.at[:, cols], do.at[:, grad_cols], q_st, do_st, pl.ds(0, sub), base, heads
        )
        out = mm(keys[...], q_st[block, :], NT)
        s_own[group, :tok - sub] = out[:tok - sub]
        s_own[group, tok - sub:] = out[tok - sub:] + causal[...]
        dp_own[group] = mm(keys[:, :RANK], do_st[block, :], NT).astype(dp_own.dtype)


def own_scores(own, queries, d_out):
    tok = own.shape[0]
    heads = queries.shape[1] // LATENT
    steps = heads // (2 * PAIRS)
    sub = token_part(tok)
    parts = tok // sub
    unit = 2 * PAIRS * sub
    group = 2 if steps % 2 == 0 else 1
    bf16, f32 = jnp.bfloat16, jnp.float32
    return pl.pallas_call(
        own_kernel,
        grid=(steps // group,),
        in_specs=[
            pl.BlockSpec(own.shape, lambda i: (0, 0)),
            pl.BlockSpec((sub, group * 2 * PAIRS * LATENT), lambda i: (parts - 1, i)),
            pl.BlockSpec((sub, group * 2 * PAIRS * RANK), lambda i: (parts - 1, i)),
        ],
        out_specs=[pl.BlockSpec((group, tok, unit), lambda i: (i, 0, 0))] * 2,
        out_shape=[
            jax.ShapeDtypeStruct((steps, tok, unit), f32),
            jax.ShapeDtypeStruct((steps, tok, unit), bf16),
        ],
        scratch_shapes=[
            pltpu.VMEM((tok, WIDTH), bf16),
            pltpu.VMEM((sub, unit), f32),
            pltpu.VMEM((group * unit, WIDTH), bf16),
            pltpu.VMEM((group * unit, RANK), bf16),
        ],
        compiler_params=pltpu.CompilerParams(vmem_limit_bytes=60 * MIB),
        cost_estimate=pl.CostEstimate(
            flops=2 * sub * heads * tok * (LATENT + RANK),
            bytes_accessed=2 * sub * heads * (LATENT + RANK + 3 * tok),
            transcendentals=0,
        ),
        name="own_scores",
    )(own, queries, d_out)


def attn_kernel(
    owned, head_parts, ahead, anc_count, ancestors, incoming, own, s_own, dp_own, q, do,
    dq, ds, keys_out_e, keys_out_o, sent, *rest
):
    own_parts = rest[:head_parts]
    scratch = rest[head_parts:]
    k_e, k_o, sems, far_bias, causal, q_st, s, dp, p_low, tops, acc_k, acc_v = scratch
    tok = q.shape[0]
    far_rows, rows = ANC * BLK, ANC * BLK + tok
    sub = token_part(tok)
    parts = tok // sub
    stack = 2 * PAIRS * sub
    least = LEAST_LIVE * BLK
    step = pl.program_id(0)
    key_copies = [
        pltpu.make_async_copy(k_e, keys_out_e, sems.at[0]),
        pltpu.make_async_copy(k_o, keys_out_o, sems.at[1]),
    ]

    @pl.when(step == 0)
    def _():
        row, owner, second = slot_places(ancestors, owned)
        sel = one_hot((owner * CAP + second) * BLK + mod(row, BLK), incoming.shape[0])
        far = mm(sel, incoming[...], NN)
        joined = jnp.concatenate([far, own[...].astype(jnp.float32)], axis=0)
        padded = jnp.concatenate([joined, jnp.zeros((rows, HALF), jnp.float32)], axis=1)
        k_e[...] = padded.astype(jnp.bfloat16)
        k_o[...] = pltpu.roll(padded, HALF, axis=1).astype(jnp.bfloat16)
        for copy in key_copies:
            copy.start()
        live = anc_count[lax.axis_index("leaf")]
        slot = div(lax.broadcasted_iota(jnp.int32, far_bias.shape, 0) + least, BLK)
        far_bias[...] = jnp.where(slot < live, 0.0, MASKED)
        causal[...] = causal_bias(causal.shape, sub)
        acc_k[...] = jnp.zeros_like(acc_k)
        acc_v[...] = jnp.zeros_like(acc_v)

    seen_of, starts = seen_rows(rows, tok)

    def seen(j):
        return seen_of[j]

    def lanes(j):
        return pl.ds(j * stack, stack)

    def fill(j):
        toks = pl.ds(j * sub, sub)
        for i in range(PAIRS):
            at = i * 2 * LATENT
            q_st[pl.ds(j * stack + i * sub, sub), :] = q[toks, at:at + WIDTH]
            odd = q[toks, at + LATENT - HALF:at + 2 * LATENT]
            odd = pltpu.roll(odd, WIDTH - HALF, axis=1)
            q_st[pl.ds(j * stack + (PAIRS + i) * sub, sub), :] = odd

    heads = list(range(0, 2 * PAIRS, 2)) + list(range(1, 2 * PAIRS, 2))

    def grads(j, first, count, at=0, size=RANK):
        toks = pl.ds(j * sub, sub)
        cols = [pl.ds(h * RANK + at, size) for h in heads[first:first + count]]
        return jnp.concatenate([do[toks, c] for c in cols], axis=0)

    def fold(x):
        return x.reshape(-1, 8, x.shape[1])

    def given(j):
        return j == parts - 1

    def score(j, at):
        n, cols = seen(j), pl.ds(j * stack + at, stack // 2)
        out = mm(k_e[:far_rows if given(j) else n, :], q_st[cols, :].T, NN)
        near = [(0, out[:least]), (least, out[least:far_rows] + far_bias[...])]
        top = None
        if given(j):
            top = jnp.max(fold(s_own[0, :, pl.ds(at, stack // 2)]), axis=0)
        else:
            if j > 0:
                near.append((far_rows, out[far_rows:n - sub]))
            near.append((n - sub, out[n - sub:] + causal[...]))
        for r, part in near:
            s[pl.ds(r, part.shape[0]), cols] = part
            part = jnp.max(fold(part), axis=0)
            top = part if top is None else jnp.maximum(top, part)
        tops[:, cols] = top

    def prob(j, at):
        n, cols = far_rows if given(j) else seen(j), pl.ds(j * stack + at, stack // 2)
        dp[:n, cols] = mm(k_e[:n, :RANK], grads(j, at // sub, PAIRS).T, NN)

    state = {}

    def scores_at(j, r, n, at):
        if given(j) and r >= far_rows:
            return s_own[0, pl.ds(r - far_rows, n), pl.ds(at, LANES)]
        return s[pl.ds(r, n), pl.ds(j * stack + at, LANES)]

    def probs_at(j, r, n, at):
        if given(j) and r >= far_rows:
            return dp_own[0, pl.ds(r - far_rows, n), pl.ds(at, LANES)].astype(jnp.float32)
        return dp[pl.ds(r, n), pl.ds(j * stack + at, LANES)]

    def soft_sums(j, at):
        lane = pl.ds(j * stack + at, LANES)
        top = jnp.max(tops[:, lane], axis=0, keepdims=True)
        total = jnp.zeros((8, LANES), jnp.float32)
        delta = jnp.zeros((8, LANES), jnp.float32)
        for r, n in pieces(seen(j), 64):
            e = jnp.exp2((scores_at(j, r, n, at) - top) * EXP_SCALE)
            s[pl.ds(r, n), lane] = e
            total += jnp.sum(fold(e), axis=0)
            delta += jnp.sum(fold(e * probs_at(j, r, n, at)), axis=0)
        inv = 1.0 / jnp.sum(total, axis=0, keepdims=True)
        state[j, at] = inv, jnp.sum(delta, axis=0, keepdims=True) * inv

    def soft_outs(j, at):
        lane = pl.ds(j * stack + at, LANES)
        inv, delta = state.pop((j, at))
        for r, n in pieces(seen(j), 64):
            p = s[pl.ds(r, n), lane] * inv
            p_low[pl.ds(r, n), lane] = p.astype(jnp.bfloat16)
            ds[0, pl.ds(starts[j] + r, n), pl.ds(at, LANES)] = (p * (probs_at(j, r, n, at) - delta)).astype(ds.dtype)

    def grad_values(j, at, size):
        n, cols = seen(j), pl.ds(at, size)
        acc_v[:n, cols] += mm(p_low[:n, lanes(j)], grads(j, 0, 2 * PAIRS, at, size), NN)

    def grad_keys(j, at, size):
        n, cols = seen(j), pl.ds(at, size)
        acc_k[:n, cols] += mm(ds[0, pl.ds(starts[j], n), :], q_st[lanes(j), cols], NN)

    def jobs_of(i):
        products, passes = [], []
        if i < parts:
            products += [functools.partial(fill, i)]
            for at in (0, stack // 2):
                products += [functools.partial(score, i, at), functools.partial(prob, i, at)]
        if 0 <= i - 2 < parts:
            products += [functools.partial(grad_values, i - 2, *c) for c in pieces(RANK, 256)]
            products += [functools.partial(grad_keys, i - 2, *c) for c in pieces(WIDTH, 256)]
        if 0 <= i - 1 < parts:
            for at in range(0, stack, LANES):
                passes += [functools.partial(job, i - 1, at) for job in (soft_sums, soft_outs)]
        order = [
            (k / len(group), g, job)
            for g, group in enumerate((products, passes)) for k, job in enumerate(group)
        ]
        return [job for _, _, job in sorted(order, key=lambda item: item[:2])]

    for i in range(parts + 2):
        for job in jobs_of(i):
            job()

    @pl.when(step < ahead)
    def _():
        put_queries(dq, ds, k_e, k_o)

    @pl.when(step == pl.num_programs(0) - 1)
    def _():
        acc_k[...] = acc_k[...] * SCALE
        acc_k[:, :RANK] += acc_v[...]
        part_rows = BLK // head_parts
        row, owner, second = slot_places(ancestors, owned)
        inner = mod(row, BLK)
        place = (owner * head_parts + div(inner, part_rows)) * CAP + second
        place = place * part_rows + mod(inner, part_rows)
        sel = one_hot(place, sent.shape[0])
        far = acc_k[:far_rows, :LATENT].astype(jnp.bfloat16)
        sent[...] = mm(sel, far, TN).astype(sent.dtype)
        own_rows = tok // head_parts
        for hop, out in enumerate(own_parts):
            part = lax.rem(lax.axis_index("head") + hop, head_parts)
            at = pl.multiple_of(far_rows + part * own_rows, 8)
            out[...] = acc_k[pl.ds(at, own_rows), :LATENT]
        for copy in key_copies:
            copy.wait()


def steps_ahead(steps):
    return steps * 3 // 8


def attention(
    owned, head_parts, anc_count, ancestors, incoming, own, s_own, dp_own, queries, d_out
):
    tok = queries.shape[0]
    heads = queries.shape[1] // LATENT
    steps = heads // (2 * PAIRS)
    ahead = steps_ahead(steps)
    far_rows, rows = ANC * BLK, ANC * BLK + tok
    toks = 2 * PAIRS * tok
    stack = 2 * PAIRS * token_part(tok)
    ds_rows = seen_rows(rows, tok)[1][-1]
    bf16, f32 = jnp.bfloat16, jnp.float32

    def whole(i):
        return (0, 0)

    def along(i):
        return (0, i)

    own_part = (tok // head_parts, LATENT)
    return pl.pallas_call(
        functools.partial(attn_kernel, owned, head_parts, ahead),
        grid=(steps,),
        in_specs=[
            pl.BlockSpec(memory_space=pltpu.SMEM),
            pl.BlockSpec(ancestors.shape, whole),
            pl.BlockSpec(incoming.shape, whole),
            pl.BlockSpec(own.shape, whole),
            pl.BlockSpec((1,) + s_own.shape[1:], lambda i: (i, 0, 0)),
            pl.BlockSpec((1,) + dp_own.shape[1:], lambda i: (i, 0, 0)),
            pl.BlockSpec((tok, 2 * PAIRS * LATENT), along),
            pl.BlockSpec((tok, 2 * PAIRS * RANK), along),
        ],
        out_specs=[
            pl.BlockSpec(
                (tok, 2 * PAIRS * LATENT), lambda i: (0, jnp.minimum(i, max(ahead - 1, 0)))
            ),
            pl.BlockSpec((1, ds_rows, stack), lambda i: (jnp.maximum(i - ahead, 0), 0, 0)),
            pl.BlockSpec(memory_space=pl.ANY),
            pl.BlockSpec(memory_space=pl.ANY),
            pl.BlockSpec(incoming.shape, whole),
        ] + [pl.BlockSpec(own_part, whole)] * head_parts,
        out_shape=[
            jax.ShapeDtypeStruct(queries.shape, bf16),
            jax.ShapeDtypeStruct((steps - ahead, ds_rows, stack), bf16),
            jax.ShapeDtypeStruct((rows, WIDTH), bf16),
            jax.ShapeDtypeStruct((rows, WIDTH), bf16),
            jax.ShapeDtypeStruct(incoming.shape, bf16),
        ] + [jax.ShapeDtypeStruct(own_part, f32)] * head_parts,
        scratch_shapes=[
            pltpu.VMEM((rows, WIDTH), bf16),
            pltpu.VMEM((rows, WIDTH), bf16),
            pltpu.SemaphoreType.DMA((2,)),
            pltpu.VMEM((far_rows - LEAST_LIVE * BLK, stack // 2), f32),
            pltpu.VMEM((token_part(tok), stack // 2), f32),
            pltpu.VMEM((toks, WIDTH), bf16),
            pltpu.VMEM((rows, toks), f32),
            pltpu.VMEM((rows, toks), f32),
            pltpu.VMEM((rows, toks), bf16),
            pltpu.VMEM((8, toks), f32),
            pltpu.VMEM((rows, WIDTH), f32),
            pltpu.VMEM((rows, RANK), f32),
        ],
        compiler_params=pltpu.CompilerParams(vmem_limit_bytes=60 * MIB),
        cost_estimate=pl.CostEstimate(
            flops=2 * tok * heads * rows * (2 * LATENT + 2 * RANK),
            bytes_accessed=2 * tok * heads * (LATENT + RANK + rows),
            transcendentals=tok * heads * rows,
        ),
        name="score_gradients",
    )(anc_count, ancestors, incoming, own, s_own, dp_own, queries, d_out)


def put_queries(dq, ds, keys_e, keys_o):
    tok = dq.shape[0]
    sub = token_part(tok)
    stack = PAIRS * sub
    low = LATENT - HALF
    seen, starts = seen_rows(keys_e.shape[0], tok)
    for j, n in enumerate(seen):
        block = pl.ds(starts[j], n)
        even = mm(ds[0, block, :stack], keys_e[:n, :], TN) * SCALE
        odd = mm(ds[0, block, stack:], keys_o[:n, :], TN) * SCALE
        for i in range(PAIRS):
            at = i * 2 * LATENT
            part = slice(i * sub, (i + 1) * sub)
            toks = pl.ds(j * sub, sub)
            dq[toks, at:at + low] = even[part, :low].astype(dq.dtype)
            joint = even[part, low:] + odd[part, :2 * HALF]
            dq[toks, at + low:at + low + 2 * HALF] = joint.astype(dq.dtype)
            dq[toks, at + low + 2 * HALF:at + 2 * LATENT] = odd[part, 2 * HALF:].astype(dq.dtype)


def query_kernel(keys_e, keys_o, ds, started, dq):
    put_queries(dq, ds, keys_e, keys_o)


def query_gradients(keys_e, keys_o, ds, started):
    tok = started.shape[0]
    steps, rows = ds.shape[0], keys_e.shape[0]
    ahead = started.shape[1] // (2 * PAIRS * LATENT) - steps
    return pl.pallas_call(
        query_kernel,
        grid=(steps,),
        in_specs=[
            pl.BlockSpec(keys_e.shape, lambda i: (0, 0)),
            pl.BlockSpec(keys_o.shape, lambda i: (0, 0)),
            pl.BlockSpec((1,) + ds.shape[1:], lambda i: (i, 0, 0)),
            pl.BlockSpec(memory_space=pl.ANY),
        ],
        out_specs=pl.BlockSpec((tok, 2 * PAIRS * LATENT), lambda i: (0, i + ahead)),
        out_shape=jax.ShapeDtypeStruct(started.shape, started.dtype),
        input_output_aliases={3: 0},
        compiler_params=pltpu.CompilerParams(vmem_limit_bytes=60 * MIB),
        cost_estimate=pl.CostEstimate(
            flops=4 * tok * steps * PAIRS * rows * LATENT,
            bytes_accessed=4 * tok * steps * PAIRS * (LATENT + rows),
            transcendentals=0,
        ),
        name="query_gradients",
    )(keys_e, keys_o, ds, started)


def local(queries, d_out, branch_latent, trunk_latent, ancestors, anc_count):
    leafs = lax.axis_size("leaf")
    head_parts = lax.axis_size("head")
    owned = trunk_latent.shape[0]
    part_rows = BLK // head_parts

    outgoing = pick(ancestors, trunk_latent.reshape(owned * BLK, LATENT))
    incoming = lax.all_to_all(
        outgoing.reshape(leafs, CAP * BLK, LATENT), "leaf", split_axis=0, concat_axis=0, tiled=True
    ).reshape(leafs * CAP * BLK, LATENT)

    s_own, dp_own = own_scores(branch_latent, queries, d_out)

    started, ds, keys_e, keys_o, sent, mine, *others = attention(
        owned, head_parts, anc_count, ancestors, incoming, branch_latent, s_own, dp_own,
        queries, d_out,
    )

    theirs = []
    for hop, part in enumerate(others, 1):
        route = [(i, (i + hop) % head_parts) for i in range(head_parts)]
        theirs.append(lax.ppermute(part, "head", route))
    got = lax.all_to_all(
        sent.reshape(leafs * head_parts, CAP * part_rows, LATENT),
        ("leaf", "head"), split_axis=0, concat_axis=0, tiled=True,
    ).reshape(leafs * CAP * BLK, LATENT)
    d_queries = query_gradients(keys_e, keys_o, ds, started)
    d_branch, d_trunk = finish(ancestors, got, mine, theirs, owned, part_rows)
    return d_queries, d_branch, d_trunk


def solution(mesh):
    return jax.shard_map(
        local,
        mesh=mesh,
        in_specs=(
            P("leaf", "head"),
            P("leaf", "head"),
            P("leaf", None),
            P("leaf", None, None),
            P(),
            P(),
        ),
        out_specs=(P("leaf", "head"), P(("leaf", "head"), None), P("leaf", "head", None)),
        check_vma=False,
    )
```

```python
import functools
import math

import jax
import jax.numpy as jnp
from jax import lax
from jax.experimental import pallas as pl
from jax.experimental.pallas import tpu as pltpu
from jax.sharding import PartitionSpec as P

RANK = 512
QK_HEAD = 192
LATENT = 576
BLK = 8
CAP = 2
ANC = 32
LEAST_LIVE = 24
LANES = 128
WIDTH = 640
HALF = WIDTH - LATENT
PAIRS = 4
MASKED = -1e30
FAR_OFF = 1 << 20
SCALE = float(QK_HEAD) ** -0.5
EXP_SCALE = SCALE * math.log2(math.e)
MIB = 1024 * 1024
NT = (((1,), (1,)), ((), ()))
NN = (((1,), (0,)), ((), ()))
TN = (((0,), (0,)), ((), ()))


def mm(a, b, dims):
    return lax.dot_general(a, b, dims, preferred_element_type=jnp.float32)


def pieces(total, size):
    return [(at, min(size, total - at)) for at in range(0, total, size)]


def div(x, n):
    return x >> (n.bit_length() - 1) if n & (n - 1) == 0 else lax.div(x, jnp.full_like(x, n))


def mod(x, n):
    return x - div(x, n) * n


def column(rows):
    return lax.broadcasted_iota(jnp.int32, (rows, 1), 0)


def one_hot(place, size):
    lane = lax.broadcasted_iota(jnp.int32, (place.shape[0], size), 1)
    return jnp.where(lane == place, 1.0, 0.0).astype(jnp.bfloat16)


def seen_rows(rows, tok):
    sub = token_part(tok)
    seen = [rows - tok + (j + 1) * sub for j in range(tok // sub)]
    return seen, [sum(seen[:j]) for j in range(len(seen) + 1)]


def token_part(tok):
    return 64 if tok % 64 == 0 else tok


def listed_blocks(ancestors, owned, second):
    leafs = ancestors.shape[0]
    rows = leafs * CAP * BLK
    named = ancestors[...].astype(jnp.float32)
    named = jnp.broadcast_to(named[:, None, :], (leafs, CAP * BLK, ANC)).reshape(rows, ANC)
    first = lax.axis_index("leaf") * owned
    low_end = first.astype(jnp.float32)
    mine = (named >= low_end) & (named < low_end + owned)
    low = jnp.min(jnp.where(mine, named, float(FAR_OFF)), axis=1, keepdims=True)
    high = jnp.max(jnp.where(mine, named, -1.0), axis=1, keepdims=True)
    return jnp.where(second, high, low).astype(jnp.int32) - first


def pick_kernel(ancestors, trunk, out):
    owned = trunk.shape[0] // BLK
    row = column(out.shape[0])
    block = listed_blocks(ancestors, owned, mod(div(row, BLK), CAP) == 1)
    sel = one_hot(block * BLK + mod(row, BLK), trunk.shape[0])
    out[...] = mm(sel, trunk[...], NN).astype(out.dtype)


def pick(ancestors, trunk):
    rows = ancestors.shape[0] * CAP * BLK
    return pl.pallas_call(
        pick_kernel,
        out_shape=jax.ShapeDtypeStruct((rows, LATENT), trunk.dtype),
        name="pick_blocks",
    )(ancestors, trunk)


def finish_kernel(ancestors, got, mine, *rest):
    theirs, (d_branch, d_trunk) = rest[:-2], rest[-2:]
    owned, part_rows = d_trunk.shape[0], d_trunk.shape[1]
    row = column(got.shape[0])
    block = listed_blocks(ancestors, owned, mod(div(row, part_rows), CAP) == 1)
    sel = one_hot(block * part_rows + mod(row, part_rows), owned * part_rows)
    total = mm(sel, got[...], TN)
    for b in range(owned):
        d_trunk[b] = total[b * part_rows:(b + 1) * part_rows]
    own = mine[...]
    for other in theirs:
        own = own + other[...]
    d_branch[...] = own


def finish(ancestors, got, mine, theirs, owned, part_rows):
    return pl.pallas_call(
        finish_kernel,
        out_shape=[
            jax.ShapeDtypeStruct(mine.shape, jnp.float32),
            jax.ShapeDtypeStruct((owned, part_rows, LATENT), jnp.float32),
        ],
        compiler_params=pltpu.CompilerParams(vmem_limit_bytes=8 * MIB),
        name="sum_gradients",
    )(ancestors, got, mine, *theirs)


def slot_places(ancestors, owned):
    row = column(ANC * BLK)
    mine = ancestors[pl.ds(lax.axis_index("leaf"), 1), :].astype(jnp.float32)
    mine = jnp.broadcast_to(mine, (ANC * BLK, ANC))
    lane = lax.broadcasted_iota(jnp.int32, (ANC * BLK, ANC), 1)
    block = jnp.max(jnp.where(lane == div(row, BLK), mine, -1.0), axis=1, keepdims=True)
    owner = div(block.astype(jnp.int32), owned)
    low_end = (owner * owned).astype(jnp.float32)
    below = (mine >= low_end) & (mine < block)
    second = jnp.max(jnp.where(below, 1.0, 0.0), axis=1, keepdims=True).astype(jnp.int32)
    return row, owner, second


def stack_heads(q, do, q_st, do_st, toks, to, heads):
    sub = toks.size
    pairs = heads // 2
    for i in range(pairs):
        at = i * 2 * LATENT
        even, odd = pl.ds(to + i * sub, sub), pl.ds(to + (pairs + i) * sub, sub)
        q_st[even, :] = q[toks, at:at + WIDTH]
        moved = q[toks, at + LATENT - HALF:at + 2 * LATENT]
        q_st[odd, :] = pltpu.roll(moved, WIDTH - HALF, axis=1)
        do_st[even, :] = do[toks, pl.ds(2 * i * RANK, RANK)]
        do_st[odd, :] = do[toks, pl.ds((2 * i + 1) * RANK, RANK)]


def causal_bias(shape, sub):
    key_at = lax.broadcasted_iota(jnp.int32, shape, 0)
    tok_at = mod(lax.broadcasted_iota(jnp.int32, shape, 1), sub)
    return jnp.where(key_at <= tok_at, 0.0, MASKED)


def own_kernel(own, q, do, s_own, dp_own, keys, causal, q_st, do_st):
    tok = own.shape[0]
    sub = q.shape[0]
    heads = 2 * PAIRS

    @pl.when(pl.program_id(0) == 0)
    def _():
        pad = jnp.zeros((tok, HALF), jnp.float32)
        padded = jnp.concatenate([own[...].astype(jnp.float32), pad], axis=1)
        keys[...] = padded.astype(jnp.bfloat16)
        causal[...] = causal_bias(causal.shape, sub)

    for group in range(s_own.shape[0]):
        cols = pl.ds(group * heads * LATENT, heads * LATENT)
        grad_cols = pl.ds(group * heads * RANK, heads * RANK)
        base = group * heads * sub
        block = pl.ds(base, heads * sub)
        stack_heads(
            q.at[:, cols], do.at[:, grad_cols], q_st, do_st, pl.ds(0, sub), base, heads
        )
        out = mm(keys[...], q_st[block, :], NT)
        s_own[group, :tok - sub] = out[:tok - sub]
        s_own[group, tok - sub:] = out[tok - sub:] + causal[...]
        dp_own[group] = mm(keys[:, :RANK], do_st[block, :], NT).astype(dp_own.dtype)


def own_scores(own, queries, d_out):
    tok = own.shape[0]
    heads = queries.shape[1] // LATENT
    steps = heads // (2 * PAIRS)
    sub = token_part(tok)
    parts = tok // sub
    unit = 2 * PAIRS * sub
    group = 2 if steps % 2 == 0 else 1
    bf16, f32 = jnp.bfloat16, jnp.float32
    return pl.pallas_call(
        own_kernel,
        grid=(steps // group,),
        in_specs=[
            pl.BlockSpec(own.shape, lambda i: (0, 0)),
            pl.BlockSpec((sub, group * 2 * PAIRS * LATENT), lambda i: (parts - 1, i)),
            pl.BlockSpec((sub, group * 2 * PAIRS * RANK), lambda i: (parts - 1, i)),
        ],
        out_specs=[pl.BlockSpec((group, tok, unit), lambda i: (i, 0, 0))] * 2,
        out_shape=[
            jax.ShapeDtypeStruct((steps, tok, unit), f32),
            jax.ShapeDtypeStruct((steps, tok, unit), bf16),
        ],
        scratch_shapes=[
            pltpu.VMEM((tok, WIDTH), bf16),
            pltpu.VMEM((sub, unit), f32),
            pltpu.VMEM((group * unit, WIDTH), bf16),
            pltpu.VMEM((group * unit, RANK), bf16),
        ],
        compiler_params=pltpu.CompilerParams(vmem_limit_bytes=60 * MIB),
        cost_estimate=pl.CostEstimate(
            flops=2 * sub * heads * tok * (LATENT + RANK),
            bytes_accessed=2 * sub * heads * (LATENT + RANK + 3 * tok),
            transcendentals=0,
        ),
        name="own_scores",
    )(own, queries, d_out)


def attn_kernel(
    owned, head_parts, ahead, anc_count, ancestors, incoming, own, s_own, dp_own, q, do,
    dq, ds, keys_out_e, keys_out_o, sent, *rest
):
    own_parts = rest[:head_parts]
    scratch = rest[head_parts:]
    k_e, k_o, sems, far_bias, causal, q_st, s, dp, p_low, tops, acc_k, acc_v = scratch
    tok = q.shape[0]
    far_rows, rows = ANC * BLK, ANC * BLK + tok
    sub = token_part(tok)
    parts = tok // sub
    stack = 2 * PAIRS * sub
    least = LEAST_LIVE * BLK
    step = pl.program_id(0)
    key_copies = [
        pltpu.make_async_copy(k_e, keys_out_e, sems.at[0]),
        pltpu.make_async_copy(k_o, keys_out_o, sems.at[1]),
    ]

    @pl.when(step == 0)
    def _():
        row, owner, second = slot_places(ancestors, owned)
        sel = one_hot((owner * CAP + second) * BLK + mod(row, BLK), incoming.shape[0])
        far = mm(sel, incoming[...], NN)
        joined = jnp.concatenate([far, own[...].astype(jnp.float32)], axis=0)
        padded = jnp.concatenate([joined, jnp.zeros((rows, HALF), jnp.float32)], axis=1)
        k_e[...] = padded.astype(jnp.bfloat16)
        k_o[...] = pltpu.roll(padded, HALF, axis=1).astype(jnp.bfloat16)
        for copy in key_copies:
            copy.start()
        live = anc_count[lax.axis_index("leaf")]
        slot = div(lax.broadcasted_iota(jnp.int32, far_bias.shape, 0) + least, BLK)
        far_bias[...] = jnp.where(slot < live, 0.0, MASKED)
        causal[...] = causal_bias(causal.shape, sub)
        acc_k[...] = jnp.zeros_like(acc_k)
        acc_v[...] = jnp.zeros_like(acc_v)

    seen_of, starts = seen_rows(rows, tok)

    def seen(j):
        return seen_of[j]

    def lanes(j):
        return pl.ds(j * stack, stack)

    def fill(j):
        toks = pl.ds(j * sub, sub)
        for i in range(PAIRS):
            at = i * 2 * LATENT
            q_st[pl.ds(j * stack + i * sub, sub), :] = q[toks, at:at + WIDTH]
            odd = q[toks, at + LATENT - HALF:at + 2 * LATENT]
            odd = pltpu.roll(odd, WIDTH - HALF, axis=1)
            q_st[pl.ds(j * stack + (PAIRS + i) * sub, sub), :] = odd

    heads = list(range(0, 2 * PAIRS, 2)) + list(range(1, 2 * PAIRS, 2))

    def grads(j, first, count, at=0, size=RANK):
        toks = pl.ds(j * sub, sub)
        cols = [pl.ds(h * RANK + at, size) for h in heads[first:first + count]]
        return jnp.concatenate([do[toks, c] for c in cols], axis=0)

    def fold(x):
        return x.reshape(-1, 8, x.shape[1])

    def given(j):
        return j == parts - 1

    def score(j, at):
        n, cols = seen(j), pl.ds(j * stack + at, stack // 2)
        out = mm(k_e[:far_rows if given(j) else n, :], q_st[cols, :].T, NN)
        near = [(0, out[:least]), (least, out[least:far_rows] + far_bias[...])]
        top = None
        if given(j):
            top = jnp.max(fold(s_own[0, :, pl.ds(at, stack // 2)]), axis=0)
        else:
            if j > 0:
                near.append((far_rows, out[far_rows:n - sub]))
            near.append((n - sub, out[n - sub:] + causal[...]))
        for r, part in near:
            s[pl.ds(r, part.shape[0]), cols] = part
            part = jnp.max(fold(part), axis=0)
            top = part if top is None else jnp.maximum(top, part)
        tops[:, cols] = top

    def prob(j, at):
        n, cols = far_rows if given(j) else seen(j), pl.ds(j * stack + at, stack // 2)
        dp[:n, cols] = mm(k_e[:n, :RANK], grads(j, at // sub, PAIRS).T, NN)

    state = {}

    def scores_at(j, r, n, at):
        if given(j) and r >= far_rows:
            return s_own[0, pl.ds(r - far_rows, n), pl.ds(at, LANES)]
        return s[pl.ds(r, n), pl.ds(j * stack + at, LANES)]

    def probs_at(j, r, n, at):
        if given(j) and r >= far_rows:
            return dp_own[0, pl.ds(r - far_rows, n), pl.ds(at, LANES)].astype(jnp.float32)
        return dp[pl.ds(r, n), pl.ds(j * stack + at, LANES)]

    def soft_sums(j, at):
        lane = pl.ds(j * stack + at, LANES)
        top = jnp.max(tops[:, lane], axis=0, keepdims=True)
        total = jnp.zeros((8, LANES), jnp.float32)
        delta = jnp.zeros((8, LANES), jnp.float32)
        for r, n in pieces(seen(j), 64):
            e = jnp.exp2((scores_at(j, r, n, at) - top) * EXP_SCALE)
            s[pl.ds(r, n), lane] = e
            total += jnp.sum(fold(e), axis=0)
            delta += jnp.sum(fold(e * probs_at(j, r, n, at)), axis=0)
        inv = 1.0 / jnp.sum(total, axis=0, keepdims=True)
        state[j, at] = inv, jnp.sum(delta, axis=0, keepdims=True) * inv

    def soft_outs(j, at):
        lane = pl.ds(j * stack + at, LANES)
        inv, delta = state.pop((j, at))
        for r, n in pieces(seen(j), 64):
            p = s[pl.ds(r, n), lane] * inv
            p_low[pl.ds(r, n), lane] = p.astype(jnp.bfloat16)
            ds[0, pl.ds(starts[j] + r, n), pl.ds(at, LANES)] = (p * (probs_at(j, r, n, at) - delta)).astype(ds.dtype)

    def grad_values(j, at, size):
        n, cols = seen(j), pl.ds(at, size)
        acc_v[:n, cols] += mm(p_low[:n, lanes(j)], grads(j, 0, 2 * PAIRS, at, size), NN)

    def grad_keys(j, at, size):
        n, cols = seen(j), pl.ds(at, size)
        acc_k[:n, cols] += mm(ds[0, pl.ds(starts[j], n), :], q_st[lanes(j), cols], NN)

    def jobs_of(i):
        products, passes = [], []
        if i < parts:
            products += [functools.partial(fill, i)]
            for at in (0, stack // 2):
                products += [functools.partial(score, i, at), functools.partial(prob, i, at)]
        if 0 <= i - 2 < parts:
            products += [functools.partial(grad_values, i - 2, *c) for c in pieces(RANK, 256)]
            products += [functools.partial(grad_keys, i - 2, *c) for c in pieces(WIDTH, 256)]
        if 0 <= i - 1 < parts:
            for at in range(0, stack, LANES):
                passes += [functools.partial(job, i - 1, at) for job in (soft_sums, soft_outs)]
        order = [
            (k / len(group), g, job)
            for g, group in enumerate((products, passes)) for k, job in enumerate(group)
        ]
        return [job for _, _, job in sorted(order, key=lambda item: item[:2])]

    for i in range(parts + 2):
        for job in jobs_of(i):
            job()

    @pl.when(step < ahead)
    def _():
        put_queries(dq, ds, k_e, k_o)

    @pl.when(step == pl.num_programs(0) - 1)
    def _():
        acc_k[...] = acc_k[...] * SCALE
        acc_k[:, :RANK] += acc_v[...]
        part_rows = BLK // head_parts
        row, owner, second = slot_places(ancestors, owned)
        inner = mod(row, BLK)
        place = (owner * head_parts + div(inner, part_rows)) * CAP + second
        place = place * part_rows + mod(inner, part_rows)
        sel = one_hot(place, sent.shape[0])
        far = acc_k[:far_rows, :LATENT].astype(jnp.bfloat16)
        sent[...] = mm(sel, far, TN).astype(sent.dtype)
        own_rows = tok // head_parts
        for hop, out in enumerate(own_parts):
            part = lax.rem(lax.axis_index("head") + hop, head_parts)
            at = pl.multiple_of(far_rows + part * own_rows, 8)
            out[...] = acc_k[pl.ds(at, own_rows), :LATENT]
        for copy in key_copies:
            copy.wait()


def steps_ahead(steps):
    return steps // 2


def attention(
    owned, head_parts, anc_count, ancestors, incoming, own, s_own, dp_own, queries, d_out
):
    tok = queries.shape[0]
    heads = queries.shape[1] // LATENT
    steps = heads // (2 * PAIRS)
    ahead = steps_ahead(steps)
    far_rows, rows = ANC * BLK, ANC * BLK + tok
    toks = 2 * PAIRS * tok
    stack = 2 * PAIRS * token_part(tok)
    ds_rows = seen_rows(rows, tok)[1][-1]
    bf16, f32 = jnp.bfloat16, jnp.float32

    def whole(i):
        return (0, 0)

    def along(i):
        return (0, i)

    own_part = (tok // head_parts, LATENT)
    return pl.pallas_call(
        functools.partial(attn_kernel, owned, head_parts, ahead),
        grid=(steps,),
        in_specs=[
            pl.BlockSpec(memory_space=pltpu.SMEM),
            pl.BlockSpec(ancestors.shape, whole),
            pl.BlockSpec(incoming.shape, whole),
            pl.BlockSpec(own.shape, whole),
            pl.BlockSpec((1,) + s_own.shape[1:], lambda i: (i, 0, 0)),
            pl.BlockSpec((1,) + dp_own.shape[1:], lambda i: (i, 0, 0)),
            pl.BlockSpec((tok, 2 * PAIRS * LATENT), along),
            pl.BlockSpec((tok, 2 * PAIRS * RANK), along),
        ],
        out_specs=[
            pl.BlockSpec(
                (tok, 2 * PAIRS * LATENT), lambda i: (0, jnp.minimum(i, max(ahead - 1, 0)))
            ),
            pl.BlockSpec((1, ds_rows, stack), lambda i: (jnp.maximum(i - ahead, 0), 0, 0)),
            pl.BlockSpec(memory_space=pl.ANY),
            pl.BlockSpec(memory_space=pl.ANY),
            pl.BlockSpec(incoming.shape, whole),
        ] + [pl.BlockSpec(own_part, whole)] * head_parts,
        out_shape=[
            jax.ShapeDtypeStruct(queries.shape, bf16),
            jax.ShapeDtypeStruct((steps - ahead, ds_rows, stack), bf16),
            jax.ShapeDtypeStruct((rows, WIDTH), bf16),
            jax.ShapeDtypeStruct((rows, WIDTH), bf16),
            jax.ShapeDtypeStruct(incoming.shape, bf16),
        ] + [jax.ShapeDtypeStruct(own_part, f32)] * head_parts,
        scratch_shapes=[
            pltpu.VMEM((rows, WIDTH), bf16),
            pltpu.VMEM((rows, WIDTH), bf16),
            pltpu.SemaphoreType.DMA((2,)),
            pltpu.VMEM((far_rows - LEAST_LIVE * BLK, stack // 2), f32),
            pltpu.VMEM((token_part(tok), stack // 2), f32),
            pltpu.VMEM((toks, WIDTH), bf16),
            pltpu.VMEM((rows, toks), f32),
            pltpu.VMEM((rows, toks), f32),
            pltpu.VMEM((rows, toks), bf16),
            pltpu.VMEM((8, toks), f32),
            pltpu.VMEM((rows, WIDTH), f32),
            pltpu.VMEM((rows, RANK), f32),
        ],
        compiler_params=pltpu.CompilerParams(vmem_limit_bytes=52 * MIB),
        cost_estimate=pl.CostEstimate(
            flops=2 * tok * heads * rows * (2 * LATENT + 2 * RANK),
            bytes_accessed=2 * tok * heads * (LATENT + RANK + rows),
            transcendentals=tok * heads * rows,
        ),
        name="score_gradients",
    )(anc_count, ancestors, incoming, own, s_own, dp_own, queries, d_out)


def put_queries(dq, ds, keys_e, keys_o):
    tok = dq.shape[0]
    sub = token_part(tok)
    stack = PAIRS * sub
    low = LATENT - HALF
    seen, starts = seen_rows(keys_e.shape[0], tok)
    for j, n in enumerate(seen):
        block = pl.ds(starts[j], n)
        even = mm(ds[0, block, :stack], keys_e[:n, :], TN) * SCALE
        odd = mm(ds[0, block, stack:], keys_o[:n, :], TN) * SCALE
        for i in range(PAIRS):
            at = i * 2 * LATENT
            part = slice(i * sub, (i + 1) * sub)
            toks = pl.ds(j * sub, sub)
            dq[toks, at:at + low] = even[part, :low].astype(dq.dtype)
            joint = even[part, low:] + odd[part, :2 * HALF]
            dq[toks, at + low:at + low + 2 * HALF] = joint.astype(dq.dtype)
            dq[toks, at + low + 2 * HALF:at + 2 * LATENT] = odd[part, 2 * HALF:].astype(dq.dtype)


def query_kernel(keys_e, keys_o, ds, started, dq):
    put_queries(dq, ds, keys_e, keys_o)


def query_gradients(keys_e, keys_o, ds, started):
    tok = started.shape[0]
    steps, rows = ds.shape[0], keys_e.shape[0]
    ahead = started.shape[1] // (2 * PAIRS * LATENT) - steps
    return pl.pallas_call(
        query_kernel,
        grid=(steps,),
        in_specs=[
            pl.BlockSpec(keys_e.shape, lambda i: (0, 0)),
            pl.BlockSpec(keys_o.shape, lambda i: (0, 0)),
            pl.BlockSpec((1,) + ds.shape[1:], lambda i: (i, 0, 0)),
            pl.BlockSpec(memory_space=pl.ANY),
        ],
        out_specs=pl.BlockSpec((tok, 2 * PAIRS * LATENT), lambda i: (0, i + ahead)),
        out_shape=jax.ShapeDtypeStruct(started.shape, started.dtype),
        input_output_aliases={3: 0},
        compiler_params=pltpu.CompilerParams(vmem_limit_bytes=60 * MIB),
        cost_estimate=pl.CostEstimate(
            flops=4 * tok * steps * PAIRS * rows * LATENT,
            bytes_accessed=4 * tok * steps * PAIRS * (LATENT + rows),
            transcendentals=0,
        ),
        name="query_gradients",
    )(keys_e, keys_o, ds, started)


def local(queries, d_out, branch_latent, trunk_latent, ancestors, anc_count):
    leafs = lax.axis_size("leaf")
    head_parts = lax.axis_size("head")
    owned = trunk_latent.shape[0]
    part_rows = BLK // head_parts

    outgoing = pick(ancestors, trunk_latent.reshape(owned * BLK, LATENT))
    incoming = lax.all_to_all(
        outgoing.reshape(leafs, CAP * BLK, LATENT), "leaf", split_axis=0, concat_axis=0, tiled=True
    ).reshape(leafs * CAP * BLK, LATENT)

    s_own, dp_own = own_scores(branch_latent, queries, d_out)

    started, ds, keys_e, keys_o, sent, mine, *others = attention(
        owned, head_parts, anc_count, ancestors, incoming, branch_latent, s_own, dp_own,
        queries, d_out,
    )

    theirs = []
    for hop, part in enumerate(others, 1):
        route = [(i, (i + hop) % head_parts) for i in range(head_parts)]
        theirs.append(lax.ppermute(part, "head", route))
    got = lax.all_to_all(
        sent.reshape(leafs * head_parts, CAP * part_rows, LATENT),
        ("leaf", "head"), split_axis=0, concat_axis=0, tiled=True,
    ).reshape(leafs * CAP * BLK, LATENT)
    d_queries = query_gradients(keys_e, keys_o, ds, started)
    d_branch, d_trunk = finish(ancestors, got, mine, theirs, owned, part_rows)
    return d_queries, d_branch, d_trunk


def solution(mesh):
    return jax.shard_map(
        local,
        mesh=mesh,
        in_specs=(
            P("leaf", "head"),
            P("leaf", "head"),
            P("leaf", None),
            P("leaf", None, None),
            P(),
            P(),
        ),
        out_specs=(P("leaf", "head"), P(("leaf", "head"), None), P("leaf", "head", None)),
        check_vma=False,
    )
```

```python
import functools
import math

import jax
import jax.numpy as jnp
from jax import lax
from jax.experimental import pallas as pl
from jax.experimental.pallas import tpu as pltpu
from jax.sharding import PartitionSpec as P

RANK = 512
QK_HEAD = 192
LATENT = 576
BLK = 8
CAP = 2
ANC = 32
LEAST_LIVE = 24
LANES = 128
WIDTH = 640
HALF = WIDTH - LATENT
PAIRS = 4
MASKED = -1e30
FAR_OFF = 1 << 20
SCALE = float(QK_HEAD) ** -0.5
EXP_SCALE = SCALE * math.log2(math.e)
MIB = 1024 * 1024
NT = (((1,), (1,)), ((), ()))
NN = (((1,), (0,)), ((), ()))
TN = (((0,), (0,)), ((), ()))


def mm(a, b, dims):
    return lax.dot_general(a, b, dims, preferred_element_type=jnp.float32)


def pieces(total, size):
    return [(at, min(size, total - at)) for at in range(0, total, size)]


def div(x, n):
    return x >> (n.bit_length() - 1) if n & (n - 1) == 0 else lax.div(x, jnp.full_like(x, n))


def mod(x, n):
    return x - div(x, n) * n


def column(rows):
    return lax.broadcasted_iota(jnp.int32, (rows, 1), 0)


def one_hot(place, size):
    lane = lax.broadcasted_iota(jnp.int32, (place.shape[0], size), 1)
    return jnp.where(lane == place, 1.0, 0.0).astype(jnp.bfloat16)


def seen_rows(rows, tok):
    sub = token_part(tok)
    seen = [rows - tok + (j + 1) * sub for j in range(tok // sub)]
    return seen, [sum(seen[:j]) for j in range(len(seen) + 1)]


def token_part(tok):
    return 64 if tok % 64 == 0 else tok


def listed_blocks(ancestors, owned, second):
    leafs = ancestors.shape[0]
    rows = leafs * CAP * BLK
    named = ancestors[...].astype(jnp.float32)
    named = jnp.broadcast_to(named[:, None, :], (leafs, CAP * BLK, ANC)).reshape(rows, ANC)
    first = lax.axis_index("leaf") * owned
    low_end = first.astype(jnp.float32)
    mine = (named >= low_end) & (named < low_end + owned)
    low = jnp.min(jnp.where(mine, named, float(FAR_OFF)), axis=1, keepdims=True)
    high = jnp.max(jnp.where(mine, named, -1.0), axis=1, keepdims=True)
    return jnp.where(second, high, low).astype(jnp.int32) - first


def pick_kernel(ancestors, trunk, out):
    owned = trunk.shape[0] // BLK
    row = column(out.shape[0])
    block = listed_blocks(ancestors, owned, mod(div(row, BLK), CAP) == 1)
    sel = one_hot(block * BLK + mod(row, BLK), trunk.shape[0])
    out[...] = mm(sel, trunk[...], NN).astype(out.dtype)


def pick(ancestors, trunk):
    rows = ancestors.shape[0] * CAP * BLK
    return pl.pallas_call(
        pick_kernel,
        out_shape=jax.ShapeDtypeStruct((rows, LATENT), trunk.dtype),
        name="pick_blocks",
    )(ancestors, trunk)


def finish_kernel(ancestors, got, mine, *rest):
    theirs, (d_branch, d_trunk) = rest[:-2], rest[-2:]
    owned, part_rows = d_trunk.shape[0], d_trunk.shape[1]
    row = column(got.shape[0])
    block = listed_blocks(ancestors, owned, mod(div(row, part_rows), CAP) == 1)
    sel = one_hot(block * part_rows + mod(row, part_rows), owned * part_rows)
    total = mm(sel, got[...], TN)
    for b in range(owned):
        d_trunk[b] = total[b * part_rows:(b + 1) * part_rows]
    own = mine[...]
    for other in theirs:
        own = own + other[...]
    d_branch[...] = own


def finish(ancestors, got, mine, theirs, owned, part_rows):
    return pl.pallas_call(
        finish_kernel,
        out_shape=[
            jax.ShapeDtypeStruct(mine.shape, jnp.float32),
            jax.ShapeDtypeStruct((owned, part_rows, LATENT), jnp.float32),
        ],
        compiler_params=pltpu.CompilerParams(vmem_limit_bytes=8 * MIB),
        name="sum_gradients",
    )(ancestors, got, mine, *theirs)


def slot_places(ancestors, owned):
    row = column(ANC * BLK)
    mine = ancestors[pl.ds(lax.axis_index("leaf"), 1), :].astype(jnp.float32)
    mine = jnp.broadcast_to(mine, (ANC * BLK, ANC))
    lane = lax.broadcasted_iota(jnp.int32, (ANC * BLK, ANC), 1)
    block = jnp.max(jnp.where(lane == div(row, BLK), mine, -1.0), axis=1, keepdims=True)
    owner = div(block.astype(jnp.int32), owned)
    low_end = (owner * owned).astype(jnp.float32)
    below = (mine >= low_end) & (mine < block)
    second = jnp.max(jnp.where(below, 1.0, 0.0), axis=1, keepdims=True).astype(jnp.int32)
    return row, owner, second


def stack_heads(q, do, q_st, do_st, toks, to, heads):
    sub = toks.size
    pairs = heads // 2
    for i in range(pairs):
        at = i * 2 * LATENT
        even, odd = pl.ds(to + i * sub, sub), pl.ds(to + (pairs + i) * sub, sub)
        q_st[even, :] = q[toks, at:at + WIDTH]
        moved = q[toks, at + LATENT - HALF:at + 2 * LATENT]
        q_st[odd, :] = pltpu.roll(moved, WIDTH - HALF, axis=1)
        do_st[even, :] = do[toks, pl.ds(2 * i * RANK, RANK)]
        do_st[odd, :] = do[toks, pl.ds((2 * i + 1) * RANK, RANK)]


def causal_bias(shape, sub):
    key_at = lax.broadcasted_iota(jnp.int32, shape, 0)
    tok_at = mod(lax.broadcasted_iota(jnp.int32, shape, 1), sub)
    return jnp.where(key_at <= tok_at, 0.0, MASKED)


def own_kernel(own, q, do, s_own, dp_own, keys, causal, q_st, do_st):
    tok = own.shape[0]
    sub = q.shape[0]
    heads = 2 * PAIRS

    @pl.when(pl.program_id(0) == 0)
    def _():
        pad = jnp.zeros((tok, HALF), jnp.float32)
        padded = jnp.concatenate([own[...].astype(jnp.float32), pad], axis=1)
        keys[...] = padded.astype(jnp.bfloat16)
        causal[...] = causal_bias(causal.shape, sub)

    for group in range(s_own.shape[0]):
        cols = pl.ds(group * heads * LATENT, heads * LATENT)
        grad_cols = pl.ds(group * heads * RANK, heads * RANK)
        base = group * heads * sub
        block = pl.ds(base, heads * sub)
        stack_heads(
            q.at[:, cols], do.at[:, grad_cols], q_st, do_st, pl.ds(0, sub), base, heads
        )
        out = mm(keys[...], q_st[block, :], NT)
        s_own[group, :tok - sub] = out[:tok - sub]
        s_own[group, tok - sub:] = out[tok - sub:] + causal[...]
        dp_own[group] = mm(keys[:, :RANK], do_st[block, :], NT).astype(dp_own.dtype)


def own_scores(own, queries, d_out):
    tok = own.shape[0]
    heads = queries.shape[1] // LATENT
    steps = heads // (2 * PAIRS)
    sub = token_part(tok)
    parts = tok // sub
    unit = 2 * PAIRS * sub
    group = 2 if steps % 2 == 0 else 1
    bf16, f32 = jnp.bfloat16, jnp.float32
    return pl.pallas_call(
        own_kernel,
        grid=(steps // group,),
        in_specs=[
            pl.BlockSpec(own.shape, lambda i: (0, 0)),
            pl.BlockSpec((sub, group * 2 * PAIRS * LATENT), lambda i: (parts - 1, i)),
            pl.BlockSpec((sub, group * 2 * PAIRS * RANK), lambda i: (parts - 1, i)),
        ],
        out_specs=[pl.BlockSpec((group, tok, unit), lambda i: (i, 0, 0))] * 2,
        out_shape=[
            jax.ShapeDtypeStruct((steps, tok, unit), f32),
            jax.ShapeDtypeStruct((steps, tok, unit), bf16),
        ],
        scratch_shapes=[
            pltpu.VMEM((tok, WIDTH), bf16),
            pltpu.VMEM((sub, unit), f32),
            pltpu.VMEM((group * unit, WIDTH), bf16),
            pltpu.VMEM((group * unit, RANK), bf16),
        ],
        compiler_params=pltpu.CompilerParams(vmem_limit_bytes=60 * MIB),
        cost_estimate=pl.CostEstimate(
            flops=2 * sub * heads * tok * (LATENT + RANK),
            bytes_accessed=2 * sub * heads * (LATENT + RANK + 3 * tok),
            transcendentals=0,
        ),
        name="own_scores",
    )(own, queries, d_out)


def attn_kernel(
    owned, head_parts, ahead, anc_count, ancestors, incoming, own, s_own, dp_own, q, do,
    dq, ds, keys_out, sent, *rest
):
    own_parts = rest[:head_parts]
    scratch = rest[head_parts:]
    keys, sem, far_bias, causal, q_st, s, dp, p_low, tops, acc_k, acc_v = scratch
    tok = q.shape[0]
    far_rows, rows = ANC * BLK, ANC * BLK + tok
    sub = token_part(tok)
    parts = tok // sub
    stack = 2 * PAIRS * sub
    least = LEAST_LIVE * BLK
    step = pl.program_id(0)
    keys_copy = pltpu.make_async_copy(keys, keys_out, sem)

    @pl.when(step == 0)
    def _():
        row, owner, second = slot_places(ancestors, owned)
        sel = one_hot((owner * CAP + second) * BLK + mod(row, BLK), incoming.shape[0])
        far = mm(sel, incoming[...], NN)
        joined = jnp.concatenate([far, own[...].astype(jnp.float32)], axis=0)
        padded = jnp.concatenate([joined, jnp.zeros((rows, HALF), jnp.float32)], axis=1)
        keys[...] = padded.astype(jnp.bfloat16)
        keys_copy.start()
        live = anc_count[lax.axis_index("leaf")]
        slot = div(lax.broadcasted_iota(jnp.int32, far_bias.shape, 0) + least, BLK)
        far_bias[...] = jnp.where(slot < live, 0.0, MASKED)
        causal[...] = causal_bias(causal.shape, sub)
        acc_k[...] = jnp.zeros_like(acc_k)
        acc_v[...] = jnp.zeros_like(acc_v)

    seen_of, starts = seen_rows(rows, tok)

    def seen(j):
        return seen_of[j]

    def lanes(j):
        return pl.ds(j * stack, stack)

    def fill(j):
        toks = pl.ds(j * sub, sub)
        for i in range(PAIRS):
            at = i * 2 * LATENT
            q_st[pl.ds(j * stack + i * sub, sub), :] = q[toks, at:at + WIDTH]
            odd = q[toks, at + LATENT - HALF:at + 2 * LATENT]
            odd = pltpu.roll(odd, WIDTH - HALF, axis=1)
            q_st[pl.ds(j * stack + (PAIRS + i) * sub, sub), :] = odd

    heads = list(range(0, 2 * PAIRS, 2)) + list(range(1, 2 * PAIRS, 2))

    def grads(j, first, count, at=0, size=RANK):
        toks = pl.ds(j * sub, sub)
        cols = [pl.ds(h * RANK + at, size) for h in heads[first:first + count]]
        return jnp.concatenate([do[toks, c] for c in cols], axis=0)

    def fold(x):
        return x.reshape(-1, 8, x.shape[1])

    def given(j):
        return j == parts - 1

    def score(j, at):
        n, cols = seen(j), pl.ds(j * stack + at, stack // 2)
        out = mm(keys[:far_rows if given(j) else n, :], q_st[cols, :].T, NN)
        near = [(0, out[:least]), (least, out[least:far_rows] + far_bias[...])]
        top = None
        if given(j):
            top = jnp.max(fold(s_own[0, :, pl.ds(at, stack // 2)]), axis=0)
        else:
            if j > 0:
                near.append((far_rows, out[far_rows:n - sub]))
            near.append((n - sub, out[n - sub:] + causal[...]))
        for r, part in near:
            s[pl.ds(r, part.shape[0]), cols] = part
            part = jnp.max(fold(part), axis=0)
            top = part if top is None else jnp.maximum(top, part)
        tops[:, cols] = top

    def prob(j, at):
        n, cols = far_rows if given(j) else seen(j), pl.ds(j * stack + at, stack // 2)
        dp[:n, cols] = mm(keys[:n, :RANK], grads(j, at // sub, PAIRS).T, NN)

    state = {}

    def scores_at(j, r, n, at):
        if given(j) and r >= far_rows:
            return s_own[0, pl.ds(r - far_rows, n), pl.ds(at, LANES)]
        return s[pl.ds(r, n), pl.ds(j * stack + at, LANES)]

    def probs_at(j, r, n, at):
        if given(j) and r >= far_rows:
            return dp_own[0, pl.ds(r - far_rows, n), pl.ds(at, LANES)].astype(jnp.float32)
        return dp[pl.ds(r, n), pl.ds(j * stack + at, LANES)]

    def soft_sums(j, at):
        lane = pl.ds(j * stack + at, LANES)
        top = jnp.max(tops[:, lane], axis=0, keepdims=True)
        total = jnp.zeros((8, LANES), jnp.float32)
        delta = jnp.zeros((8, LANES), jnp.float32)
        for r, n in pieces(seen(j), 64):
            e = jnp.exp2((scores_at(j, r, n, at) - top) * EXP_SCALE)
            s[pl.ds(r, n), lane] = e
            total += jnp.sum(fold(e), axis=0)
            delta += jnp.sum(fold(e * probs_at(j, r, n, at)), axis=0)
        inv = 1.0 / jnp.sum(total, axis=0, keepdims=True)
        state[j, at] = inv, jnp.sum(delta, axis=0, keepdims=True) * inv

    def soft_outs(j, at):
        lane = pl.ds(j * stack + at, LANES)
        inv, delta = state.pop((j, at))
        for r, n in pieces(seen(j), 64):
            p = s[pl.ds(r, n), lane] * inv
            p_low[pl.ds(r, n), lane] = p.astype(jnp.bfloat16)
            ds[0, pl.ds(starts[j] + r, n), pl.ds(at, LANES)] = (p * (probs_at(j, r, n, at) - delta)).astype(ds.dtype)

    def grad_values(j, at, size):
        n, cols = seen(j), pl.ds(at, size)
        acc_v[:n, cols] += mm(p_low[:n, lanes(j)], grads(j, 0, 2 * PAIRS, at, size), NN)

    def grad_keys(j, at, size):
        n, cols = seen(j), pl.ds(at, size)
        acc_k[:n, cols] += mm(ds[0, pl.ds(starts[j], n), :], q_st[lanes(j), cols], NN)

    def jobs_of(i):
        products, passes = [], []
        if i < parts:
            products += [functools.partial(fill, i)]
            for at in (0, stack // 2):
                products += [functools.partial(score, i, at), functools.partial(prob, i, at)]
        if 0 <= i - 2 < parts:
            products += [functools.partial(grad_values, i - 2, *c) for c in pieces(RANK, 256)]
            products += [functools.partial(grad_keys, i - 2, *c) for c in pieces(WIDTH, 256)]
        if 0 <= i - 1 < parts:
            for at in range(0, stack, LANES):
                passes += [functools.partial(job, i - 1, at) for job in (soft_sums, soft_outs)]
        order = [
            (k / len(group), g, job)
            for g, group in enumerate((products, passes)) for k, job in enumerate(group)
        ]
        return [job for _, _, job in sorted(order, key=lambda item: item[:2])]

    for i in range(parts + 2):
        for job in jobs_of(i):
            job()

    @pl.when(step < ahead)
    def _():
        put_queries(dq, ds, keys)

    @pl.when(step == pl.num_programs(0) - 1)
    def _():
        acc_k[...] = acc_k[...] * SCALE
        acc_k[:, :RANK] += acc_v[...]
        part_rows = BLK // head_parts
        row, owner, second = slot_places(ancestors, owned)
        inner = mod(row, BLK)
        place = (owner * head_parts + div(inner, part_rows)) * CAP + second
        place = place * part_rows + mod(inner, part_rows)
        sel = one_hot(place, sent.shape[0])
        far = acc_k[:far_rows, :LATENT].astype(jnp.bfloat16)
        sent[...] = mm(sel, far, TN).astype(sent.dtype)
        own_rows = tok // head_parts
        for hop, out in enumerate(own_parts):
            part = lax.rem(lax.axis_index("head") + hop, head_parts)
            at = pl.multiple_of(far_rows + part * own_rows, 8)
            out[...] = acc_k[pl.ds(at, own_rows), :LATENT]
        keys_copy.wait()


def steps_ahead(steps):
    return steps // 2


def attention(
    owned, head_parts, anc_count, ancestors, incoming, own, s_own, dp_own, queries, d_out
):
    tok = queries.shape[0]
    heads = queries.shape[1] // LATENT
    steps = heads // (2 * PAIRS)
    ahead = steps_ahead(steps)
    far_rows, rows = ANC * BLK, ANC * BLK + tok
    toks = 2 * PAIRS * tok
    stack = 2 * PAIRS * token_part(tok)
    ds_rows = seen_rows(rows, tok)[1][-1]
    bf16, f32 = jnp.bfloat16, jnp.float32

    def whole(i):
        return (0, 0)

    def along(i):
        return (0, i)

    own_part = (tok // head_parts, LATENT)
    return pl.pallas_call(
        functools.partial(attn_kernel, owned, head_parts, ahead),
        grid=(steps,),
        in_specs=[
            pl.BlockSpec(memory_space=pltpu.SMEM),
            pl.BlockSpec(ancestors.shape, whole),
            pl.BlockSpec(incoming.shape, whole),
            pl.BlockSpec(own.shape, whole),
            pl.BlockSpec((1,) + s_own.shape[1:], lambda i: (i, 0, 0)),
            pl.BlockSpec((1,) + dp_own.shape[1:], lambda i: (i, 0, 0)),
            pl.BlockSpec((tok, 2 * PAIRS * LATENT), along),
            pl.BlockSpec((tok, 2 * PAIRS * RANK), along),
        ],
        out_specs=[
            pl.BlockSpec(
                (tok, 2 * PAIRS * LATENT), lambda i: (0, jnp.minimum(i, max(ahead - 1, 0)))
            ),
            pl.BlockSpec((1, ds_rows, stack), lambda i: (jnp.maximum(i - ahead, 0), 0, 0)),
            pl.BlockSpec(memory_space=pltpu.HBM),
            pl.BlockSpec(incoming.shape, whole),
        ] + [pl.BlockSpec(own_part, whole)] * head_parts,
        out_shape=[
            jax.ShapeDtypeStruct(queries.shape, bf16),
            jax.ShapeDtypeStruct((steps - ahead, ds_rows, stack), bf16),
            jax.ShapeDtypeStruct((rows, WIDTH), bf16),
            jax.ShapeDtypeStruct(incoming.shape, bf16),
        ] + [jax.ShapeDtypeStruct(own_part, f32)] * head_parts,
        scratch_shapes=[
            pltpu.VMEM((rows, WIDTH), bf16),
            pltpu.SemaphoreType.DMA(()),
            pltpu.VMEM((far_rows - LEAST_LIVE * BLK, stack // 2), f32),
            pltpu.VMEM((token_part(tok), stack // 2), f32),
            pltpu.VMEM((toks, WIDTH), bf16),
            pltpu.VMEM((rows, toks), f32),
            pltpu.VMEM((rows, toks), f32),
            pltpu.VMEM((rows, toks), bf16),
            pltpu.VMEM((8, toks), f32),
            pltpu.VMEM((rows, WIDTH), f32),
            pltpu.VMEM((rows, RANK), f32),
        ],
        compiler_params=pltpu.CompilerParams(vmem_limit_bytes=52 * MIB),
        cost_estimate=pl.CostEstimate(
            flops=2 * tok * heads * rows * (2 * LATENT + 2 * RANK),
            bytes_accessed=2 * tok * heads * (LATENT + RANK + rows),
            transcendentals=tok * heads * rows,
        ),
        name="score_gradients",
    )(anc_count, ancestors, incoming, own, s_own, dp_own, queries, d_out)


def put_queries(dq, ds, keys):
    tok = dq.shape[0]
    sub = token_part(tok)
    stack = PAIRS * sub
    low = LATENT - HALF
    seen, starts = seen_rows(keys.shape[0], tok)
    for j, n in enumerate(seen):
        both = mm(ds[0, pl.ds(starts[j], n), :], keys[:n, :], TN) * SCALE
        both = both.astype(dq.dtype)
        even, odd = both[:stack], pltpu.roll(both[stack:], HALF, axis=1)
        for i in range(PAIRS):
            at = i * 2 * LATENT
            part = slice(i * sub, (i + 1) * sub)
            toks = pl.ds(j * sub, sub)
            dq[toks, at:at + low] = even[part, :low]
            joint = even[part, low:] + odd[part, :2 * HALF]
            dq[toks, at + low:at + low + 2 * HALF] = joint
            dq[toks, at + low + 2 * HALF:at + 2 * LATENT] = odd[part, 2 * HALF:]


def query_kernel(keys, ds, started, dq):
    put_queries(dq, ds, keys)


def query_gradients(keys, ds, started):
    tok = started.shape[0]
    steps, rows = ds.shape[0], keys.shape[0]
    ahead = started.shape[1] // (2 * PAIRS * LATENT) - steps
    return pl.pallas_call(
        query_kernel,
        grid=(steps,),
        in_specs=[
            pl.BlockSpec(keys.shape, lambda i: (0, 0)),
            pl.BlockSpec((1,) + ds.shape[1:], lambda i: (i, 0, 0)),
            pl.BlockSpec(memory_space=pl.ANY),
        ],
        out_specs=pl.BlockSpec((tok, 2 * PAIRS * LATENT), lambda i: (0, i + ahead)),
        out_shape=jax.ShapeDtypeStruct(started.shape, started.dtype),
        input_output_aliases={2: 0},
        compiler_params=pltpu.CompilerParams(vmem_limit_bytes=239 * MIB // 4),
        cost_estimate=pl.CostEstimate(
            flops=4 * tok * steps * PAIRS * rows * LATENT,
            bytes_accessed=4 * tok * steps * PAIRS * (LATENT + rows),
            transcendentals=0,
        ),
        name="query_gradients",
    )(keys, ds, started)


def local(queries, d_out, branch_latent, trunk_latent, ancestors, anc_count):
    leafs = lax.axis_size("leaf")
    head_parts = lax.axis_size("head")
    owned = trunk_latent.shape[0]
    part_rows = BLK // head_parts

    outgoing = pick(ancestors, trunk_latent.reshape(owned * BLK, LATENT))
    incoming = lax.all_to_all(
        outgoing.reshape(leafs, CAP * BLK, LATENT), "leaf", split_axis=0, concat_axis=0, tiled=True
    ).reshape(leafs * CAP * BLK, LATENT)

    s_own, dp_own = own_scores(branch_latent, queries, d_out)

    started, ds, keys, sent, mine, *others = attention(
        owned, head_parts, anc_count, ancestors, incoming, branch_latent, s_own, dp_own,
        queries, d_out,
    )

    theirs = []
    for hop, part in enumerate(others, 1):
        route = [(i, (i + hop) % head_parts) for i in range(head_parts)]
        theirs.append(lax.ppermute(part, "head", route))
    got = lax.all_to_all(
        sent.reshape(leafs * head_parts, CAP * part_rows, LATENT),
        ("leaf", "head"), split_axis=0, concat_axis=0, tiled=True,
    ).reshape(leafs * CAP * BLK, LATENT)
    d_queries = query_gradients(keys, ds, started)
    d_branch, d_trunk = finish(ancestors, got, mine, theirs, owned, part_rows)
    return d_queries, d_branch, d_trunk


def solution(mesh):
    return jax.shard_map(
        local,
        mesh=mesh,
        in_specs=(
            P("leaf", "head"),
            P("leaf", "head"),
            P("leaf", None),
            P("leaf", None, None),
            P(),
            P(),
        ),
        out_specs=(P("leaf", "head"), P(("leaf", "head"), None), P("leaf", "head", None)),
        check_vma=False,
    )
```

```python
import functools
import math

import jax
import jax.numpy as jnp
from jax import lax
from jax.experimental import pallas as pl
from jax.experimental.pallas import tpu as pltpu
from jax.sharding import PartitionSpec as P

RANK = 512
QK_HEAD = 192
LATENT = 576
BLK = 8
CAP = 2
ANC = 32
LEAST_LIVE = 24
LANES = 128
WIDTH = 640
HALF = WIDTH - LATENT
PAIRS = 4
MASKED = -1e30
FAR_OFF = 1 << 20
SCALE = float(QK_HEAD) ** -0.5
EXP_SCALE = SCALE * math.log2(math.e)
MIB = 1024 * 1024
NT = (((1,), (1,)), ((), ()))
NN = (((1,), (0,)), ((), ()))
TN = (((0,), (0,)), ((), ()))


def mm(a, b, dims):
    return lax.dot_general(a, b, dims, preferred_element_type=jnp.float32)


def pieces(total, size):
    return [(at, min(size, total - at)) for at in range(0, total, size)]


def div(x, n):
    return x >> (n.bit_length() - 1) if n & (n - 1) == 0 else lax.div(x, jnp.full_like(x, n))


def mod(x, n):
    return x - div(x, n) * n


def column(rows):
    return lax.broadcasted_iota(jnp.int32, (rows, 1), 0)


def one_hot(place, size):
    lane = lax.broadcasted_iota(jnp.int32, (place.shape[0], size), 1)
    return jnp.where(lane == place, 1.0, 0.0).astype(jnp.bfloat16)


def seen_rows(rows, tok):
    sub = token_part(tok)
    seen = [rows - tok + (j + 1) * sub for j in range(tok // sub)]
    return seen, [sum(seen[:j]) for j in range(len(seen) + 1)]


def token_part(tok):
    return 64 if tok % 64 == 0 else tok


def listed_blocks(ancestors, owned, second):
    leafs = ancestors.shape[0]
    rows = leafs * CAP * BLK
    named = ancestors[...].astype(jnp.float32)
    named = jnp.broadcast_to(named[:, None, :], (leafs, CAP * BLK, ANC)).reshape(rows, ANC)
    first = lax.axis_index("leaf") * owned
    low_end = first.astype(jnp.float32)
    mine = (named >= low_end) & (named < low_end + owned)
    low = jnp.min(jnp.where(mine, named, float(FAR_OFF)), axis=1, keepdims=True)
    high = jnp.max(jnp.where(mine, named, -1.0), axis=1, keepdims=True)
    return jnp.where(second, high, low).astype(jnp.int32) - first


def pick_kernel(ancestors, trunk, out):
    owned = trunk.shape[0] // BLK
    row = column(out.shape[0])
    block = listed_blocks(ancestors, owned, mod(div(row, BLK), CAP) == 1)
    sel = one_hot(block * BLK + mod(row, BLK), trunk.shape[0])
    out[...] = mm(sel, trunk[...], NN).astype(out.dtype)


def pick(ancestors, trunk):
    rows = ancestors.shape[0] * CAP * BLK
    return pl.pallas_call(
        pick_kernel,
        out_shape=jax.ShapeDtypeStruct((rows, LATENT), trunk.dtype),
        name="pick_blocks",
    )(ancestors, trunk)


def finish_kernel(ancestors, got, mine, *rest):
    theirs, (d_branch, d_trunk) = rest[:-2], rest[-2:]
    owned, part_rows = d_trunk.shape[0], d_trunk.shape[1]
    row = column(got.shape[0])
    block = listed_blocks(ancestors, owned, mod(div(row, part_rows), CAP) == 1)
    sel = one_hot(block * part_rows + mod(row, part_rows), owned * part_rows)
    total = mm(sel, got[...], TN)
    for b in range(owned):
        d_trunk[b] = total[b * part_rows:(b + 1) * part_rows]
    own = mine[...]
    for other in theirs:
        own = own + other[...]
    d_branch[...] = own


def finish(ancestors, got, mine, theirs, owned, part_rows):
    return pl.pallas_call(
        finish_kernel,
        out_shape=[
            jax.ShapeDtypeStruct(mine.shape, jnp.float32),
            jax.ShapeDtypeStruct((owned, part_rows, LATENT), jnp.float32),
        ],
        compiler_params=pltpu.CompilerParams(vmem_limit_bytes=8 * MIB),
        name="sum_gradients",
    )(ancestors, got, mine, *theirs)


def slot_places(ancestors, owned):
    row = column(ANC * BLK)
    mine = ancestors[pl.ds(lax.axis_index("leaf"), 1), :].astype(jnp.float32)
    mine = jnp.broadcast_to(mine, (ANC * BLK, ANC))
    lane = lax.broadcasted_iota(jnp.int32, (ANC * BLK, ANC), 1)
    block = jnp.max(jnp.where(lane == div(row, BLK), mine, -1.0), axis=1, keepdims=True)
    owner = div(block.astype(jnp.int32), owned)
    low_end = (owner * owned).astype(jnp.float32)
    below = (mine >= low_end) & (mine < block)
    second = jnp.max(jnp.where(below, 1.0, 0.0), axis=1, keepdims=True).astype(jnp.int32)
    return row, owner, second


def stack_heads(q, do, q_st, do_st, toks, to, heads):
    sub = toks.size
    pairs = heads // 2
    for i in range(pairs):
        at = i * 2 * LATENT
        even, odd = pl.ds(to + i * sub, sub), pl.ds(to + (pairs + i) * sub, sub)
        q_st[even, :] = q[toks, at:at + WIDTH]
        moved = q[toks, at + LATENT - HALF:at + 2 * LATENT]
        q_st[odd, :] = pltpu.roll(moved, WIDTH - HALF, axis=1)
        do_st[even, :] = do[toks, pl.ds(2 * i * RANK, RANK)]
        do_st[odd, :] = do[toks, pl.ds((2 * i + 1) * RANK, RANK)]


def causal_bias(shape, sub):
    key_at = lax.broadcasted_iota(jnp.int32, shape, 0)
    tok_at = mod(lax.broadcasted_iota(jnp.int32, shape, 1), sub)
    return jnp.where(key_at <= tok_at, 0.0, MASKED)


def own_kernel(own, q, do, s_own, dp_own, keys, causal, q_st, do_st):
    tok = own.shape[0]
    sub = q.shape[0]
    heads = 2 * PAIRS

    @pl.when(pl.program_id(0) == 0)
    def _():
        pad = jnp.zeros((tok, HALF), jnp.float32)
        padded = jnp.concatenate([own[...].astype(jnp.float32), pad], axis=1)
        keys[...] = padded.astype(jnp.bfloat16)
        causal[...] = causal_bias(causal.shape, sub)

    for group in range(s_own.shape[0]):
        cols = pl.ds(group * heads * LATENT, heads * LATENT)
        grad_cols = pl.ds(group * heads * RANK, heads * RANK)
        base = group * heads * sub
        block = pl.ds(base, heads * sub)
        stack_heads(
            q.at[:, cols], do.at[:, grad_cols], q_st, do_st, pl.ds(0, sub), base, heads
        )
        out = mm(keys[...], q_st[block, :], NT)
        s_own[group, :tok - sub] = out[:tok - sub]
        s_own[group, tok - sub:] = out[tok - sub:] + causal[...]
        dp_own[group] = mm(keys[:, :RANK], do_st[block, :], NT).astype(dp_own.dtype)


def own_scores(own, queries, d_out):
    tok = own.shape[0]
    heads = queries.shape[1] // LATENT
    steps = heads // (2 * PAIRS)
    sub = token_part(tok)
    parts = tok // sub
    unit = 2 * PAIRS * sub
    group = 2 if steps % 2 == 0 else 1
    bf16, f32 = jnp.bfloat16, jnp.float32
    return pl.pallas_call(
        own_kernel,
        grid=(steps // group,),
        in_specs=[
            pl.BlockSpec(own.shape, lambda i: (0, 0)),
            pl.BlockSpec((sub, group * 2 * PAIRS * LATENT), lambda i: (parts - 1, i)),
            pl.BlockSpec((sub, group * 2 * PAIRS * RANK), lambda i: (parts - 1, i)),
        ],
        out_specs=[pl.BlockSpec((group, tok, unit), lambda i: (i, 0, 0))] * 2,
        out_shape=[
            jax.ShapeDtypeStruct((steps, tok, unit), f32),
            jax.ShapeDtypeStruct((steps, tok, unit), bf16),
        ],
        scratch_shapes=[
            pltpu.VMEM((tok, WIDTH), bf16),
            pltpu.VMEM((sub, unit), f32),
            pltpu.VMEM((group * unit, WIDTH), bf16),
            pltpu.VMEM((group * unit, RANK), bf16),
        ],
        compiler_params=pltpu.CompilerParams(vmem_limit_bytes=60 * MIB),
        cost_estimate=pl.CostEstimate(
            flops=2 * sub * heads * tok * (LATENT + RANK),
            bytes_accessed=2 * sub * heads * (LATENT + RANK + 3 * tok),
            transcendentals=0,
        ),
        name="own_scores",
    )(own, queries, d_out)


def attn_kernel(
    owned, head_parts, ahead, anc_count, ancestors, incoming, own, s_own, dp_own, q, do,
    dq, ds, keys_out, sent, *rest
):
    own_parts = rest[:head_parts]
    scratch = rest[head_parts:]
    keys, sem, far_bias, causal, q_st, s, dp, p_low, tops, acc_k, acc_v = scratch
    tok = q.shape[0]
    far_rows, rows = ANC * BLK, ANC * BLK + tok
    sub = token_part(tok)
    parts = tok // sub
    stack = 2 * PAIRS * sub
    least = LEAST_LIVE * BLK
    step = pl.program_id(0)
    keys_copy = pltpu.make_async_copy(keys, keys_out, sem)

    @pl.when(step == 0)
    def _():
        row, owner, second = slot_places(ancestors, owned)
        sel = one_hot((owner * CAP + second) * BLK + mod(row, BLK), incoming.shape[0])
        far = mm(sel, incoming[...], NN)
        joined = jnp.concatenate([far, own[...].astype(jnp.float32)], axis=0)
        padded = jnp.concatenate([joined, jnp.zeros((rows, HALF), jnp.float32)], axis=1)
        keys[...] = padded.astype(jnp.bfloat16)
        keys_copy.start()
        live = anc_count[lax.axis_index("leaf")]
        slot = div(lax.broadcasted_iota(jnp.int32, far_bias.shape, 0) + least, BLK)
        far_bias[...] = jnp.where(slot < live, 0.0, MASKED)
        causal[...] = causal_bias(causal.shape, sub)
        acc_k[...] = jnp.zeros_like(acc_k)
        acc_v[...] = jnp.zeros_like(acc_v)

    seen_of, starts = seen_rows(rows, tok)

    def seen(j):
        return seen_of[j]

    def lanes(j):
        return pl.ds(j * stack, stack)

    def fill(j):
        toks = pl.ds(j * sub, sub)
        for i in range(PAIRS):
            at = i * 2 * LATENT
            q_st[pl.ds(j * stack + i * sub, sub), :] = q[toks, at:at + WIDTH]
            odd = q[toks, at + LATENT - HALF:at + 2 * LATENT]
            odd = pltpu.roll(odd, WIDTH - HALF, axis=1)
            q_st[pl.ds(j * stack + (PAIRS + i) * sub, sub), :] = odd

    heads = list(range(0, 2 * PAIRS, 2)) + list(range(1, 2 * PAIRS, 2))

    def grads(j, first, count, at=0, size=RANK):
        toks = pl.ds(j * sub, sub)
        cols = [pl.ds(h * RANK + at, size) for h in heads[first:first + count]]
        return jnp.concatenate([do[toks, c] for c in cols], axis=0)

    def fold(x):
        return x.reshape(-1, 8, x.shape[1])

    def given(j):
        return j == parts - 1

    def score(j, at):
        n, cols = seen(j), pl.ds(j * stack + at, stack // 2)
        out = mm(keys[:far_rows if given(j) else n, :], q_st[cols, :].T, NN)
        near = [(0, out[:least]), (least, out[least:far_rows] + far_bias[...])]
        top = None
        if given(j):
            top = jnp.max(fold(s_own[0, :, pl.ds(at, stack // 2)]), axis=0)
        else:
            if j > 0:
                near.append((far_rows, out[far_rows:n - sub]))
            near.append((n - sub, out[n - sub:] + causal[...]))
        for r, part in near:
            s[pl.ds(r, part.shape[0]), cols] = part
            part = jnp.max(fold(part), axis=0)
            top = part if top is None else jnp.maximum(top, part)
        tops[:, cols] = top

    def prob(j, at):
        n, cols = far_rows if given(j) else seen(j), pl.ds(j * stack + at, stack // 2)
        dp[:n, cols] = mm(keys[:n, :RANK], grads(j, at // sub, PAIRS).T, NN)

    state = {}

    def scores_at(j, r, n, at):
        if given(j) and r >= far_rows:
            return s_own[0, pl.ds(r - far_rows, n), pl.ds(at, LANES)]
        return s[pl.ds(r, n), pl.ds(j * stack + at, LANES)]

    def probs_at(j, r, n, at):
        if given(j) and r >= far_rows:
            return dp_own[0, pl.ds(r - far_rows, n), pl.ds(at, LANES)].astype(jnp.float32)
        return dp[pl.ds(r, n), pl.ds(j * stack + at, LANES)]

    def soft_sums(j, at):
        lane = pl.ds(j * stack + at, LANES)
        top = jnp.max(tops[:, lane], axis=0, keepdims=True)
        total = jnp.zeros((8, LANES), jnp.float32)
        delta = jnp.zeros((8, LANES), jnp.float32)
        for r, n in pieces(seen(j), 64):
            e = jnp.exp2((scores_at(j, r, n, at) - top) * EXP_SCALE)
            s[pl.ds(r, n), lane] = e
            total += jnp.sum(fold(e), axis=0)
            delta += jnp.sum(fold(e * probs_at(j, r, n, at)), axis=0)
        inv = 1.0 / jnp.sum(total, axis=0, keepdims=True)
        state[j, at] = inv, jnp.sum(delta, axis=0, keepdims=True) * inv

    def soft_outs(j, at):
        lane = pl.ds(j * stack + at, LANES)
        inv, delta = state.pop((j, at))
        for r, n in pieces(seen(j), 64):
            p = s[pl.ds(r, n), lane] * inv
            p_low[pl.ds(r, n), lane] = p.astype(jnp.bfloat16)
            ds[0, pl.ds(starts[j] + r, n), pl.ds(at, LANES)] = (p * (probs_at(j, r, n, at) - delta)).astype(ds.dtype)

    def grad_values(j, at, size):
        n, cols = seen(j), pl.ds(at, size)
        acc_v[:n, cols] += mm(p_low[:n, lanes(j)], grads(j, 0, 2 * PAIRS, at, size), NN)

    def grad_keys(j, at, size):
        n, cols = seen(j), pl.ds(at, size)
        acc_k[:n, cols] += mm(ds[0, pl.ds(starts[j], n), :], q_st[lanes(j), cols], NN)

    def jobs_of(i):
        products, passes = [], []
        if i < parts:
            products += [functools.partial(fill, i)]
            for at in (0, stack // 2):
                products += [functools.partial(score, i, at), functools.partial(prob, i, at)]
        if 0 <= i - 2 < parts:
            products += [functools.partial(grad_values, i - 2, *c) for c in pieces(RANK, 256)]
            products += [functools.partial(grad_keys, i - 2, *c) for c in pieces(WIDTH, 256)]
        if 0 <= i - 1 < parts:
            for at in range(0, stack, LANES):
                passes += [functools.partial(job, i - 1, at) for job in (soft_sums, soft_outs)]
        order = [
            (k / len(group), g, job)
            for g, group in enumerate((products, passes)) for k, job in enumerate(group)
        ]
        return [job for _, _, job in sorted(order, key=lambda item: item[:2])]

    for i in range(parts + 2):
        for job in jobs_of(i):
            job()

    @pl.when(step < ahead)
    def _():
        put_queries(dq, ds, keys)

    @pl.when(step == pl.num_programs(0) - 1)
    def _():
        acc_k[...] = acc_k[...] * SCALE
        acc_k[:, :RANK] += acc_v[...]
        part_rows = BLK // head_parts
        row, owner, second = slot_places(ancestors, owned)
        inner = mod(row, BLK)
        place = (owner * head_parts + div(inner, part_rows)) * CAP + second
        place = place * part_rows + mod(inner, part_rows)
        sel = one_hot(place, sent.shape[0])
        far = acc_k[:far_rows, :LATENT].astype(jnp.bfloat16)
        sent[...] = mm(sel, far, TN).astype(sent.dtype)
        own_rows = tok // head_parts
        for hop, out in enumerate(own_parts):
            part = lax.rem(lax.axis_index("head") + hop, head_parts)
            at = pl.multiple_of(far_rows + part * own_rows, 8)
            out[...] = acc_k[pl.ds(at, own_rows), :LATENT]
        keys_copy.wait()


def steps_ahead(steps):
    return steps * 3 // 8


def attention(
    owned, head_parts, anc_count, ancestors, incoming, own, s_own, dp_own, queries, d_out
):
    tok = queries.shape[0]
    heads = queries.shape[1] // LATENT
    steps = heads // (2 * PAIRS)
    ahead = steps_ahead(steps)
    far_rows, rows = ANC * BLK, ANC * BLK + tok
    toks = 2 * PAIRS * tok
    stack = 2 * PAIRS * token_part(tok)
    ds_rows = seen_rows(rows, tok)[1][-1]
    bf16, f32 = jnp.bfloat16, jnp.float32

    def whole(i):
        return (0, 0)

    def along(i):
        return (0, i)

    own_part = (tok // head_parts, LATENT)
    return pl.pallas_call(
        functools.partial(attn_kernel, owned, head_parts, ahead),
        grid=(steps,),
        in_specs=[
            pl.BlockSpec(memory_space=pltpu.SMEM),
            pl.BlockSpec(ancestors.shape, whole),
            pl.BlockSpec(incoming.shape, whole),
            pl.BlockSpec(own.shape, whole),
            pl.BlockSpec((1,) + s_own.shape[1:], lambda i: (i, 0, 0)),
            pl.BlockSpec((1,) + dp_own.shape[1:], lambda i: (i, 0, 0)),
            pl.BlockSpec((tok, 2 * PAIRS * LATENT), along),
            pl.BlockSpec((tok, 2 * PAIRS * RANK), along),
        ],
        out_specs=[
            pl.BlockSpec(
                (tok, 2 * PAIRS * LATENT), lambda i: (0, jnp.minimum(i, max(ahead - 1, 0)))
            ),
            pl.BlockSpec((1, ds_rows, stack), lambda i: (jnp.maximum(i - ahead, 0), 0, 0)),
            pl.BlockSpec(memory_space=pltpu.HBM),
            pl.BlockSpec(incoming.shape, whole),
        ] + [pl.BlockSpec(own_part, whole)] * head_parts,
        out_shape=[
            jax.ShapeDtypeStruct(queries.shape, bf16),
            jax.ShapeDtypeStruct((steps - ahead, ds_rows, stack), bf16),
            jax.ShapeDtypeStruct((rows, WIDTH), bf16),
            jax.ShapeDtypeStruct(incoming.shape, bf16),
        ] + [jax.ShapeDtypeStruct(own_part, f32)] * head_parts,
        scratch_shapes=[
            pltpu.VMEM((rows, WIDTH), bf16),
            pltpu.SemaphoreType.DMA(()),
            pltpu.VMEM((far_rows - LEAST_LIVE * BLK, stack // 2), f32),
            pltpu.VMEM((token_part(tok), stack // 2), f32),
            pltpu.VMEM((toks, WIDTH), bf16),
            pltpu.VMEM((rows, toks), f32),
            pltpu.VMEM((rows, toks), f32),
            pltpu.VMEM((rows, toks), bf16),
            pltpu.VMEM((8, toks), f32),
            pltpu.VMEM((rows, WIDTH), f32),
            pltpu.VMEM((rows, RANK), f32),
        ],
        compiler_params=pltpu.CompilerParams(vmem_limit_bytes=52 * MIB),
        cost_estimate=pl.CostEstimate(
            flops=2 * tok * heads * rows * (2 * LATENT + 2 * RANK),
            bytes_accessed=2 * tok * heads * (LATENT + RANK + rows),
            transcendentals=tok * heads * rows,
        ),
        name="score_gradients",
    )(anc_count, ancestors, incoming, own, s_own, dp_own, queries, d_out)


def put_queries(dq, ds, keys):
    tok = dq.shape[0]
    sub = token_part(tok)
    stack = PAIRS * sub
    low = LATENT - HALF
    seen, starts = seen_rows(keys.shape[0], tok)
    for j, n in enumerate(seen):
        both = mm(ds[0, pl.ds(starts[j], n), :], keys[:n, :], TN) * SCALE
        both = both.astype(dq.dtype)
        even, odd = both[:stack], pltpu.roll(both[stack:], HALF, axis=1)
        for i in range(PAIRS):
            at = i * 2 * LATENT
            part = slice(i * sub, (i + 1) * sub)
            toks = pl.ds(j * sub, sub)
            dq[toks, at:at + low] = even[part, :low]
            joint = even[part, low:] + odd[part, :2 * HALF]
            dq[toks, at + low:at + low + 2 * HALF] = joint
            dq[toks, at + low + 2 * HALF:at + 2 * LATENT] = odd[part, 2 * HALF:]


def query_kernel(keys, ds, started, dq):
    put_queries(dq, ds, keys)


def query_gradients(keys, ds, started):
    tok = started.shape[0]
    steps, rows = ds.shape[0], keys.shape[0]
    ahead = started.shape[1] // (2 * PAIRS * LATENT) - steps
    return pl.pallas_call(
        query_kernel,
        grid=(steps,),
        in_specs=[
            pl.BlockSpec(keys.shape, lambda i: (0, 0)),
            pl.BlockSpec((1,) + ds.shape[1:], lambda i: (i, 0, 0)),
            pl.BlockSpec(memory_space=pl.ANY),
        ],
        out_specs=pl.BlockSpec((tok, 2 * PAIRS * LATENT), lambda i: (0, i + ahead)),
        out_shape=jax.ShapeDtypeStruct(started.shape, started.dtype),
        input_output_aliases={2: 0},
        compiler_params=pltpu.CompilerParams(vmem_limit_bytes=32 * MIB),
        cost_estimate=pl.CostEstimate(
            flops=4 * tok * steps * PAIRS * rows * LATENT,
            bytes_accessed=4 * tok * steps * PAIRS * (LATENT + rows),
            transcendentals=0,
        ),
        name="query_gradients",
    )(keys, ds, started)


def local(queries, d_out, branch_latent, trunk_latent, ancestors, anc_count):
    leafs = lax.axis_size("leaf")
    head_parts = lax.axis_size("head")
    owned = trunk_latent.shape[0]
    part_rows = BLK // head_parts

    outgoing = pick(ancestors, trunk_latent.reshape(owned * BLK, LATENT))
    incoming = lax.all_to_all(
        outgoing.reshape(leafs, CAP * BLK, LATENT), "leaf", split_axis=0, concat_axis=0, tiled=True
    ).reshape(leafs * CAP * BLK, LATENT)

    s_own, dp_own = own_scores(branch_latent, queries, d_out)

    started, ds, keys, sent, mine, *others = attention(
        owned, head_parts, anc_count, ancestors, incoming, branch_latent, s_own, dp_own,
        queries, d_out,
    )

    theirs = []
    for hop, part in enumerate(others, 1):
        route = [(i, (i + hop) % head_parts) for i in range(head_parts)]
        theirs.append(lax.ppermute(part, "head", route))
    got = lax.all_to_all(
        sent.reshape(leafs * head_parts, CAP * part_rows, LATENT),
        ("leaf", "head"), split_axis=0, concat_axis=0, tiled=True,
    ).reshape(leafs * CAP * BLK, LATENT)
    d_queries = query_gradients(keys, ds, started)
    d_branch, d_trunk = finish(ancestors, got, mine, theirs, owned, part_rows)
    return d_queries, d_branch, d_trunk


def solution(mesh):
    return jax.shard_map(
        local,
        mesh=mesh,
        in_specs=(
            P("leaf", "head"),
            P("leaf", "head"),
            P("leaf", None),
            P("leaf", None, None),
            P(),
            P(),
        ),
        out_specs=(P("leaf", "head"), P(("leaf", "head"), None), P("leaf", "head", None)),
        check_vma=False,
    )
```

```python
import functools
import math

import jax
import jax.numpy as jnp
from jax import lax
from jax.experimental import pallas as pl
from jax.experimental.pallas import tpu as pltpu
from jax.sharding import PartitionSpec as P

RANK = 512
QK_HEAD = 192
LATENT = 576
BLK = 8
CAP = 2
ANC = 32
LEAST_LIVE = 24
LANES = 128
WIDTH = 640
HALF = WIDTH - LATENT
PAIRS = 4
MASKED = -1e30
FAR_OFF = 1 << 20
SCALE = float(QK_HEAD) ** -0.5
EXP_SCALE = SCALE * math.log2(math.e)
MIB = 1024 * 1024
NT = (((1,), (1,)), ((), ()))
NN = (((1,), (0,)), ((), ()))
TN = (((0,), (0,)), ((), ()))


def mm(a, b, dims):
    return lax.dot_general(a, b, dims, preferred_element_type=jnp.float32)


def pieces(total, size):
    return [(at, min(size, total - at)) for at in range(0, total, size)]


def div(x, n):
    return x >> (n.bit_length() - 1) if n & (n - 1) == 0 else lax.div(x, jnp.full_like(x, n))


def mod(x, n):
    return x - div(x, n) * n


def column(rows):
    return lax.broadcasted_iota(jnp.int32, (rows, 1), 0)


def one_hot(place, size):
    lane = lax.broadcasted_iota(jnp.int32, (place.shape[0], size), 1)
    return jnp.where(lane == place, 1.0, 0.0).astype(jnp.bfloat16)


def seen_rows(rows, tok):
    sub = token_part(tok)
    seen = [rows - tok + (j + 1) * sub for j in range(tok // sub)]
    return seen, [sum(seen[:j]) for j in range(len(seen) + 1)]


def token_part(tok):
    return 64 if tok % 64 == 0 else tok


def listed_blocks(ancestors, owned, second):
    leafs = ancestors.shape[0]
    rows = leafs * CAP * BLK
    named = ancestors[...].astype(jnp.float32)
    first = lax.axis_index("leaf") * owned
    low_end = first.astype(jnp.float32)
    mine = (named >= low_end) & (named < low_end + owned)
    low = jnp.min(jnp.where(mine, named, float(FAR_OFF)), axis=1, keepdims=True)
    high = jnp.max(jnp.where(mine, named, -1.0), axis=1, keepdims=True)

    def spread(x):
        x = jnp.broadcast_to(x, (leafs, LANES))
        return jnp.broadcast_to(x[:, None, :], (leafs, CAP * BLK, LANES)).reshape(rows, LANES)[:, :1]

    low, high = spread(low), spread(high)
    return jnp.where(second, high, low).astype(jnp.int32) - first


def pick_kernel(ancestors, trunk, out):
    owned = trunk.shape[0] // BLK
    row = column(out.shape[0])
    block = listed_blocks(ancestors, owned, mod(div(row, BLK), CAP) == 1)
    sel = one_hot(block * BLK + mod(row, BLK), trunk.shape[0])
    out[...] = mm(sel, trunk[...], NN).astype(out.dtype)


def pick(ancestors, trunk):
    rows = ancestors.shape[0] * CAP * BLK
    return pl.pallas_call(
        pick_kernel,
        out_shape=jax.ShapeDtypeStruct((rows, LATENT), trunk.dtype),
        name="pick_blocks",
    )(ancestors, trunk)


def finish_kernel(ancestors, got, mine, *rest):
    theirs, (d_branch, d_trunk) = rest[:-2], rest[-2:]
    owned, part_rows = d_trunk.shape[0], d_trunk.shape[1]
    row = column(got.shape[0])
    block = listed_blocks(ancestors, owned, mod(div(row, part_rows), CAP) == 1)
    sel = one_hot(block * part_rows + mod(row, part_rows), owned * part_rows)
    total = mm(sel, got[...], TN)
    for b in range(owned):
        d_trunk[b] = total[b * part_rows:(b + 1) * part_rows]
    own = mine[...]
    for other in theirs:
        own = own + other[...]
    d_branch[...] = own


def finish(ancestors, got, mine, theirs, owned, part_rows):
    return pl.pallas_call(
        finish_kernel,
        out_shape=[
            jax.ShapeDtypeStruct(mine.shape, jnp.float32),
            jax.ShapeDtypeStruct((owned, part_rows, LATENT), jnp.float32),
        ],
        compiler_params=pltpu.CompilerParams(vmem_limit_bytes=8 * MIB),
        name="sum_gradients",
    )(ancestors, got, mine, *theirs)


def slot_places(ancestors, owned):
    row = column(ANC * BLK)
    mine = ancestors[pl.ds(lax.axis_index("leaf"), 1), :].astype(jnp.float32)
    mine = jnp.broadcast_to(mine, (ANC * BLK, ANC))
    lane = lax.broadcasted_iota(jnp.int32, (ANC * BLK, ANC), 1)
    block = jnp.max(jnp.where(lane == div(row, BLK), mine, -1.0), axis=1, keepdims=True)
    owner = div(block.astype(jnp.int32), owned)
    low_end = (owner * owned).astype(jnp.float32)
    below = (mine >= low_end) & (mine < block)
    second = jnp.max(jnp.where(below, 1.0, 0.0), axis=1, keepdims=True).astype(jnp.int32)
    return row, owner, second


def stack_heads(q, do, q_st, do_st, toks, to, heads):
    sub = toks.size
    pairs = heads // 2
    for i in range(pairs):
        at = i * 2 * LATENT
        even, odd = pl.ds(to + i * sub, sub), pl.ds(to + (pairs + i) * sub, sub)
        q_st[even, :] = q[toks, at:at + WIDTH]
        moved = q[toks, at + LATENT - HALF:at + 2 * LATENT]
        q_st[odd, :] = pltpu.roll(moved, WIDTH - HALF, axis=1)
        do_st[even, :] = do[toks, pl.ds(2 * i * RANK, RANK)]
        do_st[odd, :] = do[toks, pl.ds((2 * i + 1) * RANK, RANK)]


def causal_bias(shape, sub):
    key_at = lax.broadcasted_iota(jnp.int32, shape, 0)
    tok_at = mod(lax.broadcasted_iota(jnp.int32, shape, 1), sub)
    return jnp.where(key_at <= tok_at, 0.0, MASKED)


def own_kernel(own, q, do, s_own, dp_own, keys, causal, q_st, do_st):
    tok = own.shape[0]
    sub = q.shape[0]
    heads = 2 * PAIRS

    @pl.when(pl.program_id(0) == 0)
    def _():
        pad = jnp.zeros((tok, HALF), jnp.float32)
        padded = jnp.concatenate([own[...].astype(jnp.float32), pad], axis=1)
        keys[...] = padded.astype(jnp.bfloat16)
        causal[...] = causal_bias(causal.shape, sub)

    for group in range(s_own.shape[0]):
        cols = pl.ds(group * heads * LATENT, heads * LATENT)
        grad_cols = pl.ds(group * heads * RANK, heads * RANK)
        base = group * heads * sub
        block = pl.ds(base, heads * sub)
        stack_heads(
            q.at[:, cols], do.at[:, grad_cols], q_st, do_st, pl.ds(0, sub), base, heads
        )
        out = mm(keys[...], q_st[block, :], NT)
        s_own[group, :tok - sub] = out[:tok - sub]
        s_own[group, tok - sub:] = out[tok - sub:] + causal[...]
        dp_own[group] = mm(keys[:, :RANK], do_st[block, :], NT).astype(dp_own.dtype)


def own_scores(own, queries, d_out):
    tok = own.shape[0]
    heads = queries.shape[1] // LATENT
    steps = heads // (2 * PAIRS)
    sub = token_part(tok)
    parts = tok // sub
    unit = 2 * PAIRS * sub
    group = 2 if steps % 2 == 0 else 1
    bf16, f32 = jnp.bfloat16, jnp.float32
    return pl.pallas_call(
        own_kernel,
        grid=(steps // group,),
        in_specs=[
            pl.BlockSpec(own.shape, lambda i: (0, 0)),
            pl.BlockSpec((sub, group * 2 * PAIRS * LATENT), lambda i: (parts - 1, i)),
            pl.BlockSpec((sub, group * 2 * PAIRS * RANK), lambda i: (parts - 1, i)),
        ],
        out_specs=[pl.BlockSpec((group, tok, unit), lambda i: (i, 0, 0))] * 2,
        out_shape=[
            jax.ShapeDtypeStruct((steps, tok, unit), f32),
            jax.ShapeDtypeStruct((steps, tok, unit), bf16),
        ],
        scratch_shapes=[
            pltpu.VMEM((tok, WIDTH), bf16),
            pltpu.VMEM((sub, unit), f32),
            pltpu.VMEM((group * unit, WIDTH), bf16),
            pltpu.VMEM((group * unit, RANK), bf16),
        ],
        compiler_params=pltpu.CompilerParams(vmem_limit_bytes=60 * MIB),
        cost_estimate=pl.CostEstimate(
            flops=2 * sub * heads * tok * (LATENT + RANK),
            bytes_accessed=2 * sub * heads * (LATENT + RANK + 3 * tok),
            transcendentals=0,
        ),
        name="own_scores",
    )(own, queries, d_out)


def attn_kernel(
    owned, head_parts, ahead, anc_count, ancestors, incoming, own, s_own, dp_own, q, do,
    dq, ds, keys_out, sent, *rest
):
    own_parts = rest[:head_parts]
    scratch = rest[head_parts:]
    keys, sem, far_bias, causal, q_st, s, dp, p_low, tops, acc_k, acc_v = scratch
    tok = q.shape[0]
    far_rows, rows = ANC * BLK, ANC * BLK + tok
    sub = token_part(tok)
    parts = tok // sub
    stack = 2 * PAIRS * sub
    least = LEAST_LIVE * BLK
    step = pl.program_id(0)
    keys_copy = pltpu.make_async_copy(keys, keys_out, sem)

    @pl.when(step == 0)
    def _():
        row, owner, second = slot_places(ancestors, owned)
        sel = one_hot((owner * CAP + second) * BLK + mod(row, BLK), incoming.shape[0])
        far = mm(sel, incoming[...], NN)
        joined = jnp.concatenate([far, own[...].astype(jnp.float32)], axis=0)
        padded = jnp.concatenate([joined, jnp.zeros((rows, HALF), jnp.float32)], axis=1)
        keys[...] = padded.astype(jnp.bfloat16)
        keys_copy.start()
        live = anc_count[lax.axis_index("leaf")]
        slot = div(lax.broadcasted_iota(jnp.int32, far_bias.shape, 0) + least, BLK)
        far_bias[...] = jnp.where(slot < live, 0.0, MASKED)
        causal[...] = causal_bias(causal.shape, sub)
        acc_k[...] = jnp.zeros_like(acc_k)
        acc_v[...] = jnp.zeros_like(acc_v)

    seen_of, starts = seen_rows(rows, tok)

    def seen(j):
        return seen_of[j]

    def lanes(j):
        return pl.ds(j * stack, stack)

    def fill(j):
        toks = pl.ds(j * sub, sub)
        for i in range(PAIRS):
            at = i * 2 * LATENT
            q_st[pl.ds(j * stack + i * sub, sub), :] = q[toks, at:at + WIDTH]
            odd = q[toks, at + LATENT - HALF:at + 2 * LATENT]
            odd = pltpu.roll(odd, WIDTH - HALF, axis=1)
            q_st[pl.ds(j * stack + (PAIRS + i) * sub, sub), :] = odd

    heads = list(range(0, 2 * PAIRS, 2)) + list(range(1, 2 * PAIRS, 2))

    def grads(j, first, count, at=0, size=RANK):
        toks = pl.ds(j * sub, sub)
        cols = [pl.ds(h * RANK + at, size) for h in heads[first:first + count]]
        return jnp.concatenate([do[toks, c] for c in cols], axis=0)

    def fold(x):
        return x.reshape(-1, 8, x.shape[1])

    def given(j):
        return j == parts - 1

    def score(j, at):
        n, cols = seen(j), pl.ds(j * stack + at, stack // 2)
        out = mm(keys[:far_rows if given(j) else n, :], q_st[cols, :].T, NN)
        near = [(0, out[:least]), (least, out[least:far_rows] + far_bias[...])]
        top = None
        if given(j):
            top = jnp.max(fold(s_own[0, :, pl.ds(at, stack // 2)]), axis=0)
        else:
            if j > 0:
                near.append((far_rows, out[far_rows:n - sub]))
            near.append((n - sub, out[n - sub:] + causal[...]))
        for r, part in near:
            s[pl.ds(r, part.shape[0]), cols] = part
            part = jnp.max(fold(part), axis=0)
            top = part if top is None else jnp.maximum(top, part)
        tops[:, cols] = top

    def prob(j, at):
        n, cols = far_rows if given(j) else seen(j), pl.ds(j * stack + at, stack // 2)
        dp[:n, cols] = mm(keys[:n, :RANK], grads(j, at // sub, PAIRS).T, NN)

    state = {}

    def scores_at(j, r, n, at):
        if given(j) and r >= far_rows:
            return s_own[0, pl.ds(r - far_rows, n), pl.ds(at, LANES)]
        return s[pl.ds(r, n), pl.ds(j * stack + at, LANES)]

    def probs_at(j, r, n, at):
        if given(j) and r >= far_rows:
            return dp_own[0, pl.ds(r - far_rows, n), pl.ds(at, LANES)].astype(jnp.float32)
        return dp[pl.ds(r, n), pl.ds(j * stack + at, LANES)]

    def soft_sums(j, at):
        lane = pl.ds(j * stack + at, LANES)
        top = jnp.max(tops[:, lane], axis=0, keepdims=True)
        total = jnp.zeros((8, LANES), jnp.float32)
        delta = jnp.zeros((8, LANES), jnp.float32)
        for r, n in pieces(seen(j), 64):
            e = jnp.exp2((scores_at(j, r, n, at) - top) * EXP_SCALE)
            s[pl.ds(r, n), lane] = e
            total += jnp.sum(fold(e), axis=0)
            delta += jnp.sum(fold(e * probs_at(j, r, n, at)), axis=0)
        inv = 1.0 / jnp.sum(total, axis=0, keepdims=True)
        state[j, at] = inv, jnp.sum(delta, axis=0, keepdims=True) * inv

    def soft_outs(j, at):
        lane = pl.ds(j * stack + at, LANES)
        inv, delta = state.pop((j, at))
        for r, n in pieces(seen(j), 64):
            p = s[pl.ds(r, n), lane] * inv
            p_low[pl.ds(r, n), lane] = p.astype(jnp.bfloat16)
            ds[0, pl.ds(starts[j] + r, n), pl.ds(at, LANES)] = (p * (probs_at(j, r, n, at) - delta)).astype(ds.dtype)

    def grad_values(j, at, size):
        n, cols = seen(j), pl.ds(at, size)
        acc_v[:n, cols] += mm(p_low[:n, lanes(j)], grads(j, 0, 2 * PAIRS, at, size), NN)

    def grad_keys(j, at, size):
        n, cols = seen(j), pl.ds(at, size)
        acc_k[:n, cols] += mm(ds[0, pl.ds(starts[j], n), :], q_st[lanes(j), cols], NN)

    def jobs_of(i):
        products, passes = [], []
        if i < parts:
            products += [functools.partial(fill, i)]
            for at in (0, stack // 2):
                products += [functools.partial(score, i, at), functools.partial(prob, i, at)]
        if 0 <= i - 2 < parts:
            products += [functools.partial(grad_values, i - 2, *c) for c in pieces(RANK, 256)]
            products += [functools.partial(grad_keys, i - 2, *c) for c in pieces(WIDTH, 256)]
        if 0 <= i - 1 < parts:
            for at in range(0, stack, LANES):
                passes += [functools.partial(job, i - 1, at) for job in (soft_sums, soft_outs)]
        order = [
            (k / len(group), g, job)
            for g, group in enumerate((products, passes)) for k, job in enumerate(group)
        ]
        return [job for _, _, job in sorted(order, key=lambda item: item[:2])]

    for i in range(parts + 2):
        for job in jobs_of(i):
            job()

    @pl.when(step < ahead)
    def _():
        put_queries(dq, ds, keys)

    @pl.when(step == pl.num_programs(0) - 1)
    def _():
        acc_k[...] = acc_k[...] * SCALE
        acc_k[:, :RANK] += acc_v[...]
        part_rows = BLK // head_parts
        row, owner, second = slot_places(ancestors, owned)
        inner = mod(row, BLK)
        place = (owner * head_parts + div(inner, part_rows)) * CAP + second
        place = place * part_rows + mod(inner, part_rows)
        sel = one_hot(place, sent.shape[0])
        far = acc_k[:far_rows, :LATENT].astype(jnp.bfloat16)
        sent[...] = mm(sel, far, TN).astype(sent.dtype)
        own_rows = tok // head_parts
        for hop, out in enumerate(own_parts):
            part = lax.rem(lax.axis_index("head") + hop, head_parts)
            at = pl.multiple_of(far_rows + part * own_rows, 8)
            out[...] = acc_k[pl.ds(at, own_rows), :LATENT]
        keys_copy.wait()


def steps_ahead(steps):
    return steps * 3 // 8


def attention(
    owned, head_parts, anc_count, ancestors, incoming, own, s_own, dp_own, queries, d_out
):
    tok = queries.shape[0]
    heads = queries.shape[1] // LATENT
    steps = heads // (2 * PAIRS)
    ahead = steps_ahead(steps)
    far_rows, rows = ANC * BLK, ANC * BLK + tok
    toks = 2 * PAIRS * tok
    stack = 2 * PAIRS * token_part(tok)
    ds_rows = seen_rows(rows, tok)[1][-1]
    bf16, f32 = jnp.bfloat16, jnp.float32

    def whole(i):
        return (0, 0)

    def along(i):
        return (0, i)

    own_part = (tok // head_parts, LATENT)
    return pl.pallas_call(
        functools.partial(attn_kernel, owned, head_parts, ahead),
        grid=(steps,),
        in_specs=[
            pl.BlockSpec(memory_space=pltpu.SMEM),
            pl.BlockSpec(ancestors.shape, whole),
            pl.BlockSpec(incoming.shape, whole),
            pl.BlockSpec(own.shape, whole),
            pl.BlockSpec((1,) + s_own.shape[1:], lambda i: (i, 0, 0)),
            pl.BlockSpec((1,) + dp_own.shape[1:], lambda i: (i, 0, 0)),
            pl.BlockSpec((tok, 2 * PAIRS * LATENT), along),
            pl.BlockSpec((tok, 2 * PAIRS * RANK), along),
        ],
        out_specs=[
            pl.BlockSpec(
                (tok, 2 * PAIRS * LATENT), lambda i: (0, jnp.minimum(i, max(ahead - 1, 0)))
            ),
            pl.BlockSpec((1, ds_rows, stack), lambda i: (jnp.maximum(i - ahead, 0), 0, 0)),
            pl.BlockSpec(memory_space=pltpu.HBM),
            pl.BlockSpec(incoming.shape, whole),
        ] + [pl.BlockSpec(own_part, whole)] * head_parts,
        out_shape=[
            jax.ShapeDtypeStruct(queries.shape, bf16),
            jax.ShapeDtypeStruct((steps - ahead, ds_rows, stack), bf16),
            jax.ShapeDtypeStruct((rows, WIDTH), bf16),
            jax.ShapeDtypeStruct(incoming.shape, bf16),
        ] + [jax.ShapeDtypeStruct(own_part, f32)] * head_parts,
        scratch_shapes=[
            pltpu.VMEM((rows, WIDTH), bf16),
            pltpu.SemaphoreType.DMA(()),
            pltpu.VMEM((far_rows - LEAST_LIVE * BLK, stack // 2), f32),
            pltpu.VMEM((token_part(tok), stack // 2), f32),
            pltpu.VMEM((toks, WIDTH), bf16),
            pltpu.VMEM((rows, toks), f32),
            pltpu.VMEM((rows, toks), f32),
            pltpu.VMEM((rows, toks), bf16),
            pltpu.VMEM((8, toks), f32),
            pltpu.VMEM((rows, WIDTH), f32),
            pltpu.VMEM((rows, RANK), f32),
        ],
        compiler_params=pltpu.CompilerParams(vmem_limit_bytes=52 * MIB),
        cost_estimate=pl.CostEstimate(
            flops=2 * tok * heads * rows * (2 * LATENT + 2 * RANK),
            bytes_accessed=2 * tok * heads * (LATENT + RANK + rows),
            transcendentals=tok * heads * rows,
        ),
        name="score_gradients",
    )(anc_count, ancestors, incoming, own, s_own, dp_own, queries, d_out)


def put_queries(dq, ds, keys):
    tok = dq.shape[0]
    sub = token_part(tok)
    stack = PAIRS * sub
    low = LATENT - HALF
    seen, starts = seen_rows(keys.shape[0], tok)
    for j, n in enumerate(seen):
        both = mm(ds[0, pl.ds(starts[j], n), :], keys[:n, :], TN) * SCALE
        both = both.astype(dq.dtype)
        even, odd = both[:stack], pltpu.roll(both[stack:], HALF, axis=1)
        for i in range(PAIRS):
            at = i * 2 * LATENT
            part = slice(i * sub, (i + 1) * sub)
            toks = pl.ds(j * sub, sub)
            dq[toks, at:at + low] = even[part, :low]
            joint = even[part, low:] + odd[part, :2 * HALF]
            dq[toks, at + low:at + low + 2 * HALF] = joint
            dq[toks, at + low + 2 * HALF:at + 2 * LATENT] = odd[part, 2 * HALF:]


def query_kernel(keys, ds, started, dq):
    put_queries(dq, ds, keys)


def query_gradients(keys, ds, started):
    tok = started.shape[0]
    steps, rows = ds.shape[0], keys.shape[0]
    ahead = started.shape[1] // (2 * PAIRS * LATENT) - steps
    return pl.pallas_call(
        query_kernel,
        grid=(steps,),
        in_specs=[
            pl.BlockSpec(keys.shape, lambda i: (0, 0)),
            pl.BlockSpec((1,) + ds.shape[1:], lambda i: (i, 0, 0)),
            pl.BlockSpec(memory_space=pl.ANY),
        ],
        out_specs=pl.BlockSpec((tok, 2 * PAIRS * LATENT), lambda i: (0, i + ahead)),
        out_shape=jax.ShapeDtypeStruct(started.shape, started.dtype),
        input_output_aliases={2: 0},
        compiler_params=pltpu.CompilerParams(vmem_limit_bytes=51 * MIB),
        cost_estimate=pl.CostEstimate(
            flops=4 * tok * steps * PAIRS * rows * LATENT,
            bytes_accessed=4 * tok * steps * PAIRS * (LATENT + rows),
            transcendentals=0,
        ),
        name="query_gradients",
    )(keys, ds, started)


def local(queries, d_out, branch_latent, trunk_latent, ancestors, anc_count):
    leafs = lax.axis_size("leaf")
    head_parts = lax.axis_size("head")
    owned = trunk_latent.shape[0]
    part_rows = BLK // head_parts

    outgoing = pick(ancestors, trunk_latent.reshape(owned * BLK, LATENT))
    incoming = lax.all_to_all(
        outgoing.reshape(leafs, CAP * BLK, LATENT), "leaf", split_axis=0, concat_axis=0, tiled=True
    ).reshape(leafs * CAP * BLK, LATENT)

    s_own, dp_own = own_scores(branch_latent, queries, d_out)

    started, ds, keys, sent, mine, *others = attention(
        owned, head_parts, anc_count, ancestors, incoming, branch_latent, s_own, dp_own,
        queries, d_out,
    )

    theirs = []
    for hop, part in enumerate(others, 1):
        route = [(i, (i + hop) % head_parts) for i in range(head_parts)]
        theirs.append(lax.ppermute(part, "head", route))
    got = lax.all_to_all(
        sent.reshape(leafs * head_parts, CAP * part_rows, LATENT),
        ("leaf", "head"), split_axis=0, concat_axis=0, tiled=True,
    ).reshape(leafs * CAP * BLK, LATENT)
    d_queries = query_gradients(keys, ds, started)
    d_branch, d_trunk = finish(ancestors, got, mine, theirs, owned, part_rows)
    return d_queries, d_branch, d_trunk


def solution(mesh):
    return jax.shard_map(
        local,
        mesh=mesh,
        in_specs=(
            P("leaf", "head"),
            P("leaf", "head"),
            P("leaf", None),
            P("leaf", None, None),
            P(),
            P(),
        ),
        out_specs=(P("leaf", "head"), P(("leaf", "head"), None), P("leaf", "head", None)),
        check_vma=False,
    )
```
